32 devices in a mesh: dp: 8 (over z, x), tensor: 4 (over y, core).
Axes of the slice: x: 2, y: 2, z: 4, core: 2. Of those that a mesh axis runs over, the one named last changes fastest.
Arguments:
- inputs: bfloat16 [8, 3, 512, 1024], P('dp', None, 'tensor'), may hold values from -6 to 6
- lengths: int32 [8, 3], P('dp'), may hold values from 128 to 512, as said below
- cotangent: bfloat16 [8, 3, 512, 1024], P('dp', None, 'tensor'), may hold values from -6 to 6
- w_qkv: bfloat16 [1024, 3, 1024], P(None, None, 'tensor'), may hold values from -0.1875 to 0.1875
- b_query: bfloat16 [1024], P('tensor'), may hold values from -3 to 3
- b_value: bfloat16 [1024], P('tensor'), may hold values from -3 to 3
- w_out: bfloat16 [1024, 1024], P('tensor'), may hold values from -0.75 to 0.75
- b_out: bfloat16 [1024], replicated, may hold values from -3 to 3
- ln1_gain: bfloat16 [1024], replicated, may hold values from 0.5 to 1.5
- ln1_bias: bfloat16 [1024], replicated, may hold values from -3 to 3
- w_up: bfloat16 [1024, 4096], P(None, 'tensor'), may hold values from -0.1875 to 0.1875
- b_up: bfloat16 [4096], P('tensor'), may hold values from -3 to 3
- w_down: bfloat16 [4096, 1024], P('tensor'), may hold values from -0.09375 to 0.09375
- b_down: bfloat16 [1024], replicated, may hold values from -3 to 3
- ln2_gain: bfloat16 [1024], replicated, may hold values from 0.5 to 1.5
- ln2_bias: bfloat16 [1024], replicated, may hold values from -3 to 3
Outputs:
- output: bfloat16 [8, 3, 512, 1024], P('dp', None, 'tensor')
- grad_inputs: bfloat16 [8, 3, 512, 1024], P('dp', None, 'tensor')
- grad_qkv: float32 [1024, 3, 1024], P(None, None, 'tensor')
- grad_query_bias: float32 [1024], P('tensor')
- grad_value_bias: float32 [1024], P('tensor')
- grad_out: float32 [1024, 1024], P('tensor')
- grad_out_bias: float32 [1024], replicated
- grad_ln1_gain: float32 [1024], replicated
- grad_ln1_bias: float32 [1024], replicated
- grad_up: float32 [1024, 4096], P(None, 'tensor')
- grad_up_bias: float32 [4096], P('tensor')
- grad_down: float32 [4096, 1024], P('tensor')
- grad_down_bias: float32 [1024], replicated
- grad_ln2_gain: float32 [1024], replicated
- grad_ln2_bias: float32 [1024], replicated
The draws below stay inside these ranges and needn't reach their ends.
Inputs may be any that keep to these rules, and one draw needn't show every extreme that they name: Each row of lengths has one entry equal to 512; a sequence fills the first lengths entries of its 512 slots, the rest is padding.
All inputs are finite; a program needn't handle non-finite values.
Results may differ from the reference program's by a relative error of at most 0.018.
Values may be sent and summed in bfloat16 or wider, within the bound.
A program may use at most 128 MiB of HBM per device.

```python
import jax
import jax.numpy as jnp
from jax import lax

D = 1024
H = 16
HD = 64
FF = 4096
SEQ = 512
MB = 3
N_DP = 8


def draw_lengths(key, part):
    key = jax.random.fold_in(key, 11)
    base_key, full_key = jax.random.split(key)
    spread = jax.random.randint(base_key, (N_DP, MB), SEQ // 4, SEQ + 1, dtype=jnp.int32)
    chosen = jax.random.randint(full_key, (N_DP, 1), 0, MB, dtype=jnp.int32)
    columns = jnp.arange(MB, dtype=jnp.int32)[None, :]
    return jnp.where(columns == chosen, SEQ, spread).astype(jnp.int32)


def block_levels(rng, dims, pieces, smallest, top_value):
    level, own = 1.0, jax.random.fold_in(rng, 6)
    for dim, blocks in pieces:
        draws = jnp.exp(jax.random.uniform(jax.random.fold_in(own, dim), (blocks,), jnp.float32, smallest / len(pieces), top_value / len(pieces)))
        level = level * jnp.repeat(draws, dims[dim] // blocks).reshape([-1 if axis == dim else 1 for axis in range(len(dims))])
    return level


def scatter_about(rng, shape, width, most, cuts=(), held_as=jnp.bfloat16):
    values = jax.random.normal(rng, shape, jnp.float32) * width
    if len(cuts) > 0:
        values = block_levels(rng, shape, cuts, -0.22, 0.18) * values
    return jnp.clip(values, min=-most, max=most).astype(held_as)


def setup_inputs(seed: int = 0) -> dict:
    key_of = jax.random.split(jax.random.key(seed), 17)
    return {
        "inputs": scatter_about(key_of[0], (N_DP, MB, SEQ, D), 1.0, 6.0, ((0, 8), (2, 4))),
        "lengths": draw_lengths(jax.random.fold_in(key_of[16], 71), 0),
        "cotangent": scatter_about(key_of[2], (N_DP, MB, SEQ, D), 1.0, 6.0, ((0, 8), (2, 4))),
        "w_qkv": scatter_about(key_of[3], (D, 3, D), D ** -0.5, 0.1875, ((2, 4),)),
        "b_query": scatter_about(key_of[4], (D,), 0.5, 3.0, ((0, 4),)),
        "b_value": scatter_about(key_of[5], (D,), 0.5, 3.0, ((0, 4),)),
        "w_out": scatter_about(key_of[6], (D, D), (D // 16) ** -0.5, 0.75, ((0, 4),)),
        "b_out": scatter_about(key_of[7], (D,), 0.5, 3.0),
        "ln1_gain": jnp.clip(1.0 + 0.1 * jax.random.normal(key_of[8], (D,), jnp.float32), 0.5, 1.5).astype(jnp.bfloat16),
        "ln1_bias": scatter_about(key_of[9], (D,), 0.5, 3.0),
        "w_up": scatter_about(key_of[10], (D, FF), D ** -0.5, 0.1875, ((1, 4),)),
        "b_up": scatter_about(key_of[11], (FF,), 0.5, 3.0, ((0, 4),)),
        "w_down": scatter_about(key_of[12], (FF, D), FF ** -0.5, 0.09375, ((0, 4),)),
        "b_down": scatter_about(key_of[13], (D,), 0.5, 3.0),
        "ln2_gain": jnp.clip(1.0 + 0.1 * jax.random.normal(key_of[14], (D,), jnp.float32), 0.5, 1.5).astype(jnp.bfloat16),
        "ln2_bias": scatter_about(key_of[15], (D,), 0.5, 3.0),
    }


EPSILON = 1e-05
HIGHEST_PRECISION = lax.Precision.HIGHEST

@jax.custom_vjp
def low(v):
    return lax.optimization_barrier(v.astype(jnp.bfloat16)).astype(jnp.float32)

@jax.custom_vjp
def low_back(v):
    return v

def low_keep(v):
    return (low(v), None)

def low_pass(kept, grad):
    return (grad,)

def back_keep(v):
    return (v, None)

def back_low(kept, grad):
    return (low(grad),)
low.defvjp(low_keep, low_pass)
low_back.defvjp(back_keep, back_low)

def product(left, right):
    return jnp.dot(left, right, precision=HIGHEST_PRECISION, preferred_element_type=jnp.float32)

def layer_norm(values, norm_gain, norm_shift):
    row_mean = lax.optimization_barrier(jnp.mean(values, axis=-1, keepdims=True))
    centred = values - row_mean
    spread = lax.optimization_barrier(jnp.mean(centred * centred, axis=-1, keepdims=True))
    return centred * lax.rsqrt(spread + EPSILON) * norm_gain + norm_shift

def exact_gelu(values):
    return jax.nn.gelu(values, approximate=False)

def attend_block(query_block, key_heads, value_heads, key_mask):
    scores = jnp.einsum('hqd,hkd->hqk', query_block, key_heads, precision=HIGHEST_PRECISION) * HD ** (-0.5)
    scores = jnp.where(key_mask[None, None, :], low_back(scores), -1e+30)
    weights = jax.nn.softmax(scores, axis=-1)
    return jnp.einsum('hqk,hkd->hqd', low(weights), value_heads, precision=HIGHEST_PRECISION)

def forward(sequence_in, w_qkv, b_query, b_value, w_out, b_out, ln1_gain, ln1_bias, w_up, b_up, w_down, b_down, ln2_gain, ln2_bias, length):
    key_mask = jnp.arange(SEQ, dtype=jnp.int32) < length
    projected = product(sequence_in, w_qkv.reshape(D, 3 * D)).reshape(SEQ, 3, D)
    queries = low(low_back(projected[:, 0]) + b_query)
    keys_low = low(low_back(projected[:, 1]))
    values_low = low(low_back(projected[:, 2]) + b_value)
    block_rows = min(512, SEQ)
    block_count = SEQ // block_rows

    def heads_first(matrix):
        return matrix.reshape(SEQ, H, HD).transpose(1, 0, 2)
    query_blocks = heads_first(queries).reshape(H, block_count, block_rows, HD).transpose(1, 0, 2, 3)
    key_heads = heads_first(keys_low)
    value_heads = heads_first(values_low)
    context = lax.map(jax.checkpoint(lambda query_block: attend_block(query_block, key_heads, value_heads, key_mask)), query_blocks)
    context = context.transpose(0, 2, 1, 3).reshape(SEQ, D)
    context = low_back(low(context))
    attended = low_back(product(context, w_out)) + b_out
    normed = layer_norm(sequence_in + attended, ln1_gain, ln1_bias)
    hidden = low_back(product(low(normed), w_up)) + b_up
    activated = low(exact_gelu(hidden))
    mixed = low_back(product(activated, w_down)) + b_down
    result = layer_norm(normed + mixed, ln2_gain, ln2_bias)
    return result * key_mask.astype(jnp.float32)[:, None]

def reference(inputs, lengths, cotangent, w_qkv, b_query, b_value, w_out, b_out, ln1_gain, ln1_bias, w_up, b_up, w_down, b_down, ln2_gain, ln2_bias):
    parameters = tuple((weight.astype(jnp.float32) for weight in (w_qkv, b_query, b_value, w_out, b_out, ln1_gain, ln1_bias, w_up, b_up, w_down, b_down, ln2_gain, ln2_bias)))
    flat_inputs = inputs.reshape(N_DP * MB, SEQ, D).astype(jnp.float32)
    flat_cotangent = cotangent.reshape(N_DP * MB, SEQ, D).astype(jnp.float32)
    flat_lengths = lengths.reshape(N_DP * MB).astype(jnp.int32)

    def one_sequence(totals, sequence_item):
        sequence_in, sequence_cotangent, length = sequence_item

        def layer_call(layer_input, *weights):
            return forward(layer_input, *weights, length)
        outputs, pullback = jax.vjp(layer_call, sequence_in, *parameters)
        gradients = pullback(sequence_cotangent)
        return (tuple((total + gradient for total, gradient in zip(totals, gradients[1:]))), (outputs, gradients[0]))
    initial = tuple((jnp.zeros_like(weight) for weight in parameters))
    totals, (outputs, grad_rows) = lax.scan(one_sequence, initial, (flat_inputs, flat_cotangent, flat_lengths))
    full_shape = (N_DP, MB, SEQ, D)
    return (outputs.reshape(full_shape).astype(jnp.bfloat16), grad_rows.reshape(full_shape).astype(jnp.bfloat16), totals[0], totals[1], totals[2], totals[3], totals[4], totals[5], totals[6], totals[7], totals[8], totals[9], totals[10], totals[11], totals[12])
```

```python
import jax
import jax.numpy as jnp
from jax import lax
from jax.sharding import PartitionSpec as P

HD = 64


EPSILON = 1e-05


def layer_norm(values, norm_gain, norm_shift):
    row_mean = jnp.mean(values, axis=-1, keepdims=True)
    centred = values - row_mean
    spread = jnp.mean(centred * centred, axis=-1, keepdims=True)
    return centred * lax.rsqrt(spread + EPSILON) * norm_gain + norm_shift


def exact_gelu(values):
    return jax.nn.gelu(values, approximate=False)


def attention_forward(queries, keys_low, values_low, key_mask):
    length_all = queries.shape[0]
    head_width = queries.shape[1]
    head_count = head_width // HD
    block_rows = min(512, length_all)
    blocks = length_all // block_rows
    score_scale = HD ** (-0.5)
    query_blocks = queries.reshape(blocks, block_rows, head_count, HD)
    key_heads = keys_low.reshape(length_all, head_count, HD)
    value_heads = values_low.reshape(length_all, head_count, HD)

    def one_block(query_block):
        scores = (
            jnp.einsum("qhd,khd->hqk", query_block, key_heads, preferred_element_type=jnp.float32)
            * score_scale
        )
        scores = jnp.where(key_mask[None, None, :], scores, -1e30)
        row_max = jnp.max(scores, axis=-1, keepdims=True)
        raw_weights = jnp.exp(scores - row_max)
        totals = jnp.sum(raw_weights, axis=-1, keepdims=True)
        probabilities = raw_weights / totals
        context = jnp.einsum(
            "hqk,khd->qhd",
            probabilities.astype(jnp.bfloat16),
            value_heads,
            preferred_element_type=jnp.float32,
        )
        return (context.astype(jnp.bfloat16), row_max[..., 0] + jnp.log(totals[..., 0]))

    context, log_totals = lax.map(one_block, query_blocks)
    return (context.reshape(length_all, head_width), log_totals)


def attention_backward(queries, keys_low, values_low, grad_context, key_mask, log_totals):
    length_all = queries.shape[0]
    head_width = queries.shape[1]
    head_count = head_width // HD
    block_rows = min(512, length_all)
    blocks = length_all // block_rows
    score_scale = HD ** (-0.5)
    query_blocks = queries.reshape(blocks, block_rows, head_count, HD)
    grad_blocks = grad_context.reshape(blocks, block_rows, head_count, HD)
    key_heads = keys_low.reshape(length_all, head_count, HD)
    value_heads = values_low.reshape(length_all, head_count, HD)

    def one_block(carried, block_item):
        grad_keys, grad_values = carried
        query_block, grad_block, log_block = block_item
        scores = (
            jnp.einsum("qhd,khd->hqk", query_block, key_heads, preferred_element_type=jnp.float32)
            * score_scale
        )
        scores = jnp.where(key_mask[None, None, :], scores, -1e30)
        probabilities = jnp.exp(scores - log_block[..., None])
        grad_values = grad_values + jnp.einsum(
            "hqk,qhd->khd",
            probabilities.astype(jnp.bfloat16),
            grad_block,
            preferred_element_type=jnp.float32,
        )
        grad_probs = jnp.einsum(
            "qhd,khd->hqk", grad_block, value_heads, preferred_element_type=jnp.float32
        )
        grad_scores = probabilities * (
            grad_probs - jnp.sum(probabilities * grad_probs, axis=-1, keepdims=True)
        )
        low_scores = grad_scores.astype(jnp.bfloat16)
        grad_query = (
            jnp.einsum("hqk,khd->qhd", low_scores, key_heads, preferred_element_type=jnp.float32)
            * score_scale
        )
        grad_keys = (
            grad_keys
            + jnp.einsum(
                "hqk,qhd->khd", low_scores, query_block, preferred_element_type=jnp.float32
            )
            * score_scale
        )
        return ((grad_keys, grad_values), grad_query)

    empty_keys = jnp.zeros((length_all, head_count, HD), jnp.float32)
    (grad_keys, grad_values), grad_queries = lax.scan(
        one_block, (empty_keys, empty_keys), (query_blocks, grad_blocks, log_totals)
    )
    return (
        grad_queries.reshape(length_all, head_width),
        grad_keys.reshape(length_all, head_width),
        grad_values.reshape(length_all, head_width),
    )


def per_device(
    inputs,
    lengths,
    cotangent,
    w_qkv,
    b_query,
    b_value,
    w_out,
    b_out,
    ln1_gain,
    ln1_bias,
    w_up,
    b_up,
    w_down,
    b_down,
    ln2_gain,
    ln2_bias,
):
    groups = lax.axis_size("tensor")
    tensor_rank = lax.axis_index("tensor")
    batches = inputs.shape[1]
    local_rows = inputs.shape[2]
    model_width = inputs.shape[3]
    full_rows = local_rows * groups
    head_width = w_qkv.shape[2]
    flat_qkv = w_qkv.reshape(model_width, 3 * head_width)
    positions = tensor_rank * local_rows + jnp.arange(local_rows, dtype=jnp.int32)
    all_positions = jnp.arange(full_rows, dtype=jnp.int32)
    gain_first = ln1_gain.astype(jnp.float32)
    shift_first = ln1_bias.astype(jnp.float32)

    def micro_batch(batch_index, carried):
        weight_grads, shared_grads, output_rows, input_grads = carried
        tokens = lax.dynamic_index_in_dim(inputs[0], batch_index, 0, keepdims=False)
        incoming = lax.dynamic_index_in_dim(cotangent[0], batch_index, 0, keepdims=False).astype(
            jnp.float32
        )
        length = lax.dynamic_index_in_dim(lengths[0], batch_index, 0, keepdims=False)
        key_mask = all_positions < length
        row_mask = (positions < length).astype(jnp.float32)[:, None]
        tokens_all = lax.all_gather(tokens, "tensor", axis=0, tiled=True)
        projected = jnp.dot(tokens_all, flat_qkv, preferred_element_type=jnp.float32).reshape(
            full_rows, 3, head_width
        )
        queries = (projected[:, 0] + b_query).astype(jnp.bfloat16)
        keys_low = projected[:, 1].astype(jnp.bfloat16)
        values_low = (projected[:, 2] + b_value).astype(jnp.bfloat16)
        context, log_totals = attention_forward(queries, keys_low, values_low, key_mask)
        attended = (
            lax.psum_scatter(
                jnp.dot(context, w_out, preferred_element_type=jnp.float32).astype(jnp.bfloat16),
                "tensor",
                scatter_dimension=0,
                tiled=True,
            ).astype(jnp.float32)
            + b_out
        )
        normed, norm1_back = jax.vjp(
            layer_norm, tokens.astype(jnp.float32) + attended, gain_first, shift_first
        )
        normed_all = lax.all_gather(normed.astype(jnp.bfloat16), "tensor", axis=0, tiled=True)
        hidden = jnp.dot(normed_all, w_up, preferred_element_type=jnp.float32) + b_up
        activated, gelu_back = jax.vjp(exact_gelu, hidden)
        activated_low = activated.astype(jnp.bfloat16)
        mixed = (
            lax.psum_scatter(
                jnp.dot(activated_low, w_down, preferred_element_type=jnp.float32).astype(
                    jnp.bfloat16
                ),
                "tensor",
                scatter_dimension=0,
                tiled=True,
            ).astype(jnp.float32)
            + b_down
        )
        result, norm2_back = jax.vjp(
            layer_norm, normed + mixed, ln2_gain.astype(jnp.float32), ln2_bias.astype(jnp.float32)
        )
        output_rows = lax.dynamic_update_index_in_dim(
            output_rows, (result * row_mask).astype(jnp.bfloat16), batch_index, 0
        )
        grad_second, grad_gain2, grad_shift2 = norm2_back(incoming * row_mask)
        grad_mixed_all = lax.all_gather(
            grad_second.astype(jnp.bfloat16), "tensor", axis=0, tiled=True
        )
        grad_downw = jnp.einsum(
            "sf,sd->fd", activated_low, grad_mixed_all, preferred_element_type=jnp.float32
        )
        grad_activated = jnp.einsum(
            "sd,fd->sf", grad_mixed_all, w_down, preferred_element_type=jnp.float32
        )
        (grad_hidden,) = gelu_back(grad_activated)
        grad_hidden_low = grad_hidden.astype(jnp.bfloat16)
        grad_upw = jnp.einsum(
            "sd,sf->df", normed_all, grad_hidden_low, preferred_element_type=jnp.float32
        )
        acc_qkv, acc_query, acc_value, acc_outw, acc_upw, acc_upb, acc_downw = weight_grads
        acc_upw = acc_upw + grad_upw
        acc_upb = acc_upb + jnp.sum(grad_hidden, axis=0)
        acc_downw = acc_downw + grad_downw
        grad_normed = (
            lax.psum_scatter(
                jnp.einsum(
                    "sf,df->sd", grad_hidden_low, w_up, preferred_element_type=jnp.float32
                ).astype(jnp.bfloat16),
                "tensor",
                scatter_dimension=0,
                tiled=True,
            ).astype(jnp.float32)
            + grad_second
        )
        grad_first, grad_gain1, grad_shift1 = norm1_back(grad_normed)
        grad_attended_all = lax.all_gather(
            grad_first.astype(jnp.bfloat16), "tensor", axis=0, tiled=True
        )
        grad_outw = jnp.einsum(
            "sl,sd->ld", context, grad_attended_all, preferred_element_type=jnp.float32
        )
        grad_context = jnp.einsum(
            "sd,ld->sl", grad_attended_all, w_out, preferred_element_type=jnp.float32
        ).astype(jnp.bfloat16)
        grad_queries, grad_keys, grad_values = attention_backward(
            queries, keys_low, values_low, grad_context, key_mask, log_totals
        )
        grad_projected = (
            jnp.stack([grad_queries, grad_keys, grad_values], axis=1)
            .astype(jnp.bfloat16)
            .reshape(full_rows, 3 * head_width)
        )
        grad_qkvw = jnp.einsum(
            "sd,sk->dk", tokens_all, grad_projected, preferred_element_type=jnp.float32
        ).reshape(model_width, 3, head_width)
        grad_tokens = (
            lax.psum_scatter(
                jnp.einsum(
                    "sk,dk->sd", grad_projected, flat_qkv, preferred_element_type=jnp.float32
                ).astype(jnp.bfloat16),
                "tensor",
                scatter_dimension=0,
                tiled=True,
            ).astype(jnp.float32)
            + grad_first
        )
        input_grads = lax.dynamic_update_index_in_dim(
            input_grads, grad_tokens.astype(jnp.bfloat16), batch_index, 0
        )
        weight_grads = (
            acc_qkv + grad_qkvw,
            acc_query + jnp.sum(grad_queries, axis=0),
            acc_value + jnp.sum(grad_values, axis=0),
            acc_outw + grad_outw,
            acc_upw,
            acc_upb,
            acc_downw,
        )
        shared_outb, shared_gain1, shared_shift1, shared_downb, shared_gain2, shared_shift2 = (
            shared_grads
        )
        shared_grads = (
            shared_outb + jnp.sum(grad_first, axis=0),
            shared_gain1 + grad_gain1,
            shared_shift1 + grad_shift1,
            shared_downb + jnp.sum(grad_second, axis=0),
            shared_gain2 + grad_gain2,
            shared_shift2 + grad_shift2,
        )
        return (weight_grads, shared_grads, output_rows, input_grads)

    vector_zero = jnp.zeros((model_width,), jnp.float32)
    weight_zero = (
        jnp.zeros(w_qkv.shape, jnp.float32),
        jnp.zeros(b_query.shape, jnp.float32),
        jnp.zeros(b_value.shape, jnp.float32),
        jnp.zeros(w_out.shape, jnp.float32),
        jnp.zeros(w_up.shape, jnp.float32),
        jnp.zeros(b_up.shape, jnp.float32),
        jnp.zeros(w_down.shape, jnp.float32),
    )
    shared_zero = (vector_zero, vector_zero, vector_zero, vector_zero, vector_zero, vector_zero)
    rows_zero = jnp.zeros((batches, local_rows, model_width), jnp.bfloat16)
    carried = (weight_zero, shared_zero, rows_zero, rows_zero)
    for batch_index in range(batches - 1):
        carried = micro_batch(batch_index, carried)
    weight_grads, shared_grads, output_rows, input_grads = micro_batch(batches - 1, carried)
    acc_qkv, acc_query, acc_value, acc_outw, acc_upw, acc_upb, acc_downw = weight_grads
    acc_qkv, acc_outw, acc_upw, acc_downw = (
        lax.psum(term.astype(jnp.bfloat16), "dp").astype(jnp.float32)
        for term in (acc_qkv, acc_outw, acc_upw, acc_downw)
    )
    acc_query, acc_value, acc_upb = lax.psum((acc_query, acc_value, acc_upb), "dp")
    shared_outb, shared_gain1, shared_shift1, shared_downb, shared_gain2, shared_shift2 = (
        shared_grads
    )
    shared_outb, shared_gain1, shared_shift1, shared_downb, shared_gain2, shared_shift2 = lax.psum(
        (shared_outb, shared_gain1, shared_shift1, shared_downb, shared_gain2, shared_shift2),
        ("dp", "tensor"),
    )
    return (
        output_rows[None],
        input_grads[None],
        acc_qkv,
        acc_query,
        acc_value,
        acc_outw,
        shared_outb,
        shared_gain1,
        shared_shift1,
        acc_upw,
        acc_upb,
        acc_downw,
        shared_downb,
        shared_gain2,
        shared_shift2,
    )


def solution(mesh):
    return jax.shard_map(
        per_device,
        mesh=mesh,
        in_specs=(
            P("dp", None, "tensor", None),
            P("dp", None),
            P("dp", None, "tensor", None),
            P(None, None, "tensor"),
            P("tensor"),
            P("tensor"),
            P("tensor", None),
            P(),
            P(),
            P(),
            P(None, "tensor"),
            P("tensor"),
            P("tensor", None),
            P(),
            P(),
            P(),
        ),
        out_specs=(
            P("dp", None, "tensor", None),
            P("dp", None, "tensor", None),
            P(None, None, "tensor"),
            P("tensor"),
            P("tensor"),
            P("tensor", None),
            P(),
            P(),
            P(),
            P(None, "tensor"),
            P("tensor"),
            P("tensor", None),
            P(),
            P(),
            P(),
        ),
        check_vma=False,
    )
```

```python
import functools

import jax
import jax.numpy as jnp
from jax import lax
from jax.experimental import pallas as pl
from jax.experimental.pallas import tpu as pltpu
from jax.sharding import PartitionSpec as P

HD = 64
EPSILON = 1e-05
F32 = jnp.float32
LOW = jnp.bfloat16
MESH = pl.DeviceIdType.MESH
TILE = 256
PHASES = 4


def dot(left, right, left_dim=1, right_dim=0):
    return lax.dot_general(
        left, right, (((left_dim,), (right_dim,)), ((), ())), preferred_element_type=F32
    )


def row_sum(values):
    return jnp.sum(values, axis=0, keepdims=True)


def row_mean(values):
    return jnp.mean(values, axis=-1, keepdims=True)


def gelu_parts(h):
    t = 1.0 / (1.0 + 0.23164188 * jnp.abs(h))
    density = jnp.exp(-0.5 * h * h)
    series = t * (
        0.127414796
        + t * (-0.142248368 + t * (0.7107068705 + t * (-0.7265760135 + t * 0.5307027145)))
    )
    tail = series * density
    return jnp.where(h < 0.0, tail, 1.0 - tail), density * 0.3989422804014327


def layer_kernel(
    lengths_ref,
    x_ref,
    cot_ref,
    wqkv_ref,
    wout_ref,
    wup_ref,
    wdown_ref,
    vec_ref,
    out_ref,
    gin_ref,
    grads_ref,
    vgrad_ref,
    xa,
    wq,
    wo,
    wu,
    wd,
    qkv,
    pt,
    cc,
    ua,
    act,
    gp,
    g2a,
    g1a,
    dpr,
    part,
    rc,
    ys,
    ry,
    xh1,
    rstd1,
    resid,
    cot,
    gin,
    gb,
    vg,
    load_sem,
    store_sem,
    agy_send,
    agy_recv,
    agc_send,
    agc_recv,
    agf_send,
    agf_recv,
    rsc_send,
    rsc_recv,
    rsy_send,
    rsy_recv,
):
    batches = x_ref.shape[0]
    block = x_ref.shape[1]
    width = x_ref.shape[2]
    head_cols = wo.shape[0]
    hidden = wu.shape[1]
    rows = 4 * block
    pairs = head_cols // 128
    t = lax.axis_index("tensor")
    c = lax.rem(t, 2)
    y = lax.div(t, 2)
    t_core = y * 2 + (1 - c)
    t_y = (1 - y) * 2 + c
    t_far = (1 - y) * 2 + (1 - c)
    core = {"tensor": t_core}
    across = {"tensor": t_y}

    gathers = (xa, ua, g2a, g1a)

    def remote(src, dst, send, recv, device):
        return pltpu.make_async_remote_copy(
            src_ref=src, dst_ref=dst, send_sem=send, recv_sem=recv, device_id=device, device_id_type=MESH
        )

    def ag_y(p, s, at, src=None):
        buf = gathers[p]
        return remote(
            buf.at[s, at] if src is None else src, buf.at[s, at], agy_send.at[p, s], agy_recv.at[p, s], across
        )

    def ag_c(p, s, at, src=None):
        buf = gathers[p]
        return remote(
            buf.at[s, at] if src is None else src, buf.at[s, at], agc_send.at[p, s], agc_recv.at[p, s], core
        )

    def ag_f(p, s, at):
        buf = gathers[p]
        return remote(buf.at[s, at], buf.at[s, at], agf_send.at[p, s], agf_recv.at[p, s], core)

    def rs_c(p, s):
        return remote(part.at[s, 1 - c], rc.at[s], rsc_send.at[p, s], rsc_recv.at[p, s], core)

    def rs_y(p, s):
        return remote(ys.at[s], ry.at[s], rsy_send.at[p, s], rsy_recv.at[p, s], across)

    def load(index, src, dst):
        return pltpu.make_async_copy(src, dst, load_sem.at[index])

    def store(index, src, dst):
        return pltpu.make_async_copy(src, dst, store_sem.at[index])

    loads = [load(s, x_ref.at[s], xa.at[s, t]) for s in range(batches)]
    n = batches
    load_wq = load(n, wqkv_ref, wq)
    load_wo = load(n + 1, wout_ref, wo)
    load_wu = load(n + 2, wup_ref, wu)
    load_wd = load(n + 3, wdown_ref, wd)
    load_cot = load(n + 4, cot_ref, cot)

    barrier = pltpu.get_barrier_semaphore()
    for device in (core, across):
        pl.semaphore_signal(barrier, inc=1, device_id=device, device_id_type=MESH)
    for cp in loads:
        cp.start()
    load_wq.start()
    load_wo.start()
    pl.semaphore_wait(barrier, 2)
    for s in range(batches):
        ag_y(0, s, t, x_ref.at[s]).start()
        ag_c(0, s, t, x_ref.at[s]).start()
    load_wu.start()
    load_wd.start()
    load_cot.start()

    vg[...] = jnp.zeros_like(vg)
    lane = lax.broadcasted_iota(jnp.int32, (rows, 128), 1)
    low_half = lane < HD
    empty = jnp.zeros((rows, 128), LOW)

    def masked(values, h):
        return jnp.where(low_half, values, empty) if h == 0 else jnp.where(low_half, empty, values)

    def vec(i):
        return vec_ref[i : i + 1, :]

    def whole(ref, s):
        return ref[s].reshape(rows, width)

    def put_part(s, j, values):
        values = values.astype(LOW)
        for b in range(4):
            part[s, b % 2, b // 2, :, j * TILE : (j + 1) * TILE] = values[b * block : (b + 1) * block]

    def compute_a(s):
        tokens = whole(xa, s)
        q = dot(tokens, wq[0]) + vec_ref[7:8, :head_cols]
        qkv[s, 0] = q.astype(LOW) * LOW(HD ** (-0.5))
        qkv[s, 1] = dot(tokens, wq[1]).astype(LOW)
        v = dot(tokens, wq[2]) + vec_ref[7:8, head_cols : 2 * head_cols]
        qkv[s, 2] = v.astype(LOW)
        keys_valid = lax.broadcasted_iota(jnp.int32, (rows, rows), 0) < lengths_ref[0, s]
        for j in range(pairs):
            cols = slice(j * 128, (j + 1) * 128)
            q, k, v = qkv[s, 0, :, cols], qkv[s, 1, :, cols], qkv[s, 2, :, cols]
            context = jnp.zeros((128, rows), F32)
            for h in range(2):
                scores = dot(k, masked(q, h), 1, 1)
                scores = jnp.where(keys_valid, scores, -1e30)
                weights = jnp.exp(scores - jnp.max(scores, axis=0, keepdims=True))
                p = (weights * (1.0 / row_sum(weights))).astype(LOW)
                pt[s, 2 * j + h] = p
                context = context + dot(masked(v, h).T, p)
            cc[s, :, cols] = context.T.astype(LOW)
        context = cc[s]
        for j in range(width // TILE):
            put_part(s, j, dot(context, wo[:, j * TILE : (j + 1) * TILE]))

    def compute_c(s):
        normed = whole(ua, s)
        for j in range(hidden // TILE):
            cols = slice(j * TILE, (j + 1) * TILE)
            h = dot(normed, wu[:, cols]) + vec_ref[6:7, cols]
            phi, density = gelu_parts(h)
            act[s, :, cols] = (h * phi).astype(LOW)
            gp[s, :, cols] = (phi + h * density).astype(LOW)
        activated = act[s]
        for j in range(width // TILE):
            put_part(s, j, dot(activated, wd[:, j * TILE : (j + 1) * TILE]))

    def compute_e(s):
        grad = whole(g2a, s)
        for j in range(hidden // TILE):
            cols = slice(j * TILE, (j + 1) * TILE)
            gh = gp[s, :, cols].astype(F32) * dot(grad, wd[cols, :], 1, 1)
            vg[6:7, cols] += row_sum(gh)
            gp[s, :, cols] = gh.astype(LOW)
        grad_hidden = gp[s]
        for j in range(width // TILE):
            put_part(s, j, dot(grad_hidden, wu[j * TILE : (j + 1) * TILE, :], 1, 1))

    def compute_g(s):
        grad_context = dot(whole(g1a, s), wo[...], 1, 1).astype(LOW)
        for j in range(pairs):
            cols = slice(j * 128, (j + 1) * 128)
            q, k, v = qkv[s, 0, :, cols], qkv[s, 1, :, cols], qkv[s, 2, :, cols]
            gc = grad_context[:, cols]
            dq = jnp.zeros((128, rows), F32)
            dk = jnp.zeros((rows, 128), F32)
            dv = jnp.zeros((rows, 128), F32)
            for h in range(2):
                gc_h = masked(gc, h)
                p = pt[s, 2 * j + h]
                wide = p.astype(F32)
                product = wide * dot(v, gc_h, 1, 1)
                ds = (product - wide * row_sum(product)).astype(LOW)
                dv = dv + dot(p, gc_h)
                dk = dk + dot(ds, masked(q, h))
                dq = dq + dot(masked(k, h).T, ds)
            dq = dq.T * (HD ** (-0.5))
            vg[7:8, cols] += row_sum(dq)
            vg[7:8, head_cols + j * 128 : head_cols + (j + 1) * 128] += row_sum(dv)
            dpr[s, 0, :, cols] = dq.astype(LOW)
            dpr[s, 1, :, cols] = dk.astype(LOW)
            dpr[s, 2, :, cols] = dv.astype(LOW)
        for j in range(width // TILE):
            at = slice(j * TILE, (j + 1) * TILE)
            total = dot(dpr[s, 0], wq[0, at, :], 1, 1)
            total = total + dot(dpr[s, 1], wq[1, at, :], 1, 1)
            total = total + dot(dpr[s, 2], wq[2, at, :], 1, 1)
            put_part(s, j, total)

    computes = (compute_a, compute_c, compute_e, compute_g)

    def reduced(p, s):
        rs_y(p, s).wait()
        rs_c(p, s).wait_send()
        return part[s, c, y].astype(F32) + rc[s, y].astype(F32) + ry[s].astype(F32)

    def send_on(p, s):
        ag_y(p, s, t).start()
        ag_c(p, s, t).start()

    def finish_a(s):
        z = xa[s, t].astype(F32) + (reduced(0, s) + vec(0))
        centred = z - row_mean(z)
        rstd = lax.rsqrt(row_mean(centred * centred) + EPSILON)
        hat = centred * rstd
        xh1[s] = hat
        rstd1[s] = jnp.broadcast_to(rstd, rstd1.shape[1:])
        ua[s, t] = (hat * vec(1) + vec(2)).astype(LOW)
        send_on(1, s)

    def finish_c(s):
        z = (xh1[s] * vec(1) + vec(2)) + (reduced(1, s) + vec(3))
        centred = z - row_mean(z)
        rstd = lax.rsqrt(row_mean(centred * centred) + EPSILON)
        hat = centred * rstd
        valid = t * block + lax.broadcasted_iota(jnp.int32, (block, width), 0) < lengths_ref[0, s]
        incoming = jnp.where(valid, cot[s].astype(F32), 0.0)
        scaled = incoming * vec(4)
        grad = rstd * (scaled - row_mean(scaled) - hat * row_mean(scaled * hat))
        resid[s] = grad
        g2a[s, t] = grad.astype(LOW)
        send_on(2, s)
        cot[s] = jnp.where(valid, hat * vec(4) + vec(5), 0.0).astype(LOW)
        store(s, cot.at[s], out_ref.at[s]).start()
        vg[3:4, :] += row_sum(grad)
        vg[4:5, :] += row_sum(incoming * hat)
        vg[5:6, :] += row_sum(incoming)

    def finish_e(s):
        gu = resid[s] + reduced(2, s)
        hat = xh1[s]
        scaled = gu * vec(1)
        grad = rstd1[s, :, :1] * (scaled - row_mean(scaled) - hat * row_mean(scaled * hat))
        resid[s] = grad
        g1a[s, t] = grad.astype(LOW)
        send_on(3, s)
        vg[0:1, :] += row_sum(grad)
        vg[1:2, :] += row_sum(gu * hat)
        vg[2:3, :] += row_sum(gu)

    def finish_g(s):
        gin[s] = (resid[s] + reduced(3, s)).astype(LOW)
        store(batches + s, gin.at[s], gin_ref.at[s]).start()

    finishes = (finish_a, finish_c, finish_e, finish_g)

    def forward_block(p, s):
        ag_y(p, s, t_y).wait_recv()
        ag_f(p, s, t_y).start()

    def slot(p, s):
        ag_c(p, s, t_core).wait_recv()
        ag_f(p, s, t_far).wait_recv()
        computes[p](s)
        rs_c(p, s).start()
        rs_c(p, s).wait_recv()
        ys[s] = (part[s, c, 1 - y].astype(F32) + rc[s, 1 - y].astype(F32)).astype(LOW)
        rs_y(p, s).start()

    forward_block(0, 0)
    for p in range(PHASES):
        if p == 0:
            for cp in loads:
                cp.wait()
            load_wq.wait()
            load_wo.wait()
        if p == 1:
            load_wu.wait()
            load_wd.wait()
            load_cot.wait()

        def step(s, carry, p=p):
            slot(p, s)
            if p > 0:

                @pl.when(s == 0)
                def _():
                    finishes[p - 1](batches - 1)

            @pl.when(s > 0)
            def _():
                finishes[p](s - 1)

            @pl.when(s < batches - 1)
            def _():
                forward_block(p, s + 1)

            if p < PHASES - 1:

                @pl.when(s == batches - 1)
                def _():
                    forward_block(p + 1, 0)

            return carry

        lax.fori_loop(0, batches, step, 0)
    def tall(ref):
        return ref[...].reshape(batches * rows, -1)

    chunk = 0
    grads2 = tall(g2a)
    for j in range(hidden // TILE):
        a = act[:, :, j * TILE : (j + 1) * TILE].reshape(batches * rows, TILE)
        gb[chunk] = dot(a, grads2, 0, 0).astype(LOW)
        store(2 * batches + chunk, gb.at[chunk], grads_ref.at[chunk]).start()
        chunk += 1
    gradh = tall(gp)
    for j in range(width // TILE):
        a = ua[:, :, :, j * TILE : (j + 1) * TILE].reshape(batches * rows, TILE)
        gb[chunk] = dot(a, gradh, 0, 0).astype(LOW)
        store(2 * batches + chunk, gb.at[chunk], grads_ref.at[chunk]).start()
        chunk += 1
    gb[chunk] = dot(tall(cc), tall(g1a), 0, 0).astype(LOW)
    store(2 * batches + chunk, gb.at[chunk], grads_ref.at[chunk]).start()
    chunk += 1
    for i in range(3):
        d = dpr[:, i].reshape(batches * rows, head_cols)
        for j in range(width // TILE):
            a = xa[:, :, :, j * TILE : (j + 1) * TILE].reshape(batches * rows, TILE)
            gb[chunk, :, j * TILE : (j + 1) * TILE] = dot(a, d, 0, 0).astype(LOW)
        store(2 * batches + chunk, gb.at[chunk], grads_ref.at[chunk]).start()
        chunk += 1
    finishes[PHASES - 1](batches - 1)
    vgrad_ref[...] = vg[...]
    for s in range(batches):
        store(s, cot.at[s], out_ref.at[s]).wait()
        store(batches + s, gin.at[s], gin_ref.at[s]).wait()
    for i in range(chunk):
        store(2 * batches + i, gb.at[i], grads_ref.at[i]).wait()

    def drain(i, carry):
        for p in range(PHASES):
            ag_y(p, i, t).wait_send()
            ag_c(p, i, t).wait_send()
            ag_f(p, i, t_y).wait_send()
        return carry

    lax.fori_loop(0, batches, drain, 0)


def run_layer(lengths, x, cot, wqkv, wout, wup, wdown, vec):
    batches, block, width = x.shape
    rows = 4 * block
    head_cols = wout.shape[0]
    heads = head_cols // HD
    hidden = wup.shape[1]
    chunks = hidden // TILE + width // TILE + 1 + 3
    any_space = pl.BlockSpec(memory_space=pl.ANY)
    vmem = pl.BlockSpec(memory_space=pltpu.VMEM)
    dma = pltpu.SemaphoreType.DMA
    low = lambda *shape: pltpu.VMEM(shape, LOW)
    wide = lambda *shape: pltpu.VMEM(shape, F32)
    gathered = low(batches, 4, block, width)
    scratch = [
        gathered,
        low(3, width, head_cols),
        low(head_cols, width),
        low(width, hidden),
        low(hidden, width),
        low(batches, 3, rows, head_cols),
        low(batches, heads, rows, rows),
        low(batches, rows, head_cols),
        gathered,
        low(batches, rows, hidden),
        low(batches, rows, hidden),
        gathered,
        gathered,
        low(batches, 3, rows, head_cols),
        low(batches, 2, 2, block, width),
        low(batches, 2, block, width),
        low(batches, block, width),
        low(batches, block, width),
        wide(batches, block, width),
        wide(batches, block, 128),
        wide(batches, block, width),
        low(batches, block, width),
        low(batches, block, width),
        low(chunks, TILE, width),
        wide(8, width),
        dma((batches + 5,)),
        dma((2 * batches + chunks,)),
    ] + [dma((PHASES, batches))] * 10
    return pl.pallas_call(
        layer_kernel,
        out_shape=(
            jax.ShapeDtypeStruct((batches, block, width), LOW),
            jax.ShapeDtypeStruct((batches, block, width), LOW),
            jax.ShapeDtypeStruct((chunks, TILE, width), LOW),
            jax.ShapeDtypeStruct((8, width), F32),
        ),
        in_specs=[pl.BlockSpec(memory_space=pltpu.SMEM)] + [any_space] * 6 + [vmem],
        out_specs=(any_space, any_space, any_space, vmem),
        scratch_shapes=scratch,
        compiler_params=pltpu.CompilerParams(
            collective_id=0, has_side_effects=True, vmem_limit_bytes=62 << 20
        ),
        name="layer",
    )(lengths, x, cot, wqkv, wout, wup, wdown, vec)


def per_device(
    inputs,
    lengths,
    cotangent,
    w_qkv,
    b_query,
    b_value,
    w_out,
    b_out,
    ln1_gain,
    ln1_bias,
    w_up,
    b_up,
    w_down,
    b_down,
    ln2_gain,
    ln2_bias,
):
    width = inputs.shape[3]
    head_cols = w_out.shape[0]
    hidden = w_up.shape[1]
    narrow = jnp.concatenate([b_query, b_value, jnp.zeros((width - 2 * head_cols,), LOW)])
    vec = jnp.stack([b_out, ln1_gain, ln1_bias, b_down, ln2_gain, ln2_bias, b_up, narrow]).astype(F32)
    output, grad_inputs, grads, vgrad = run_layer(
        lengths,
        inputs[0],
        cotangent[0],
        jnp.transpose(w_qkv, (1, 0, 2)),
        w_out,
        w_up,
        w_down,
        vec,
    )
    grads = lax.psum(grads, "dp").astype(F32)
    shared = lax.psum(vgrad[:6], ("dp", "tensor"))
    split = lax.psum(vgrad[6:], "dp")
    down = hidden // TILE
    up = down + width // TILE
    grad_down = grads[:down].reshape(hidden, width)
    grad_up = grads[down:up].reshape(width, hidden)
    grad_out = grads[up]
    grad_qkv = grads[up + 1 :].reshape(3, TILE, width // TILE, head_cols)
    grad_qkv = jnp.transpose(grad_qkv, (2, 1, 0, 3)).reshape(width, 3, head_cols)
    return (
        output[None],
        grad_inputs[None],
        grad_qkv,
        split[1, :head_cols],
        split[1, head_cols : 2 * head_cols],
        grad_out,
        shared[0],
        shared[1],
        shared[2],
        grad_up,
        split[0],
        grad_down,
        shared[3],
        shared[4],
        shared[5],
    )


def solution(mesh):
    return jax.shard_map(
        per_device,
        mesh=mesh,
        in_specs=(
            P("dp", None, "tensor", None),
            P("dp", None),
            P("dp", None, "tensor", None),
            P(None, None, "tensor"),
            P("tensor"),
            P("tensor"),
            P("tensor", None),
            P(),
            P(),
            P(),
            P(None, "tensor"),
            P("tensor"),
            P("tensor", None),
            P(),
            P(),
            P(),
        ),
        out_specs=(
            P("dp", None, "tensor", None),
            P("dp", None, "tensor", None),
            P(None, None, "tensor"),
            P("tensor"),
            P("tensor"),
            P("tensor", None),
            P(),
            P(),
            P(),
            P(None, "tensor"),
            P("tensor"),
            P("tensor", None),
            P(),
            P(),
            P(),
        ),
        check_vma=False,
    )
```

```python
import functools

import jax
import jax.numpy as jnp
from jax import lax
from jax.experimental import pallas as pl
from jax.experimental.pallas import tpu as pltpu
from jax.sharding import PartitionSpec as P

HD = 64
EPSILON = 1e-05
F32 = jnp.float32
LOW = jnp.bfloat16
MESH = pl.DeviceIdType.MESH
TILE = 256
UNIT = 64
PHASES = 4


def dot(left, right, left_dim=1, right_dim=0):
    return lax.dot_general(
        left, right, (((left_dim,), (right_dim,)), ((), ())), preferred_element_type=F32
    )


def row_sum(values):
    return jnp.sum(values, axis=0, keepdims=True)


def row_mean(values):
    return jnp.mean(values, axis=-1, keepdims=True)


def gelu_parts(h):
    t = 1.0 / (1.0 + 0.23164188 * jnp.abs(h))
    density = jnp.exp(-0.5 * h * h)
    series = t * (
        0.127414796
        + t * (-0.142248368 + t * (0.7107068705 + t * (-0.7265760135 + t * 0.5307027145)))
    )
    tail = series * density
    return jnp.where(h < 0.0, tail, 1.0 - tail), density * 0.3989422804014327


def layer_kernel(
    lengths_ref,
    x_ref,
    cot_ref,
    wqkv_ref,
    wout_ref,
    wup_ref,
    wdown_ref,
    vec_ref,
    out_ref,
    gin_ref,
    grads_ref,
    vgrad_ref,
    xa,
    wq,
    wo,
    wu,
    wd,
    qkv,
    pt,
    cc,
    ua,
    act,
    gp,
    g2a,
    g1a,
    dpr,
    part,
    rc,
    ys,
    ry,
    xh1,
    rstd1,
    resid,
    cot,
    gin,
    gb,
    vg,
    load_sem,
    store_sem,
    agy_send,
    agy_recv,
    agc_send,
    agc_recv,
    agf_send,
    agf_recv,
    rsc_send,
    rsc_recv,
    rsy_send,
    rsy_recv,
):
    batches = x_ref.shape[0]
    block = x_ref.shape[1]
    width = x_ref.shape[2]
    head_cols = wo.shape[0]
    hidden = wu.shape[1]
    rows = 4 * block
    pairs = head_cols // 128
    t = lax.axis_index("tensor")
    c = lax.rem(t, 2)
    y = lax.div(t, 2)
    t_core = y * 2 + (1 - c)
    t_y = (1 - y) * 2 + c
    t_far = (1 - y) * 2 + (1 - c)
    core = {"tensor": t_core}
    across = {"tensor": t_y}

    gathers = (xa, ua, g2a, g1a)

    def remote(src, dst, send, recv, device):
        return pltpu.make_async_remote_copy(
            src_ref=src, dst_ref=dst, send_sem=send, recv_sem=recv, device_id=device, device_id_type=MESH
        )

    def ag_y(p, s, at, src=None):
        buf = gathers[p]
        return remote(
            buf.at[s, at] if src is None else src, buf.at[s, at], agy_send.at[p, s], agy_recv.at[p, s], across
        )

    def ag_c(p, s, at, src=None):
        buf = gathers[p]
        return remote(
            buf.at[s, at] if src is None else src, buf.at[s, at], agc_send.at[p, s], agc_recv.at[p, s], core
        )

    def ag_f(p, s, at):
        buf = gathers[p]
        return remote(buf.at[s, at], buf.at[s, at], agf_send.at[p, s], agf_recv.at[p, s], core)

    def rs_c(p, s):
        return remote(part.at[s, 1 - c], rc.at[s], rsc_send.at[p, s], rsc_recv.at[p, s], core)

    def rs_y(p, s):
        return remote(ys.at[s], ry.at[s], rsy_send.at[p, s], rsy_recv.at[p, s], across)

    def load(index, src, dst):
        return pltpu.make_async_copy(src, dst, load_sem.at[index])

    def store(index, src, dst):
        return pltpu.make_async_copy(src, dst, store_sem.at[index])

    loads = [load(s, x_ref.at[s], xa.at[s, t]) for s in range(batches)]
    n = batches
    load_wq = load(n, wqkv_ref, wq)
    load_wo = load(n + 1, wout_ref, wo)
    load_wu = load(n + 2, wup_ref, wu)
    load_wd = load(n + 3, wdown_ref, wd)
    load_cot = load(n + 4, cot_ref, cot)

    barrier = pltpu.get_barrier_semaphore()
    for device in (core, across):
        pl.semaphore_signal(barrier, inc=1, device_id=device, device_id_type=MESH)
    for cp in loads:
        cp.start()
    load_wq.start()
    load_wo.start()
    pl.semaphore_wait(barrier, 2)
    for s in range(batches):
        ag_y(0, s, t, x_ref.at[s]).start()
        ag_c(0, s, t, x_ref.at[s]).start()
    load_wu.start()
    load_wd.start()
    load_cot.start()

    vg[...] = jnp.zeros_like(vg)
    lane = lax.broadcasted_iota(jnp.int32, (rows, 128), 1)
    low_half = lane < HD
    empty = jnp.zeros((rows, 128), LOW)

    def masked(values, h):
        return jnp.where(low_half, values, empty) if h == 0 else jnp.where(low_half, empty, values)

    def vec(i):
        return vec_ref[i : i + 1, :]

    def whole(ref, s):
        return ref[s].reshape(rows, width)

    def put_part(s, j, values):
        values = values.astype(LOW)
        for b in range(4):
            part[s, b % 2, b // 2, :, j * TILE : (j + 1) * TILE] = values[b * block : (b + 1) * block]

    def compute_a(s):
        tokens = whole(xa, s)
        q = dot(tokens, wq[0]) + vec_ref[7:8, :head_cols]
        qkv[s, 0] = q.astype(LOW) * LOW(HD ** (-0.5))
        qkv[s, 1] = dot(tokens, wq[1]).astype(LOW)
        v = dot(tokens, wq[2]) + vec_ref[7:8, head_cols : 2 * head_cols]
        qkv[s, 2] = v.astype(LOW)
        keys_valid = lax.broadcasted_iota(jnp.int32, (rows, rows), 0) < lengths_ref[0, s]
        for j in range(pairs):
            cols = slice(j * 128, (j + 1) * 128)
            q, k, v = qkv[s, 0, :, cols], qkv[s, 1, :, cols], qkv[s, 2, :, cols]
            context = jnp.zeros((128, rows), F32)
            for h in range(2):
                scores = dot(k, masked(q, h), 1, 1)
                scores = jnp.where(keys_valid, scores, -1e30)
                weights = jnp.exp(scores - jnp.max(scores, axis=0, keepdims=True))
                p = (weights * (1.0 / row_sum(weights))).astype(LOW)
                pt[s, 2 * j + h] = p
                context = context + dot(masked(v, h).T, p)
            cc[s, :, cols] = context.T.astype(LOW)
        context = cc[s]
        for j in range(width // TILE):
            put_part(s, j, dot(context, wo[:, j * TILE : (j + 1) * TILE]))

    def compute_c(s):
        normed = whole(ua, s)
        for j in range(hidden // TILE):
            cols = slice(j * TILE, (j + 1) * TILE)
            h = dot(normed, wu[:, cols]) + vec_ref[6:7, cols]
            phi, density = gelu_parts(h)
            act[s, :, cols] = (h * phi).astype(LOW)
            gp[s, :, cols] = (phi + h * density).astype(LOW)
        activated = act[s]
        for j in range(width // TILE):
            put_part(s, j, dot(activated, wd[:, j * TILE : (j + 1) * TILE]))

    def compute_e(s):
        grad = whole(g2a, s)
        for j in range(hidden // TILE):
            cols = slice(j * TILE, (j + 1) * TILE)
            gh = gp[s, :, cols].astype(F32) * dot(grad, wd[cols, :], 1, 1)
            vg[6:7, cols] += row_sum(gh)
            gp[s, :, cols] = gh.astype(LOW)
        grad_hidden = gp[s]
        for j in range(width // TILE):
            put_part(s, j, dot(grad_hidden, wu[j * TILE : (j + 1) * TILE, :], 1, 1))

    def compute_g(s):
        grad_context = dot(whole(g1a, s), wo[...], 1, 1).astype(LOW)
        for j in range(pairs):
            cols = slice(j * 128, (j + 1) * 128)
            q, k, v = qkv[s, 0, :, cols], qkv[s, 1, :, cols], qkv[s, 2, :, cols]
            gc = grad_context[:, cols]
            dq = jnp.zeros((128, rows), F32)
            dk = jnp.zeros((rows, 128), F32)
            dv = jnp.zeros((rows, 128), F32)
            for h in range(2):
                gc_h = masked(gc, h)
                p = pt[s, 2 * j + h]
                wide = p.astype(F32)
                product = wide * dot(v, gc_h, 1, 1)
                ds = (product - wide * row_sum(product)).astype(LOW)
                dv = dv + dot(p, gc_h)
                dk = dk + dot(ds, masked(q, h))
                dq = dq + dot(masked(k, h).T, ds)
            dq = dq.T * (HD ** (-0.5))
            vg[7:8, cols] += row_sum(dq)
            vg[7:8, head_cols + j * 128 : head_cols + (j + 1) * 128] += row_sum(dv)
            dpr[s, 0, :, cols] = dq.astype(LOW)
            dpr[s, 1, :, cols] = dk.astype(LOW)
            dpr[s, 2, :, cols] = dv.astype(LOW)
        for j in range(width // TILE):
            at = slice(j * TILE, (j + 1) * TILE)
            total = dot(dpr[s, 0], wq[0, at, :], 1, 1)
            total = total + dot(dpr[s, 1], wq[1, at, :], 1, 1)
            total = total + dot(dpr[s, 2], wq[2, at, :], 1, 1)
            put_part(s, j, total)

    computes = (compute_a, compute_c, compute_e, compute_g)

    def reduced(p, s):
        rs_y(p, s).wait()
        rs_c(p, s).wait_send()
        return part[s, c, y].astype(F32) + rc[s, y].astype(F32) + ry[s].astype(F32)

    def send_on(p, s):
        ag_y(p, s, t).start()
        ag_c(p, s, t).start()

    def finish_a(s):
        z = xa[s, t].astype(F32) + (reduced(0, s) + vec(0))
        centred = z - row_mean(z)
        rstd = lax.rsqrt(row_mean(centred * centred) + EPSILON)
        hat = centred * rstd
        xh1[s] = hat
        rstd1[s] = jnp.broadcast_to(rstd, rstd1.shape[1:])
        ua[s, t] = (hat * vec(1) + vec(2)).astype(LOW)
        send_on(1, s)

    def finish_c(s):
        z = (xh1[s] * vec(1) + vec(2)) + (reduced(1, s) + vec(3))
        centred = z - row_mean(z)
        rstd = lax.rsqrt(row_mean(centred * centred) + EPSILON)
        hat = centred * rstd
        valid = t * block + lax.broadcasted_iota(jnp.int32, (block, width), 0) < lengths_ref[0, s]
        incoming = jnp.where(valid, cot[s].astype(F32), 0.0)
        scaled = incoming * vec(4)
        grad = rstd * (scaled - row_mean(scaled) - hat * row_mean(scaled * hat))
        resid[s] = grad
        g2a[s, t] = grad.astype(LOW)
        send_on(2, s)
        cot[s] = jnp.where(valid, hat * vec(4) + vec(5), 0.0).astype(LOW)
        store(s, cot.at[s], out_ref.at[s]).start()
        vg[3:4, :] += row_sum(grad)
        vg[4:5, :] += row_sum(incoming * hat)
        vg[5:6, :] += row_sum(incoming)

    def finish_e(s):
        gu = resid[s] + reduced(2, s)
        hat = xh1[s]
        scaled = gu * vec(1)
        grad = rstd1[s, :, :1] * (scaled - row_mean(scaled) - hat * row_mean(scaled * hat))
        resid[s] = grad
        g1a[s, t] = grad.astype(LOW)
        send_on(3, s)
        vg[0:1, :] += row_sum(grad)
        vg[1:2, :] += row_sum(gu * hat)
        vg[2:3, :] += row_sum(gu)

    def finish_g(s):
        gin[s] = (resid[s] + reduced(3, s)).astype(LOW)
        store(batches + s, gin.at[s], gin_ref.at[s]).start()

    finishes = (finish_a, finish_c, finish_e, finish_g)

    def forward_block(p, s):
        ag_y(p, s, t_y).wait_recv()
        ag_f(p, s, t_y).start()

    def slot(p, s):
        ag_c(p, s, t_core).wait_recv()
        ag_f(p, s, t_far).wait_recv()
        computes[p](s)
        rs_c(p, s).start()
        rs_c(p, s).wait_recv()
        ys[s] = (part[s, c, 1 - y].astype(F32) + rc[s, 1 - y].astype(F32)).astype(LOW)
        rs_y(p, s).start()

    forward_block(0, 0)
    for p in range(PHASES):
        if p == 0:
            for cp in loads:
                cp.wait()
            load_wq.wait()
            load_wo.wait()
        if p == 1:
            load_wu.wait()
            load_wd.wait()
            load_cot.wait()

        def step(s, carry, p=p):
            slot(p, s)
            if p > 0:

                @pl.when(s == 0)
                def _():
                    finishes[p - 1](batches - 1)

            @pl.when(s > 0)
            def _():
                finishes[p](s - 1)

            @pl.when(s < batches - 1)
            def _():
                forward_block(p, s + 1)

            if p < PHASES - 1:

                @pl.when(s == batches - 1)
                def _():
                    forward_block(p + 1, 0)

            return carry

        lax.fori_loop(0, batches, step, 0)
    def tall(ref):
        return ref[...].reshape(batches * rows, -1)

    chunk = 0
    grads2 = tall(g2a)
    for j in range(hidden // TILE):
        a = act[:, :, j * TILE : (j + 1) * TILE].reshape(batches * rows, TILE)
        gb[chunk] = dot(a, grads2, 0, 0).astype(LOW)
        store(2 * batches + chunk, gb.at[chunk], grads_ref.at[chunk]).start()
        chunk += 1
    gradh = tall(gp)
    for j in range(width // TILE):
        a = ua[:, :, :, j * TILE : (j + 1) * TILE].reshape(batches * rows, TILE)
        gb[chunk] = dot(a, gradh, 0, 0).astype(LOW)
        store(2 * batches + chunk, gb.at[chunk], grads_ref.at[chunk]).start()
        chunk += 1
    gb[chunk] = dot(tall(cc), tall(g1a), 0, 0).astype(LOW)
    store(2 * batches + chunk, gb.at[chunk], grads_ref.at[chunk]).start()
    chunk += 1
    fold = width // head_cols
    for i in range(3):
        d = dpr[:, i].reshape(batches * rows, head_cols)
        for j in range(width // TILE):
            a = xa[:, :, :, j * TILE : (j + 1) * TILE].reshape(batches * rows, TILE)
            product = dot(a, d, 0, 0).astype(LOW)
            for h in range(TILE // UNIT):
                piece = j * (TILE // UNIT) + h
                at, col = piece // fold * UNIT, piece % fold * head_cols
                gb[chunk, at : at + UNIT, col : col + head_cols] = product[h * UNIT : (h + 1) * UNIT]
        store(2 * batches + chunk, gb.at[chunk], grads_ref.at[chunk]).start()
        chunk += 1
    finishes[PHASES - 1](batches - 1)
    vgrad_ref[...] = vg[...]
    for s in range(batches):
        store(s, cot.at[s], out_ref.at[s]).wait()
        store(batches + s, gin.at[s], gin_ref.at[s]).wait()
    for i in range(chunk):
        store(2 * batches + i, gb.at[i], grads_ref.at[i]).wait()

    def drain(i, carry):
        for p in range(PHASES):
            ag_y(p, i, t).wait_send()
            ag_c(p, i, t).wait_send()
            ag_f(p, i, t_y).wait_send()
        return carry

    lax.fori_loop(0, batches, drain, 0)


def run_layer(lengths, x, cot, wqkv, wout, wup, wdown, vec):
    batches, block, width = x.shape
    rows = 4 * block
    head_cols = wout.shape[0]
    heads = head_cols // HD
    hidden = wup.shape[1]
    chunks = hidden // TILE + width // TILE + 1 + 3
    any_space = pl.BlockSpec(memory_space=pl.ANY)
    vmem = pl.BlockSpec(memory_space=pltpu.VMEM)
    dma = pltpu.SemaphoreType.DMA
    low = lambda *shape: pltpu.VMEM(shape, LOW)
    wide = lambda *shape: pltpu.VMEM(shape, F32)
    gathered = low(batches, 4, block, width)
    scratch = [
        gathered,
        low(3, width, head_cols),
        low(head_cols, width),
        low(width, hidden),
        low(hidden, width),
        low(batches, 3, rows, head_cols),
        low(batches, heads, rows, rows),
        low(batches, rows, head_cols),
        gathered,
        low(batches, rows, hidden),
        low(batches, rows, hidden),
        gathered,
        gathered,
        low(batches, 3, rows, head_cols),
        low(batches, 2, 2, block, width),
        low(batches, 2, block, width),
        low(batches, block, width),
        low(batches, block, width),
        wide(batches, block, width),
        wide(batches, block, 128),
        wide(batches, block, width),
        low(batches, block, width),
        low(batches, block, width),
        low(chunks, TILE, width),
        wide(8, width),
        dma((batches + 5,)),
        dma((2 * batches + chunks,)),
    ] + [dma((PHASES, batches))] * 10
    return pl.pallas_call(
        layer_kernel,
        out_shape=(
            jax.ShapeDtypeStruct((batches, block, width), LOW),
            jax.ShapeDtypeStruct((batches, block, width), LOW),
            jax.ShapeDtypeStruct((chunks, TILE, width), LOW),
            jax.ShapeDtypeStruct((8, width), F32),
        ),
        in_specs=[pl.BlockSpec(memory_space=pltpu.SMEM)] + [any_space] * 6 + [vmem],
        out_specs=(any_space, any_space, any_space, vmem),
        scratch_shapes=scratch,
        compiler_params=pltpu.CompilerParams(
            collective_id=0, has_side_effects=True, vmem_limit_bytes=62 << 20
        ),
        name="layer",
    )(lengths, x, cot, wqkv, wout, wup, wdown, vec)


HOPS = 11


class Reducer:
    def __init__(self, gb, rx, rz, rm, rb, rn, rq, send_sems, recv_sems):
        dp = lax.axis_index("dp")
        self.x = lax.rem(dp, 2)
        self.z = lax.div(dp, 2)
        self.side = lax.rem(self.z, 2)
        self.m = lax.div(self.z, 2)
        self.inner = self.side != self.m
        self.outer = self.side == self.m
        self.to_x = {"dp": self.z * 2 + (1 - self.x)}
        self.to_pair = {"dp": (self.z + 1 - 2 * self.side) * 2 + self.x}
        self.to_mid = {"dp": (3 - self.z) * 2 + self.x}
        self.gb, self.rx, self.rz, self.rm, self.rb, self.rn, self.rq = gb, rx, rz, rm, rb, rn, rq
        self.send_sems, self.recv_sems = send_sems, recv_sems

    def greet(self, extra=()):
        barrier = pltpu.get_barrier_semaphore()

        def signal(device):
            pl.semaphore_signal(barrier, inc=1, device_id=device, device_id_type=MESH)

        for device in (self.to_x, self.to_pair) + tuple(extra):
            signal(device)

        @pl.when(self.inner)
        def _():
            signal(self.to_mid)
            pl.semaphore_wait(barrier, 3 + len(extra))

        @pl.when(self.outer)
        def _():
            pl.semaphore_wait(barrier, 2 + len(extra))

    def copy(self, hop, k, src, dst, device):
        return pltpu.make_async_remote_copy(
            src_ref=src,
            dst_ref=dst,
            send_sem=self.send_sems.at[hop, k],
            recv_sem=self.recv_sems.at[hop, k],
            device_id=device,
            device_id_type=MESH,
        )

    def ax(self, k):
        return self.copy(0, k, self.gb.at[2 * k, 1 - self.x], self.rx.at[k, 1 - self.x], self.to_x)

    def az(self, k):
        return self.copy(1, k, self.gb.at[2 * k, self.x], self.rz.at[k], self.to_pair)

    def am(self, k):
        return self.copy(2, k, self.gb.at[2 * k, self.x], self.rm.at[k], self.to_mid)

    def ao(self, k):
        return self.copy(3, k, self.rx.at[k, self.x], self.rx.at[k, self.x], self.to_pair)

    def ag(self, k):
        return self.copy(4, k, self.rx.at[k, self.x], self.rx.at[k, self.x], self.to_x)

    def bi(self, k):
        return self.copy(5, k, self.gb.at[2 * k + 1], self.rb.at[k], self.to_pair)

    def bm(self, k):
        return self.copy(6, k, self.gb.at[2 * k + 1, 1 - self.m], self.rn.at[k], self.to_mid)

    def bx(self, k):
        return self.copy(7, k, self.gb.at[2 * k + 1, self.m], self.rq.at[k], self.to_x)

    def bg(self, k):
        return self.copy(8, k, self.rb.at[k, self.m], self.rb.at[k, self.m], self.to_mid)

    def bo(self, k):
        return self.copy(9, k, self.rb.at[k, self.m], self.rb.at[k, self.m], self.to_pair)

    def bp(self, k):
        return self.copy(10, k, self.rb.at[k, 1 - self.m], self.rb.at[k, 1 - self.m], self.to_pair)

    def add(self, out, left, right):
        out[...] = (left[...].astype(F32) + right[...].astype(F32)).astype(LOW)

    def start(self, k):
        self.ax(k).start()

        @pl.when(self.outer)
        def _():
            self.bi(k).start()

    def stage1(self, k):
        self.ax(k).wait()
        own = self.gb.at[2 * k, self.x]
        self.add(own, own, self.rx.at[k, self.x])

        @pl.when(self.outer)
        def _():
            self.az(k).start()

    def stage2(self, k):
        @pl.when(self.inner)
        def _():
            self.bi(k).wait_recv()
            away = self.gb.at[2 * k + 1, 1 - self.m]
            self.add(away, away, self.rb.at[k, 1 - self.m])
            self.bm(k).start()
            own = self.gb.at[2 * k + 1, self.m]
            self.add(own, own, self.rb.at[k, self.m])
            self.az(k).wait_recv()
            own = self.gb.at[2 * k, self.x]
            self.add(own, own, self.rz.at[k])
            self.am(k).start()

    def stage3(self, k):
        @pl.when(self.inner)
        def _():
            self.bm(k).wait()
            own = self.gb.at[2 * k + 1, self.m]
            self.add(own, own, self.rn.at[k])
            self.bx(k).start()
            self.am(k).wait()
            self.add(self.rx.at[k, self.x], self.gb.at[2 * k, self.x], self.rm.at[k])
            self.ao(k).start()
            self.ag(k).start()

    def stage4(self, k):
        @pl.when(self.inner)
        def _():
            self.bx(k).wait()
            self.add(self.rb.at[k, self.m], self.gb.at[2 * k + 1, self.m], self.rq.at[k])
            self.bg(k).start()
            self.bo(k).start()

        @pl.when(self.outer)
        def _():
            self.ao(k).wait_recv()
            self.ag(k).start()

    def stage5(self, k):
        @pl.when(self.inner)
        def _():
            self.bg(k).wait_recv()
            self.bp(k).start()

        self.ag(k).wait_recv()

    def stage6(self, k):
        @pl.when(self.outer)
        def _():
            self.bo(k).wait_recv()
            self.bp(k).wait_recv()

    def drain(self, k):
        self.ag(k).wait_send()

        @pl.when(self.inner)
        def _():
            self.ao(k).wait_send()
            self.bg(k).wait_send()
            self.bo(k).wait_send()
            self.bp(k).wait_send()

        @pl.when(self.outer)
        def _():
            self.az(k).wait_send()
            self.bi(k).wait_send()

    stages = (stage1, stage2, stage3, stage4, stage5, stage6)


VECTOR_HOPS = 6


class VectorReducer:
    def __init__(self, reducer, held, landed, send_sem, recv_sem, shared):
        t = lax.axis_index("tensor")
        c = lax.rem(t, 2)
        y = lax.div(t, 2)
        self.r = reducer
        self.held, self.landed, self.send_sem, self.recv_sem = held, landed, send_sem, recv_sem
        self.shared = shared
        self.devices = (
            {"tensor": y * 2 + (1 - c)},
            {"tensor": (1 - y) * 2 + c},
            reducer.to_x,
            reducer.to_pair,
            reducer.to_mid,
            reducer.to_pair,
        )

    def copy(self, hop):
        src = self.held.at[5 if hop == 5 else hop]
        dst = self.held.at[5] if hop == 5 else self.landed.at[hop]
        return pltpu.make_async_remote_copy(
            src_ref=src,
            dst_ref=dst,
            send_sem=self.send_sem.at[hop],
            recv_sem=self.recv_sem.at[hop],
            device_id=self.devices[hop],
            device_id_type=MESH,
        )

    def begin(self, hop):
        if hop < 3:
            self.copy(hop).start()
        else:

            @pl.when(self.r.outer if hop == 3 else self.r.inner)
            def _():
                self.copy(hop).start()

    def end(self, hop):
        if hop < 3:
            self.copy(hop).wait()
            got = self.landed[hop]
            if hop < 2:
                row = lax.broadcasted_iota(jnp.int32, got.shape, 0)
                got = jnp.where(row < self.shared, got, 0.0)
            self.held[hop + 1] = self.held[hop] + got
        elif hop == 3:

            @pl.when(self.r.outer)
            def _():
                self.copy(3).wait_send()

            @pl.when(self.r.inner)
            def _():
                self.copy(3).wait_recv()
                self.held[4] = self.held[3] + self.landed[3]

        elif hop == 4:

            @pl.when(self.r.inner)
            def _():
                self.copy(4).wait()
                self.held[5] = self.held[4] + self.landed[4]

        else:

            @pl.when(self.r.inner)
            def _():
                self.copy(5).wait_send()

            @pl.when(self.r.outer)
            def _():
                self.copy(5).wait_recv()


def sum_kernel(
    grads_ref, vgrad_ref, gdown_ref, gup_ref, gout_ref, gqkv_ref, vsum_ref,
    gb, rx, rz, rm, rb, rn, rq, held, landed, load_sem, store_sem, send_sems, recv_sems, vsend, vrecv,
):
    chunks = gb.shape[0]
    pairs = chunks // 2
    rows = 2 * gb.shape[2]
    reducer = Reducer(gb, rx, rz, rm, rb, rn, rq, send_sems, recv_sems)
    vectors = VectorReducer(reducer, held, landed, vsend, vrecv, 6)

    def load(k):
        return pltpu.make_async_copy(grads_ref.at[pl.ds(2 * k, 2)], gb.at[pl.ds(2 * k, 2)], load_sem.at[k])

    for k in range(pairs):
        load(k).start()
    held[0] = vgrad_ref[...]
    reducer.greet(vectors.devices[:2])
    n = len(reducer.stages)
    ahead = 2
    for k in range(ahead):
        load(k).wait()
        reducer.start(k)
    vectors.begin(0)

    def tick(now, carry):
        @pl.when(now + ahead < pairs)
        def _():
            load(now + ahead).wait()
            reducer.start(now + ahead)

        for i in range(n):
            k = now - i

            @pl.when(jnp.logical_and(k >= 0, k < pairs))
            def _():
                reducer.stages[i](reducer, k)

        for hop in range(VECTOR_HOPS):

            @pl.when(now == hop)
            def _():
                vectors.end(hop)
                if hop + 1 < VECTOR_HOPS:
                    vectors.begin(hop + 1)

        return carry

    lax.fori_loop(0, pairs + n - 1, tick, 0)
    vsum_ref[...] = held[5]
    stores = []

    def store(src, dst):
        cp = pltpu.make_async_copy(src, dst, store_sem.at[len(stores)])
        cp.start()
        stores.append(cp)

    down = gdown_ref.shape[0] // rows
    up = down + gup_ref.shape[0] // rows
    out = up + gout_ref.shape[0] // rows
    cols = gqkv_ref.shape[2]
    each = gqkv_ref.shape[1] * cols // (rows * gb.shape[3])
    for i in range(chunks):
        src = (rx if i % 2 == 0 else rb).at[i // 2]
        for h in range(2):
            at = rows // 2 * h
            if i < down:
                store(src.at[h], gdown_ref.at[pl.ds(i * rows + at, rows // 2), :])
            elif i < up:
                store(src.at[h], gup_ref.at[pl.ds((i - down) * rows + at, rows // 2), :])
            elif i < out:
                store(src.at[h], gout_ref.at[pl.ds((i - up) * rows + at, rows // 2), :])
            else:
                for j in range(gb.shape[3] // cols):
                    row = ((i - out) % each * (gb.shape[3] // cols) + j) * rows + at
                    store(
                        src.at[h, :, pl.ds(j * cols, cols)],
                        gqkv_ref.at[(i - out) // each, pl.ds(row, rows // 2), :],
                    )
    for cp in stores:
        cp.wait()

    def drain(k, carry):
        reducer.drain(k)
        return carry

    lax.fori_loop(0, pairs, drain, 0)


def run_sum(grads, vgrad, hidden, width, head_cols):
    chunks, half = grads.shape[0], grads.shape[2]
    pairs = chunks // 2
    any_space = pl.BlockSpec(memory_space=pl.ANY)
    vmem = pl.BlockSpec(memory_space=pltpu.VMEM)
    dma = pltpu.SemaphoreType.DMA
    low = lambda *shape: pltpu.VMEM(shape, LOW)
    wide = lambda *shape: pltpu.VMEM(shape, F32)
    return pl.pallas_call(
        sum_kernel,
        out_shape=(
            jax.ShapeDtypeStruct((hidden, width), LOW),
            jax.ShapeDtypeStruct((width, hidden), LOW),
            jax.ShapeDtypeStruct((head_cols, width), LOW),
            jax.ShapeDtypeStruct((3, width, head_cols), LOW),
            jax.ShapeDtypeStruct(vgrad.shape, F32),
        ),
        in_specs=[any_space, vmem],
        out_specs=(any_space,) * 4 + (vmem,),
        scratch_shapes=[
            low(chunks, 2, half, width),
            low(pairs, 2, half, width),
            low(pairs, half, width),
            low(pairs, half, width),
            low(pairs, 2, half, width),
            low(pairs, half, width),
            low(pairs, half, width),
            wide(VECTOR_HOPS, *vgrad.shape),
            wide(VECTOR_HOPS - 1, *vgrad.shape),
            dma((pairs,)),
            dma((chunks * 8,)),
            dma((HOPS, pairs)),
            dma((HOPS, pairs)),
            dma((VECTOR_HOPS,)),
            dma((VECTOR_HOPS,)),
        ],
        compiler_params=pltpu.CompilerParams(
            collective_id=1, has_side_effects=True, vmem_limit_bytes=62 << 20
        ),
        name="gradient_sum",
    )(grads, vgrad)


def per_device(
    inputs,
    lengths,
    cotangent,
    w_qkv,
    b_query,
    b_value,
    w_out,
    b_out,
    ln1_gain,
    ln1_bias,
    w_up,
    b_up,
    w_down,
    b_down,
    ln2_gain,
    ln2_bias,
):
    width = inputs.shape[3]
    head_cols = w_out.shape[0]
    hidden = w_up.shape[1]
    narrow = jnp.concatenate([b_query, b_value, jnp.zeros((width - 2 * head_cols,), LOW)])
    vec = jnp.stack([b_out, ln1_gain, ln1_bias, b_down, ln2_gain, ln2_bias, b_up, narrow]).astype(F32)
    output, grad_inputs, grads, vgrad = run_layer(
        lengths,
        inputs[0],
        cotangent[0],
        jnp.transpose(w_qkv, (1, 0, 2)),
        w_out,
        w_up,
        w_down,
        vec,
    )
    if lax.axis_size("dp") == 8:
        units = grads.reshape(-1, 2, UNIT // 2, width)
        grad_down, grad_up, grad_out, grad_qkv, sums = run_sum(units, vgrad, hidden, width, head_cols)
    else:
        grads = lax.psum(grads, "dp")
        sums = lax.psum(vgrad, "dp")
        sums = jnp.concatenate([lax.psum(sums[:6], "tensor"), sums[6:]])
        down = hidden // TILE
        up = down + width // TILE
        grad_down = grads[:down].reshape(hidden, width)
        grad_up = grads[down:up].reshape(width, hidden)
        grad_out = grads[up]
        grad_qkv = grads[up + 1 :].reshape(3, TILE // UNIT, UNIT, width // head_cols, head_cols)
        grad_qkv = jnp.transpose(grad_qkv, (0, 1, 3, 2, 4)).reshape(3, width, head_cols)
    grad_qkv = jnp.transpose(grad_qkv.astype(F32), (1, 0, 2))
    return (
        output[None],
        grad_inputs[None],
        grad_qkv,
        sums[7, :head_cols],
        sums[7, head_cols : 2 * head_cols],
        grad_out.astype(F32),
        sums[0],
        sums[1],
        sums[2],
        grad_up.astype(F32),
        sums[6],
        grad_down.astype(F32),
        sums[3],
        sums[4],
        sums[5],
    )


def solution(mesh):
    return jax.shard_map(
        per_device,
        mesh=mesh,
        in_specs=(
            P("dp", None, "tensor", None),
            P("dp", None),
            P("dp", None, "tensor", None),
            P(None, None, "tensor"),
            P("tensor"),
            P("tensor"),
            P("tensor", None),
            P(),
            P(),
            P(),
            P(None, "tensor"),
            P("tensor"),
            P("tensor", None),
            P(),
            P(),
            P(),
        ),
        out_specs=(
            P("dp", None, "tensor", None),
            P("dp", None, "tensor", None),
            P(None, None, "tensor"),
            P("tensor"),
            P("tensor"),
            P("tensor", None),
            P(),
            P(),
            P(),
            P(None, "tensor"),
            P("tensor"),
            P("tensor", None),
            P(),
            P(),
            P(),
        ),
        check_vma=False,
    )
```

```python
import functools

import jax
import jax.numpy as jnp
from jax import lax
from jax.experimental import pallas as pl
from jax.experimental.pallas import tpu as pltpu
from jax.sharding import PartitionSpec as P

HD = 64
EPSILON = 1e-05
F32 = jnp.float32
LOW = jnp.bfloat16
MESH = pl.DeviceIdType.MESH
TILE = 256
PHASES = 4
UNIT = 64


def dot(left, right, left_dim=1, right_dim=0):
    return lax.dot_general(
        left, right, (((left_dim,), (right_dim,)), ((), ())), preferred_element_type=F32
    )


def row_sum(values):
    return jnp.sum(values, axis=0, keepdims=True)


def row_mean(values):
    return jnp.mean(values, axis=-1, keepdims=True)


def gelu_parts(h):
    t = 1.0 / (1.0 + 0.23164188 * jnp.abs(h))
    density = jnp.exp(-0.5 * h * h)
    series = t * (
        0.127414796
        + t * (-0.142248368 + t * (0.7107068705 + t * (-0.7265760135 + t * 0.5307027145)))
    )
    tail = series * density
    return jnp.where(h < 0.0, tail, 1.0 - tail), density * 0.3989422804014327


HOPS = 11
RING = 16
SHORT_RING = 8
STAGE_AT = (0, 1, 2, 3, 4, 6)
STORE_TICKS = 3


class Reducer:
    def __init__(self, gb, rx, rz, rm, rb, rn, rq, send_sems, recv_sems):
        dp = lax.axis_index("dp")
        self.x = lax.rem(dp, 2)
        self.z = lax.div(dp, 2)
        self.side = lax.rem(self.z, 2)
        self.m = lax.div(self.z, 2)
        self.inner = self.side != self.m
        self.outer = self.side == self.m
        self.to_x = {"dp": self.z * 2 + (1 - self.x)}
        self.to_pair = {"dp": (self.z + 1 - 2 * self.side) * 2 + self.x}
        self.to_mid = {"dp": (3 - self.z) * 2 + self.x}
        self.gb, self.rx, self.rz, self.rm, self.rb, self.rn, self.rq = gb, rx, rz, rm, rb, rn, rq
        self.send_sems, self.recv_sems = send_sems, recv_sems

    def greet(self, extra=()):
        barrier = pltpu.get_barrier_semaphore()

        def signal(device):
            pl.semaphore_signal(barrier, inc=1, device_id=device, device_id_type=MESH)

        for device in (self.to_x, self.to_pair) + tuple(extra):
            signal(device)

        @pl.when(self.inner)
        def _():
            signal(self.to_mid)
            pl.semaphore_wait(barrier, 3 + len(extra))

        @pl.when(self.outer)
        def _():
            pl.semaphore_wait(barrier, 2 + len(extra))

    def copy(self, hop, k, src, dst, device):
        return pltpu.make_async_remote_copy(
            src_ref=src,
            dst_ref=dst,
            send_sem=self.send_sems.at[hop, k],
            recv_sem=self.recv_sems.at[hop, k],
            device_id=device,
            device_id_type=MESH,
        )

    def ax(self, k):
        return self.copy(0, k, self.gb.at[2 * k, 1 - self.x], self.rx.at[k % RING, 1 - self.x], self.to_x)

    def az(self, k):
        return self.copy(1, k, self.gb.at[2 * k, self.x], self.rz.at[k % SHORT_RING], self.to_pair)

    def am(self, k):
        return self.copy(2, k, self.gb.at[2 * k, self.x], self.rm.at[k % SHORT_RING], self.to_mid)

    def ao(self, k):
        return self.copy(3, k, self.rx.at[k % RING, self.x], self.rx.at[k % RING, self.x], self.to_pair)

    def ag(self, k):
        return self.copy(4, k, self.rx.at[k % RING, self.x], self.rx.at[k % RING, self.x], self.to_x)

    def bi(self, k):
        return self.copy(5, k, self.gb.at[2 * k + 1], self.rb.at[k % RING], self.to_pair)

    def bm(self, k):
        return self.copy(6, k, self.gb.at[2 * k + 1, 1 - self.m], self.rn.at[k % SHORT_RING], self.to_mid)

    def bx(self, k):
        return self.copy(7, k, self.gb.at[2 * k + 1, self.m], self.rq.at[k % SHORT_RING], self.to_x)

    def bg(self, k):
        return self.copy(8, k, self.rb.at[k % RING, self.m], self.rb.at[k % RING, self.m], self.to_mid)

    def bo(self, k):
        return self.copy(9, k, self.rb.at[k % RING, self.m], self.rb.at[k % RING, self.m], self.to_pair)

    def bp(self, k):
        return self.copy(10, k, self.rb.at[k % RING, 1 - self.m], self.rb.at[k % RING, 1 - self.m], self.to_pair)

    def add(self, out, left, right):
        out[...] = (left[...].astype(F32) + right[...].astype(F32)).astype(LOW)

    def start(self, k):
        self.ax(k).start()

        @pl.when(self.outer)
        def _():
            self.bi(k).start()

    def stage1(self, k):
        self.ax(k).wait()
        own = self.gb.at[2 * k, self.x]
        self.add(own, own, self.rx.at[k % RING, self.x])

        @pl.when(self.outer)
        def _():
            self.az(k).start()

    def stage2(self, k):
        @pl.when(self.inner)
        def _():
            self.bi(k).wait_recv()
            away = self.gb.at[2 * k + 1, 1 - self.m]
            self.add(away, away, self.rb.at[k % RING, 1 - self.m])
            self.bm(k).start()
            own = self.gb.at[2 * k + 1, self.m]
            self.add(own, own, self.rb.at[k % RING, self.m])
            self.az(k).wait_recv()
            own = self.gb.at[2 * k, self.x]
            self.add(own, own, self.rz.at[k % SHORT_RING])
            self.am(k).start()

    def stage3(self, k):
        @pl.when(self.inner)
        def _():
            self.bm(k).wait()
            own = self.gb.at[2 * k + 1, self.m]
            self.add(own, own, self.rn.at[k % SHORT_RING])
            self.bx(k).start()
            self.am(k).wait()
            self.add(self.rx.at[k % RING, self.x], self.gb.at[2 * k, self.x], self.rm.at[k % SHORT_RING])
            self.ao(k).start()
            self.ag(k).start()

    def stage4(self, k):
        @pl.when(self.inner)
        def _():
            self.bx(k).wait()
            self.add(self.rb.at[k % RING, self.m], self.gb.at[2 * k + 1, self.m], self.rq.at[k % SHORT_RING])
            self.bg(k).start()
            self.bo(k).start()

        @pl.when(self.outer)
        def _():
            self.ao(k).wait_recv()
            self.ag(k).start()

    def stage5(self, k):
        @pl.when(self.inner)
        def _():
            self.bg(k).wait_recv()
            self.bp(k).start()

        self.ag(k).wait_recv()

    def stage6(self, k):
        @pl.when(self.outer)
        def _():
            self.bo(k).wait_recv()
            self.bp(k).wait_recv()

    def drain(self, k):
        self.ag(k).wait_send()

        @pl.when(self.inner)
        def _():
            self.ao(k).wait_send()
            self.bg(k).wait_send()
            self.bo(k).wait_send()
            self.bp(k).wait_send()

        @pl.when(self.outer)
        def _():
            self.az(k).wait_send()
            self.bi(k).wait_send()

    stages = (stage1, stage2, stage3, stage4, stage5, stage6)


VECTOR_HOPS = 6


class VectorReducer:
    def __init__(self, reducer, held, landed, send_sem, recv_sem, shared):
        t = lax.axis_index("tensor")
        c = lax.rem(t, 2)
        y = lax.div(t, 2)
        self.r = reducer
        self.held, self.landed, self.send_sem, self.recv_sem = held, landed, send_sem, recv_sem
        self.shared = shared
        self.devices = (
            {"tensor": y * 2 + (1 - c)},
            {"tensor": (1 - y) * 2 + c},
            reducer.to_x,
            reducer.to_pair,
            reducer.to_mid,
            reducer.to_pair,
        )

    def copy(self, hop):
        src = self.held.at[5 if hop == 5 else hop]
        dst = self.held.at[5] if hop == 5 else self.landed.at[hop]
        return pltpu.make_async_remote_copy(
            src_ref=src,
            dst_ref=dst,
            send_sem=self.send_sem.at[hop],
            recv_sem=self.recv_sem.at[hop],
            device_id=self.devices[hop],
            device_id_type=MESH,
        )

    def begin(self, hop):
        if hop < 3:
            self.copy(hop).start()
        else:

            @pl.when(self.r.outer if hop == 3 else self.r.inner)
            def _():
                self.copy(hop).start()

    def end(self, hop):
        if hop < 3:
            self.copy(hop).wait()
            got = self.landed[hop]
            if hop < 2:
                row = lax.broadcasted_iota(jnp.int32, got.shape, 0)
                got = jnp.where(row < self.shared, got, 0.0)
            self.held[hop + 1] = self.held[hop] + got
        elif hop == 3:

            @pl.when(self.r.outer)
            def _():
                self.copy(3).wait_send()

            @pl.when(self.r.inner)
            def _():
                self.copy(3).wait_recv()
                self.held[4] = self.held[3] + self.landed[3]

        elif hop == 4:

            @pl.when(self.r.inner)
            def _():
                self.copy(4).wait()
                self.held[5] = self.held[4] + self.landed[4]

        else:

            @pl.when(self.r.inner)
            def _():
                self.copy(5).wait_send()

            @pl.when(self.r.outer)
            def _():
                self.copy(5).wait_recv()


def layer_kernel(
    lengths_ref,
    x_ref,
    cot_ref,
    wqkv_ref,
    wout_ref,
    wup_ref,
    wdown_ref,
    vec_ref,
    out_ref,
    gin_ref,
    gdown_ref,
    gup_ref,
    gout_ref,
    gqkv_ref,
    vsum_ref,
    xa,
    wq,
    wo,
    wu,
    wd,
    qkv,
    pt,
    cc,
    ua,
    act,
    gp,
    g2a,
    g1a,
    part,
    rc,
    ys,
    ry,
    xh1,
    rstd1,
    resid,
    cot,
    gb,
    rx,
    rz,
    rm,
    rb,
    rn,
    rq,
    held,
    landed,
    vg,
    load_sem,
    store_sem,
    agy_send,
    agy_recv,
    agc_send,
    agc_recv,
    agf_send,
    agf_recv,
    rsc_send,
    rsc_recv,
    rsy_send,
    rsy_recv,
    hop_send,
    hop_recv,
    vec_send,
    vec_recv,
    grad_sem,
    *,
    summed,
):
    batches = x_ref.shape[0]
    block = x_ref.shape[1]
    width = x_ref.shape[2]
    head_cols = wo.shape[0]
    hidden = wu.shape[1]
    rows = 4 * block
    pairs = head_cols // 128
    t = lax.axis_index("tensor")
    c = lax.rem(t, 2)
    y = lax.div(t, 2)
    t_core = y * 2 + (1 - c)
    t_y = (1 - y) * 2 + c
    t_far = (1 - y) * 2 + (1 - c)
    core = {"tensor": t_core}
    across = {"tensor": t_y}

    gathers = (xa, ua, g2a, g1a)

    def remote(src, dst, send, recv, device):
        return pltpu.make_async_remote_copy(
            src_ref=src, dst_ref=dst, send_sem=send, recv_sem=recv, device_id=device, device_id_type=MESH
        )

    def ag_y(p, s, at, src=None):
        buf = gathers[p]
        return remote(
            buf.at[s, at] if src is None else src, buf.at[s, at], agy_send.at[p, s], agy_recv.at[p, s], across
        )

    def ag_c(p, s, at, src=None):
        buf = gathers[p]
        return remote(
            buf.at[s, at] if src is None else src, buf.at[s, at], agc_send.at[p, s], agc_recv.at[p, s], core
        )

    def ag_f(p, s, at):
        buf = gathers[p]
        return remote(buf.at[s, at], buf.at[s, at], agf_send.at[p, s], agf_recv.at[p, s], core)

    def rs_c(p, s):
        return remote(part.at[s, 1 - c], rc.at[s], rsc_send.at[p, s], rsc_recv.at[p, s], core)

    def rs_y(p, s):
        return remote(ys.at[s], ry.at[s], rsy_send.at[p, s], rsy_recv.at[p, s], across)

    def load(index, src, dst):
        return pltpu.make_async_copy(src, dst, load_sem.at[index])

    def store(index, src, dst):
        return pltpu.make_async_copy(src, dst, store_sem.at[index])

    loads = [load(s, x_ref.at[s], xa.at[s, t]) for s in range(batches)]
    n = batches
    load_wq = load(n, wqkv_ref, wq)
    load_wo = load(n + 1, wout_ref, wo)
    load_wu = load(n + 2, wup_ref, wu)
    load_wd = load(n + 3, wdown_ref, wd)
    load_cot = load(n + 4, cot_ref, cot)

    for cp in loads:
        cp.start()
    if summed:
        reducer = Reducer(gb, rx, rz, rm, rb, rn, rq, hop_send, hop_recv)
        vectors = VectorReducer(reducer, held, landed, vec_send, vec_recv, 6)
        reducer.greet((core, across))
    else:
        barrier = pltpu.get_barrier_semaphore()
        for device in (core, across):
            pl.semaphore_signal(barrier, inc=1, device_id=device, device_id_type=MESH)
        pl.semaphore_wait(barrier, 2)
    for s in range(batches):
        ag_y(0, s, t, x_ref.at[s]).start()
        ag_c(0, s, t, x_ref.at[s]).start()
    load_wq.start()
    load_wo.start()
    load_wu.start()
    load_wd.start()
    load_cot.start()

    vg[...] = jnp.zeros_like(vg)
    lane = lax.broadcasted_iota(jnp.int32, (rows, 128), 1)
    low_half = lane < HD
    empty = jnp.zeros((rows, 128), LOW)

    def masked(values, h):
        return jnp.where(low_half, values, empty) if h == 0 else jnp.where(low_half, empty, values)

    def vec(i):
        return vec_ref[i : i + 1, :]

    def whole(ref, s):
        return ref[s].reshape(rows, width)

    def put_part(s, j, values):
        values = values.astype(LOW)
        for b in range(4):
            part[s, b % 2, b // 2, :, j * TILE : (j + 1) * TILE] = values[b * block : (b + 1) * block]

    def compute_a(s):
        tokens = whole(xa, s)
        q = dot(tokens, wq[0]) + vec_ref[7:8, :head_cols]
        qkv[s, 0] = q.astype(LOW) * LOW(HD ** (-0.5))
        qkv[s, 1] = dot(tokens, wq[1]).astype(LOW)
        v = dot(tokens, wq[2]) + vec_ref[7:8, head_cols : 2 * head_cols]
        qkv[s, 2] = v.astype(LOW)
        keys_valid = lax.broadcasted_iota(jnp.int32, (rows, rows), 0) < lengths_ref[0, s]
        for j in range(pairs):
            cols = slice(j * 128, (j + 1) * 128)
            q, k, v = qkv[s, 0, :, cols], qkv[s, 1, :, cols], qkv[s, 2, :, cols]
            context = jnp.zeros((128, rows), F32)
            for h in range(2):
                scores = dot(k, masked(q, h), 1, 1)
                scores = jnp.where(keys_valid, scores, -1e30)
                weights = jnp.exp(scores - jnp.max(scores, axis=0, keepdims=True))
                p = (weights * (1.0 / row_sum(weights))).astype(LOW)
                pt[s, 2 * j + h] = p
                context = context + dot(masked(v, h).T, p)
            cc[s, :, cols] = context.T.astype(LOW)
        context = cc[s]
        for j in range(width // TILE):
            put_part(s, j, dot(context, wo[:, j * TILE : (j + 1) * TILE]))

    def compute_c(s):
        normed = whole(ua, s)
        for j in range(hidden // TILE):
            cols = slice(j * TILE, (j + 1) * TILE)
            h = dot(normed, wu[:, cols]) + vec_ref[6:7, cols]
            phi, density = gelu_parts(h)
            act[s, :, cols] = (h * phi).astype(LOW)
            gp[s, :, cols] = (phi + h * density).astype(LOW)
        activated = act[s]
        for j in range(width // TILE):
            put_part(s, j, dot(activated, wd[:, j * TILE : (j + 1) * TILE]))

    def compute_e(s):
        grad = whole(g2a, s)
        for j in range(hidden // TILE):
            cols = slice(j * TILE, (j + 1) * TILE)
            gh = gp[s, :, cols].astype(F32) * dot(grad, wd[cols, :], 1, 1)
            vg[6:7, cols] += row_sum(gh)
            gp[s, :, cols] = gh.astype(LOW)
        grad_hidden = gp[s]
        for j in range(width // TILE):
            put_part(s, j, dot(grad_hidden, wu[j * TILE : (j + 1) * TILE, :], 1, 1))

    def compute_g(s):
        grad_context = dot(whole(g1a, s), wo[...], 1, 1).astype(LOW)
        for j in range(pairs):
            cols = slice(j * 128, (j + 1) * 128)
            q, k, v = qkv[s, 0, :, cols], qkv[s, 1, :, cols], qkv[s, 2, :, cols]
            gc = grad_context[:, cols]
            dq = jnp.zeros((128, rows), F32)
            dk = jnp.zeros((rows, 128), F32)
            dv = jnp.zeros((rows, 128), F32)
            for h in range(2):
                gc_h = masked(gc, h)
                p = pt[s, 2 * j + h]
                wide = p.astype(F32)
                product = wide * dot(v, gc_h, 1, 1)
                ds = (product - wide * row_sum(product)).astype(LOW)
                dv = dv + dot(p, gc_h)
                dk = dk + dot(ds, masked(q, h))
                dq = dq + dot(masked(k, h).T, ds)
            dq = dq.T * (HD ** (-0.5))
            vg[7:8, cols] += row_sum(dq)
            vg[7:8, head_cols + j * 128 : head_cols + (j + 1) * 128] += row_sum(dv)
            qkv[s, 0, :, cols] = dq.astype(LOW)
            qkv[s, 1, :, cols] = dk.astype(LOW)
            qkv[s, 2, :, cols] = dv.astype(LOW)
        for j in range(width // TILE):
            at = slice(j * TILE, (j + 1) * TILE)
            total = dot(qkv[s, 0], wq[0, at, :], 1, 1)
            total = total + dot(qkv[s, 1], wq[1, at, :], 1, 1)
            total = total + dot(qkv[s, 2], wq[2, at, :], 1, 1)
            put_part(s, j, total)

    computes = (compute_a, compute_c, compute_e, compute_g)

    def reduced(p, s):
        rs_y(p, s).wait()
        rs_c(p, s).wait_send()
        return part[s, c, y].astype(F32) + rc[s, y].astype(F32) + ry[s].astype(F32)

    def send_on(p, s):
        ag_y(p, s, t).start()
        ag_c(p, s, t).start()

    def finish_a(s):
        z = xa[s, t].astype(F32) + (reduced(0, s) + vec(0))
        centred = z - row_mean(z)
        rstd = lax.rsqrt(row_mean(centred * centred) + EPSILON)
        hat = centred * rstd
        xh1[s] = hat
        rstd1[s] = jnp.broadcast_to(rstd, rstd1.shape[1:])
        ua[s, t] = (hat * vec(1) + vec(2)).astype(LOW)
        send_on(1, s)

    def finish_c(s):
        z = (xh1[s] * vec(1) + vec(2)) + (reduced(1, s) + vec(3))
        centred = z - row_mean(z)
        rstd = lax.rsqrt(row_mean(centred * centred) + EPSILON)
        hat = centred * rstd
        valid = t * block + lax.broadcasted_iota(jnp.int32, (block, width), 0) < lengths_ref[0, s]
        incoming = jnp.where(valid, cot[s].astype(F32), 0.0)
        scaled = incoming * vec(4)
        grad = rstd * (scaled - row_mean(scaled) - hat * row_mean(scaled * hat))
        resid[s] = grad
        g2a[s, t] = grad.astype(LOW)
        send_on(2, s)
        cot[s] = jnp.where(valid, hat * vec(4) + vec(5), 0.0).astype(LOW)
        store(s, cot.at[s], out_ref.at[s]).start()
        vg[3:4, :] += row_sum(grad)
        vg[4:5, :] += row_sum(incoming * hat)
        vg[5:6, :] += row_sum(incoming)

    def finish_e(s):
        gu = resid[s] + reduced(2, s)
        hat = xh1[s]
        scaled = gu * vec(1)
        grad = rstd1[s, :, :1] * (scaled - row_mean(scaled) - hat * row_mean(scaled * hat))
        resid[s] = grad
        g1a[s, t] = grad.astype(LOW)
        send_on(3, s)
        vg[0:1, :] += row_sum(grad)
        vg[1:2, :] += row_sum(gu * hat)
        vg[2:3, :] += row_sum(gu)

    def finish_g(s):
        store(s, cot.at[s], out_ref.at[s]).wait()
        cot[s] = (resid[s] + reduced(3, s)).astype(LOW)
        store(batches + s, cot.at[s], gin_ref.at[s]).start()

    finishes = (finish_a, finish_c, finish_e, finish_g)

    def forward_block(p, s):
        ag_y(p, s, t_y).wait_recv()
        ag_f(p, s, t_y).start()

    def gathered(p, s):
        ag_c(p, s, t_core).wait_recv()
        ag_f(p, s, t_far).wait_recv()

    def send_sums(p, s):
        rs_c(p, s).start()

    def pass_sums(p, s):
        rs_c(p, s).wait_recv()
        ys[s] = (part[s, c, 1 - y].astype(F32) + rc[s, 1 - y].astype(F32)).astype(LOW)
        rs_y(p, s).start()

    def tall(values):
        return values.reshape(batches * rows, -1)

    per_piece = TILE // UNIT
    down_pieces = hidden // TILE
    up_pieces = width // TILE
    early_pieces = down_pieces + up_pieces
    pieces = early_pieces + 1 + 3

    def piece(d):
        if d < down_pieces:
            cols = slice(d * TILE, (d + 1) * TILE)
            product = dot(tall(act[:, :, cols]), tall(g2a[...]), 0, 0)
        elif d < early_pieces:
            cols = slice((d - down_pieces) * TILE, (d - down_pieces + 1) * TILE)
            product = dot(tall(ua[:, :, :, cols]), tall(gp[...]), 0, 0)
        elif d == early_pieces:
            product = dot(tall(cc[...]), tall(g1a[...]), 0, 0)
        else:
            right = tall(qkv[:, d - early_pieces - 1])
            for j in range(per_piece):
                cols = slice(j * TILE, (j + 1) * TILE)
                product = dot(tall(xa[:, :, :, cols]), right, 0, 0).astype(LOW)
                for h in range(per_piece):
                    gb[d * per_piece + j, :, :, h * head_cols : (h + 1) * head_cols] = product[
                        h * UNIT : (h + 1) * UNIT
                    ].reshape(2, UNIT // 2, head_cols)
            return
        product = product.astype(LOW)
        for u in range(per_piece):
            gb[d * per_piece + u] = product[u * UNIT : (u + 1) * UNIT].reshape(2, UNIT // 2, width)

    def unit_stores(i, src):
        def make(n, src, dst):
            return pltpu.make_async_copy(src, dst, grad_sem.at[i, n])

        if i < down_pieces * per_piece:
            return [make(0, src, gdown_ref.at[i])]
        i_up = i - down_pieces * per_piece
        if i_up < up_pieces * per_piece:
            return [make(0, src, gup_ref.at[i_up])]
        i_out = i - early_pieces * per_piece
        if i_out < per_piece:
            return [make(0, src, gout_ref.at[i_out])]
        i_qkv = i_out - per_piece
        kind, j = i_qkv // per_piece, i_qkv % per_piece
        return [
            make(h, src.at[:, :, pl.ds(h * head_cols, head_cols)], gqkv_ref.at[kind, j * per_piece + h])
            for h in range(per_piece)
        ]

    unit_pairs = pieces * per_piece // 2

    def pair_stores(k):
        return unit_stores(2 * k, rx.at[k % RING]) + unit_stores(2 * k + 1, rb.at[k % RING])

    ticks = iter(range(-1, unit_pairs + STAGE_AT[-1] + STORE_TICKS + 1))

    def tick():
        now = next(ticks, None)
        if now is None:
            return False
        if 0 <= now - STAGE_AT[-1] - STORE_TICKS < unit_pairs:
            reducer.drain(now - STAGE_AT[-1] - STORE_TICKS)
            for cp in pair_stores(now - STAGE_AT[-1] - STORE_TICKS):
                cp.wait()
        k = now + 1
        if k < unit_pairs:
            if 2 * k % per_piece == 0:
                piece(2 * k // per_piece)
            reducer.start(k)
        for stage, at in zip(reducer.stages, STAGE_AT):
            if 0 <= now - at < unit_pairs:
                stage(reducer, now - at)
        if 0 <= now - STAGE_AT[-1] < unit_pairs:
            for cp in pair_stores(now - STAGE_AT[-1]):
                cp.start()
        return True

    def previous(p, s):
        return (p, s - 1) if s > 0 else (p - 1, batches - 1)

    def following(p, s):
        return (p, s + 1) if s < batches - 1 else (p + 1, 0)

    def step(s, carry, p):
        gathered(p, s)
        computes[p](s)
        send_sums(p, s)
        pass_sums(p, s)
        if p > 0:

            @pl.when(s == 0)
            def _():
                finishes[p - 1](batches - 1)

        @pl.when(s > 0)
        def _():
            finishes[p](s - 1)

        if p == 2:
            forward_block(p, s + 1)
        else:

            @pl.when(s < batches - 1)
            def _():
                forward_block(p, s + 1)

            @pl.when(s == batches - 1)
            def _():
                forward_block(p + 1, 0)

        return carry

    forward_block(0, 0)
    for cp in loads:
        cp.wait()
    load_wq.wait()
    load_wo.wait()
    lax.fori_loop(0, batches, functools.partial(step, p=0), 0)
    load_wu.wait()
    load_wd.wait()
    load_cot.wait()
    lax.fori_loop(0, batches, functools.partial(step, p=1), 0)
    lax.fori_loop(0, batches - 1, functools.partial(step, p=2), 0)

    def maybe_tick():
        if summed:
            tick()

    for p, s in [(2, batches - 1)] + [(3, s) for s in range(batches)]:
        gathered(p, s)
        if p == 2:
            for _ in range(3):
                maybe_tick()
        computes[p](s)
        maybe_tick()
        send_sums(p, s)
        maybe_tick()
        pass_sums(p, s)
        finishes[previous(p, s)[0]](previous(p, s)[1])
        maybe_tick()
        if following(p, s)[0] < PHASES:
            forward_block(*following(p, s))
            maybe_tick()
    finishes[PHASES - 1](batches - 1)
    if summed:
        held[0] = vg[...]
        vectors.begin(0)
        hop = 0
        while tick():
            if hop < VECTOR_HOPS:
                vectors.end(hop)
                hop += 1
                if hop < VECTOR_HOPS:
                    vectors.begin(hop)
        vsum_ref[...] = held[VECTOR_HOPS - 1]
    else:
        stores = []
        for d in range(pieces):
            piece(d)
            for i in range(d * per_piece, (d + 1) * per_piece):
                stores += unit_stores(i, gb.at[i])
                for cp in unit_stores(i, gb.at[i]):
                    cp.start()
        vsum_ref[...] = vg[...]
        for cp in stores:
            cp.wait()
    for s in range(batches):
        store(batches + s, cot.at[s], gin_ref.at[s]).wait()

    def drain(i, carry):
        for p in range(PHASES):
            ag_y(p, i, t).wait_send()
            ag_c(p, i, t).wait_send()
            ag_f(p, i, t_y).wait_send()
        return carry

    lax.fori_loop(0, batches, drain, 0)


def run_layer(lengths, x, cot, wqkv, wout, wup, wdown, vec, summed):
    batches, block, width = x.shape
    rows = 4 * block
    head_cols = wout.shape[0]
    heads = head_cols // HD
    hidden = wup.shape[1]
    half = UNIT // 2
    down, up, out = hidden // UNIT, width // UNIT, head_cols // UNIT
    units = down + up + out + 3 * out
    ring, short_ring = (RING, SHORT_RING) if summed else (1, 1)
    any_space = pl.BlockSpec(memory_space=pl.ANY)
    vmem = pl.BlockSpec(memory_space=pltpu.VMEM)
    dma = pltpu.SemaphoreType.DMA
    low = lambda *shape: pltpu.VMEM(shape, LOW)
    wide = lambda *shape: pltpu.VMEM(shape, F32)
    gathered = low(batches, 4, block, width)
    scratch = [
        gathered,
        low(3, width, head_cols),
        low(head_cols, width),
        low(width, hidden),
        low(hidden, width),
        low(batches, 3, rows, head_cols),
        low(batches, heads, rows, rows),
        low(batches, rows, head_cols),
        gathered,
        low(batches, rows, hidden),
        low(batches, rows, hidden),
        gathered,
        gathered,
        low(batches, 2, 2, block, width),
        low(batches, 2, block, width),
        low(batches, block, width),
        low(batches, block, width),
        wide(batches, block, width),
        wide(batches, block, 128),
        wide(batches, block, width),
        low(batches, block, width),
        low(units, 2, half, width),
        low(ring, 2, half, width),
        low(short_ring, half, width),
        low(short_ring, half, width),
        low(ring, 2, half, width),
        low(short_ring, half, width),
        low(short_ring, half, width),
        wide(VECTOR_HOPS, 8, width),
        wide(VECTOR_HOPS - 1, 8, width),
        wide(8, width),
        dma((batches + 5,)),
        dma((2 * batches,)),
    ]
    scratch += [dma((PHASES, batches))] * 10 + [dma((HOPS, units // 2))] * 2 + [dma((VECTOR_HOPS,))] * 2
    scratch.append(dma((units, TILE // UNIT)))
    low_out = lambda *shape: jax.ShapeDtypeStruct(shape, LOW)
    return pl.pallas_call(
        functools.partial(layer_kernel, summed=summed),
        out_shape=(
            low_out(batches, block, width),
            low_out(batches, block, width),
            low_out(down, 2, half, width),
            low_out(up, 2, half, hidden),
            low_out(out, 2, half, width),
            low_out(3, width // UNIT, 2, half, head_cols),
            jax.ShapeDtypeStruct((8, width), F32),
        ),
        in_specs=[pl.BlockSpec(memory_space=pltpu.SMEM)] + [any_space] * 6 + [vmem],
        out_specs=(any_space,) * 6 + (vmem,),
        scratch_shapes=scratch,
        compiler_params=pltpu.CompilerParams(
            collective_id=0, has_side_effects=True, vmem_limit_bytes=63 << 20
        ),
        name="layer",
    )(lengths, x, cot, wqkv, wout, wup, wdown, vec)


def per_device(
    inputs,
    lengths,
    cotangent,
    w_qkv,
    b_query,
    b_value,
    w_out,
    b_out,
    ln1_gain,
    ln1_bias,
    w_up,
    b_up,
    w_down,
    b_down,
    ln2_gain,
    ln2_bias,
):
    width = inputs.shape[3]
    head_cols = w_out.shape[0]
    hidden = w_up.shape[1]
    narrow = jnp.concatenate([b_query, b_value, jnp.zeros((width - 2 * head_cols,), LOW)])
    vec = jnp.stack([b_out, ln1_gain, ln1_bias, b_down, ln2_gain, ln2_bias, b_up, narrow]).astype(F32)
    summed = lax.axis_size("dp") == 8
    output, grad_inputs, grad_down, grad_up, grad_out, grad_qkv, sums = run_layer(
        lengths,
        inputs[0],
        cotangent[0],
        jnp.transpose(w_qkv, (1, 0, 2)),
        w_out,
        w_up,
        w_down,
        vec,
        summed,
    )
    if not summed:
        grad_down, grad_up, grad_out, grad_qkv, sums = lax.psum(
            (grad_down, grad_up, grad_out, grad_qkv, sums), "dp"
        )
        sums = jnp.concatenate([lax.psum(sums[:6], "tensor"), sums[6:]])
    grad_down = grad_down.reshape(hidden, width)
    grad_up = grad_up.reshape(width, hidden)
    grad_out = grad_out.reshape(head_cols, width)
    grad_qkv = jnp.transpose(grad_qkv.reshape(3, width, head_cols).astype(F32), (1, 0, 2))
    return (
        output[None],
        grad_inputs[None],
        grad_qkv,
        sums[7, :head_cols],
        sums[7, head_cols : 2 * head_cols],
        grad_out.astype(F32),
        sums[0],
        sums[1],
        sums[2],
        grad_up.astype(F32),
        sums[6],
        grad_down.astype(F32),
        sums[3],
        sums[4],
        sums[5],
    )


def solution(mesh):
    return jax.shard_map(
        per_device,
        mesh=mesh,
        in_specs=(
            P("dp", None, "tensor", None),
            P("dp", None),
            P("dp", None, "tensor", None),
            P(None, None, "tensor"),
            P("tensor"),
            P("tensor"),
            P("tensor", None),
            P(),
            P(),
            P(),
            P(None, "tensor"),
            P("tensor"),
            P("tensor", None),
            P(),
            P(),
            P(),
        ),
        out_specs=(
            P("dp", None, "tensor", None),
            P("dp", None, "tensor", None),
            P(None, None, "tensor"),
            P("tensor"),
            P("tensor"),
            P("tensor", None),
            P(),
            P(),
            P(),
            P(None, "tensor"),
            P("tensor"),
            P("tensor", None),
            P(),
            P(),
            P(),
        ),
        check_vma=False,
    )
```

```python
import functools

import jax
import jax.numpy as jnp
from jax import lax
from jax.experimental import pallas as pl
from jax.experimental.pallas import tpu as pltpu
from jax.sharding import PartitionSpec as P

HD = 64
EPSILON = 1e-05
F32 = jnp.float32
LOW = jnp.bfloat16
MESH = pl.DeviceIdType.MESH
TILE = 256
PHASES = 4
UNIT = 64


def dot(left, right, left_dim=1, right_dim=0):
    return lax.dot_general(
        left, right, (((left_dim,), (right_dim,)), ((), ())), preferred_element_type=F32
    )


def row_sum(values):
    return jnp.sum(values, axis=0, keepdims=True)


def row_mean(values):
    return jnp.mean(values, axis=-1, keepdims=True)


def gelu_parts(h):
    t = 1.0 / (1.0 + 0.23164188 * jnp.abs(h))
    density = jnp.exp(-0.5 * h * h)
    series = t * (
        0.127414796
        + t * (-0.142248368 + t * (0.7107068705 + t * (-0.7265760135 + t * 0.5307027145)))
    )
    tail = series * density
    return jnp.where(h < 0.0, tail, 1.0 - tail), density * 0.3989422804014327


HOPS = 11
RING = 16
SHORT_RING = 8
STAGE_AT = (0, 1, 2, 3, 4, 6)
STORE_TICKS = 3
TICK = ("tick", 0)
SCHEDULE = (
    ("finish", 5),
    ("gather", 6),
    ("compute", 6),
    ("forward", 7),
    ("send", 6),
    ("gather", 7),
    ("compute", 7),
    ("pass", 6),
    ("forward", 8),
    ("gather", 8),
    TICK,
    ("send", 7),
    ("pass", 7),
    TICK,
    ("finish", 6),
    TICK,
    ("compute", 8),
    *[TICK] * 2,
    ("finish", 7),
    ("send", 8),
    ("forward", 9),
    TICK,
    ("gather", 9),
    ("pass", 8),
    TICK,
    ("compute", 9),
    TICK,
    ("forward", 10),
    TICK,
    ("finish", 8),
    ("send", 9),
    TICK,
    ("gather", 10),
    ("pass", 9),
    TICK,
    ("compute", 10),
    ("send", 10),
    TICK,
    ("forward", 11),
    ("pass", 10),
    TICK,
    ("gather", 11),
    ("compute", 11),
    TICK,
    ("send", 11),
    TICK,
    ("pass", 11),
    *[TICK] * 4,
    ("finish", 9),
    ("finish", 10),
    *[TICK] * 2,
    ("finish", 11),
    TICK,
)


class Reducer:
    def __init__(self, gb, rx, rz, rm, rb, rn, rq, send_sems, recv_sems):
        dp = lax.axis_index("dp")
        self.x = lax.rem(dp, 2)
        self.z = lax.div(dp, 2)
        self.side = lax.rem(self.z, 2)
        self.m = lax.div(self.z, 2)
        self.inner = self.side != self.m
        self.outer = self.side == self.m
        self.to_x = {"dp": self.z * 2 + (1 - self.x)}
        self.to_pair = {"dp": (self.z + 1 - 2 * self.side) * 2 + self.x}
        self.to_mid = {"dp": (3 - self.z) * 2 + self.x}
        self.gb, self.rx, self.rz, self.rm, self.rb, self.rn, self.rq = gb, rx, rz, rm, rb, rn, rq
        self.send_sems, self.recv_sems = send_sems, recv_sems

    def greet(self, extra=()):
        barrier = pltpu.get_barrier_semaphore()

        def signal(device):
            pl.semaphore_signal(barrier, inc=1, device_id=device, device_id_type=MESH)

        for device in (self.to_x, self.to_pair) + tuple(extra):
            signal(device)

        @pl.when(self.inner)
        def _():
            signal(self.to_mid)
            pl.semaphore_wait(barrier, 3 + len(extra))

        @pl.when(self.outer)
        def _():
            pl.semaphore_wait(barrier, 2 + len(extra))

    def copy(self, hop, k, src, dst, device):
        return pltpu.make_async_remote_copy(
            src_ref=src,
            dst_ref=dst,
            send_sem=self.send_sems.at[hop, k],
            recv_sem=self.recv_sems.at[hop, k],
            device_id=device,
            device_id_type=MESH,
        )

    def ax(self, k):
        return self.copy(0, k, self.gb.at[2 * k, 1 - self.x], self.rx.at[k % RING, 1 - self.x], self.to_x)

    def az(self, k):
        return self.copy(1, k, self.gb.at[2 * k, self.x], self.rz.at[k % SHORT_RING], self.to_pair)

    def am(self, k):
        return self.copy(2, k, self.gb.at[2 * k, self.x], self.rm.at[k % SHORT_RING], self.to_mid)

    def ao(self, k):
        return self.copy(3, k, self.rx.at[k % RING, self.x], self.rx.at[k % RING, self.x], self.to_pair)

    def ag(self, k):
        return self.copy(4, k, self.rx.at[k % RING, self.x], self.rx.at[k % RING, self.x], self.to_x)

    def bi(self, k):
        return self.copy(5, k, self.gb.at[2 * k + 1], self.rb.at[k % RING], self.to_pair)

    def bm(self, k):
        return self.copy(6, k, self.gb.at[2 * k + 1, 1 - self.m], self.rn.at[k % SHORT_RING], self.to_mid)

    def bx(self, k):
        return self.copy(7, k, self.gb.at[2 * k + 1, self.m], self.rq.at[k % SHORT_RING], self.to_x)

    def bg(self, k):
        return self.copy(8, k, self.rb.at[k % RING, self.m], self.rb.at[k % RING, self.m], self.to_mid)

    def bo(self, k):
        return self.copy(9, k, self.rb.at[k % RING, self.m], self.rb.at[k % RING, self.m], self.to_pair)

    def bp(self, k):
        return self.copy(10, k, self.rb.at[k % RING, 1 - self.m], self.rb.at[k % RING, 1 - self.m], self.to_pair)

    def add(self, out, left, right):
        out[...] = (left[...].astype(F32) + right[...].astype(F32)).astype(LOW)

    def start(self, k):
        self.ax(k).start()

        @pl.when(self.outer)
        def _():
            self.bi(k).start()

    def stage1(self, k):
        self.ax(k).wait()
        own = self.gb.at[2 * k, self.x]
        self.add(own, own, self.rx.at[k % RING, self.x])

        @pl.when(self.outer)
        def _():
            self.az(k).start()

    def stage2(self, k):
        @pl.when(self.inner)
        def _():
            self.bi(k).wait_recv()
            away = self.gb.at[2 * k + 1, 1 - self.m]
            self.add(away, away, self.rb.at[k % RING, 1 - self.m])
            self.bm(k).start()
            own = self.gb.at[2 * k + 1, self.m]
            self.add(own, own, self.rb.at[k % RING, self.m])
            self.az(k).wait_recv()
            own = self.gb.at[2 * k, self.x]
            self.add(own, own, self.rz.at[k % SHORT_RING])
            self.am(k).start()

    def stage3(self, k):
        @pl.when(self.inner)
        def _():
            self.bm(k).wait()
            own = self.gb.at[2 * k + 1, self.m]
            self.add(own, own, self.rn.at[k % SHORT_RING])
            self.bx(k).start()
            self.am(k).wait()
            self.add(self.rx.at[k % RING, self.x], self.gb.at[2 * k, self.x], self.rm.at[k % SHORT_RING])
            self.ao(k).start()
            self.ag(k).start()

    def stage4(self, k):
        @pl.when(self.inner)
        def _():
            self.bx(k).wait()
            self.add(self.rb.at[k % RING, self.m], self.gb.at[2 * k + 1, self.m], self.rq.at[k % SHORT_RING])
            self.bg(k).start()
            self.bo(k).start()

        @pl.when(self.outer)
        def _():
            self.ao(k).wait_recv()
            self.ag(k).start()

    def stage5(self, k):
        @pl.when(self.inner)
        def _():
            self.bg(k).wait_recv()
            self.bp(k).start()

        self.ag(k).wait_recv()

    def stage6(self, k):
        @pl.when(self.outer)
        def _():
            self.bo(k).wait_recv()
            self.bp(k).wait_recv()

    def drain(self, k):
        self.ag(k).wait_send()

        @pl.when(self.inner)
        def _():
            self.ao(k).wait_send()
            self.bg(k).wait_send()
            self.bo(k).wait_send()
            self.bp(k).wait_send()

        @pl.when(self.outer)
        def _():
            self.az(k).wait_send()
            self.bi(k).wait_send()

    stages = (stage1, stage2, stage3, stage4, stage5, stage6)


VECTOR_HOPS = 6


class VectorReducer:
    def __init__(self, reducer, held, landed, send_sem, recv_sem, shared):
        t = lax.axis_index("tensor")
        c = lax.rem(t, 2)
        y = lax.div(t, 2)
        self.r = reducer
        self.held, self.landed, self.send_sem, self.recv_sem = held, landed, send_sem, recv_sem
        self.shared = shared
        self.devices = (
            {"tensor": y * 2 + (1 - c)},
            {"tensor": (1 - y) * 2 + c},
            reducer.to_x,
            reducer.to_pair,
            reducer.to_mid,
            reducer.to_pair,
        )

    def copy(self, hop):
        src = self.held.at[5 if hop == 5 else hop]
        dst = self.held.at[5] if hop == 5 else self.landed.at[hop]
        return pltpu.make_async_remote_copy(
            src_ref=src,
            dst_ref=dst,
            send_sem=self.send_sem.at[hop],
            recv_sem=self.recv_sem.at[hop],
            device_id=self.devices[hop],
            device_id_type=MESH,
        )

    def begin(self, hop):
        if hop < 3:
            self.copy(hop).start()
        else:

            @pl.when(self.r.outer if hop == 3 else self.r.inner)
            def _():
                self.copy(hop).start()

    def end(self, hop):
        if hop < 3:
            self.copy(hop).wait()
            got = self.landed[hop]
            if hop < 2:
                row = lax.broadcasted_iota(jnp.int32, got.shape, 0)
                got = jnp.where(row < self.shared, got, 0.0)
            self.held[hop + 1] = self.held[hop] + got
        elif hop == 3:

            @pl.when(self.r.outer)
            def _():
                self.copy(3).wait_send()

            @pl.when(self.r.inner)
            def _():
                self.copy(3).wait_recv()
                self.held[4] = self.held[3] + self.landed[3]

        elif hop == 4:

            @pl.when(self.r.inner)
            def _():
                self.copy(4).wait()
                self.held[5] = self.held[4] + self.landed[4]

        else:

            @pl.when(self.r.inner)
            def _():
                self.copy(5).wait_send()

            @pl.when(self.r.outer)
            def _():
                self.copy(5).wait_recv()


def layer_kernel(
    lengths_ref,
    x_ref,
    cot_ref,
    wqkv_ref,
    wout_ref,
    wup_ref,
    wdown_ref,
    bout_ref,
    gain1_ref,
    bias1_ref,
    bdown_ref,
    gain2_ref,
    bias2_ref,
    bup_ref,
    bquery_ref,
    bvalue_ref,
    out_ref,
    gin_ref,
    gdown_ref,
    gup_ref,
    gout_ref,
    gqkv_ref,
    vsum_ref,
    xa,
    wq,
    wo,
    wu,
    wd,
    qkv,
    pt,
    cc,
    ua,
    act,
    gp,
    g2a,
    g1a,
    part,
    rc,
    ys,
    ry,
    xh1,
    rstd1,
    resid,
    cot,
    gb,
    rx,
    rz,
    rm,
    rb,
    rn,
    rq,
    held,
    landed,
    vg,
    vec_ref,
    load_sem,
    store_sem,
    agy_send,
    agy_recv,
    agc_send,
    agc_recv,
    agf_send,
    agf_recv,
    rsc_send,
    rsc_recv,
    rsy_send,
    rsy_recv,
    hop_send,
    hop_recv,
    vec_send,
    vec_recv,
    grad_sem,
    *,
    summed,
):
    batches = x_ref.shape[0]
    block = x_ref.shape[1]
    width = x_ref.shape[2]
    head_cols = wo.shape[0]
    hidden = wu.shape[1]
    rows = 4 * block
    pairs = head_cols // 128
    t = lax.axis_index("tensor")
    c = lax.rem(t, 2)
    y = lax.div(t, 2)
    t_core = y * 2 + (1 - c)
    t_y = (1 - y) * 2 + c
    t_far = (1 - y) * 2 + (1 - c)
    core = {"tensor": t_core}
    across = {"tensor": t_y}

    gathers = (xa, ua, g2a, g1a)

    def remote(src, dst, send, recv, device):
        return pltpu.make_async_remote_copy(
            src_ref=src, dst_ref=dst, send_sem=send, recv_sem=recv, device_id=device, device_id_type=MESH
        )

    def ag_y(p, s, at, src=None):
        buf = gathers[p]
        return remote(
            buf.at[s, at] if src is None else src, buf.at[s, at], agy_send.at[p, s], agy_recv.at[p, s], across
        )

    def ag_c(p, s, at, src=None):
        buf = gathers[p]
        return remote(
            buf.at[s, at] if src is None else src, buf.at[s, at], agc_send.at[p, s], agc_recv.at[p, s], core
        )

    def ag_f(p, s, at):
        buf = gathers[p]
        return remote(buf.at[s, at], buf.at[s, at], agf_send.at[p, s], agf_recv.at[p, s], core)

    def rs_c(p, s):
        return remote(part.at[s, 1 - c], rc.at[s], rsc_send.at[p, s], rsc_recv.at[p, s], core)

    def rs_y(p, s):
        return remote(ys.at[s], ry.at[s], rsy_send.at[p, s], rsy_recv.at[p, s], across)

    def load(index, src, dst):
        return pltpu.make_async_copy(src, dst, load_sem.at[index])

    def store(index, src, dst):
        return pltpu.make_async_copy(src, dst, store_sem.at[index])

    loads = [load(s, x_ref.at[s], xa.at[s, t]) for s in range(batches)]
    n = batches
    load_wq = load(n, wqkv_ref, wq)
    load_wo = load(n + 1, wout_ref, wo)
    load_wu = load(n + 2, wup_ref, wu)
    load_wd = load(n + 3, wdown_ref, wd)
    load_cot = load(n + 4, cot_ref, cot)

    for cp in loads:
        cp.start()
    if summed:
        reducer = Reducer(gb, rx, rz, rm, rb, rn, rq, hop_send, hop_recv)
        vectors = VectorReducer(reducer, held, landed, vec_send, vec_recv, 6)
        reducer.greet((core, across))
    else:
        barrier = pltpu.get_barrier_semaphore()
        for device in (core, across):
            pl.semaphore_signal(barrier, inc=1, device_id=device, device_id_type=MESH)
        pl.semaphore_wait(barrier, 2)
    for s in range(batches):
        ag_y(0, s, t, x_ref.at[s]).start()
        ag_c(0, s, t, x_ref.at[s]).start()
    load_wq.start()
    load_wo.start()
    load_wu.start()
    load_wd.start()
    load_cot.start()

    vg[...] = jnp.zeros_like(vg)
    long_refs = (bout_ref, gain1_ref, bias1_ref, bdown_ref, gain2_ref, bias2_ref, bup_ref)
    for i, ref in enumerate(long_refs):
        vec_ref[i : i + 1, :] = ref[...].astype(F32).reshape(1, -1)
    for i, ref in enumerate((bquery_ref, bvalue_ref)):
        vec_ref[7:8, i * head_cols : (i + 1) * head_cols] = ref[...].astype(F32).reshape(1, -1)
    lane = lax.broadcasted_iota(jnp.int32, (rows, 128), 1)
    low_half = lane < HD
    empty = jnp.zeros((rows, 128), LOW)

    def masked(values, h):
        return jnp.where(low_half, values, empty) if h == 0 else jnp.where(low_half, empty, values)

    def vec(i):
        return vec_ref[i : i + 1, :]

    def whole(ref, s):
        return ref[s].reshape(rows, width)

    def put_part(s, j, values):
        values = values.astype(LOW)
        for b in range(4):
            part[s, b % 2, b // 2, :, j * TILE : (j + 1) * TILE] = values[b * block : (b + 1) * block]

    def compute_a(s):
        tokens = whole(xa, s)
        q = dot(tokens, wq[0]) + vec_ref[7:8, :head_cols]
        qkv[s, 0] = q.astype(LOW) * LOW(HD ** (-0.5))
        qkv[s, 1] = dot(tokens, wq[1]).astype(LOW)
        v = dot(tokens, wq[2]) + vec_ref[7:8, head_cols : 2 * head_cols]
        qkv[s, 2] = v.astype(LOW)
        keys_valid = lax.broadcasted_iota(jnp.int32, (rows, rows), 0) < lengths_ref[0, s]
        for j in range(pairs):
            cols = slice(j * 128, (j + 1) * 128)
            q, k, v = qkv[s, 0, :, cols], qkv[s, 1, :, cols], qkv[s, 2, :, cols]
            context = jnp.zeros((128, rows), F32)
            for h in range(2):
                scores = dot(k, masked(q, h), 1, 1)
                scores = jnp.where(keys_valid, scores, -1e30)
                weights = jnp.exp(scores - jnp.max(scores, axis=0, keepdims=True))
                p = (weights * (1.0 / row_sum(weights))).astype(LOW)
                pt[s, 2 * j + h] = p
                context = context + dot(masked(v, h).T, p)
            cc[s, :, cols] = context.T.astype(LOW)
        context = cc[s]
        for j in range(width // TILE):
            put_part(s, j, dot(context, wo[:, j * TILE : (j + 1) * TILE]))

    def compute_c(s):
        normed = whole(ua, s)
        for j in range(hidden // TILE):
            cols = slice(j * TILE, (j + 1) * TILE)
            h = dot(normed, wu[:, cols]) + vec_ref[6:7, cols]
            phi, density = gelu_parts(h)
            act[s, :, cols] = (h * phi).astype(LOW)
            gp[s, :, cols] = (phi + h * density).astype(LOW)
        activated = act[s]
        for j in range(width // TILE):
            put_part(s, j, dot(activated, wd[:, j * TILE : (j + 1) * TILE]))

    def compute_e(s):
        grad = whole(g2a, s)
        for j in range(hidden // TILE):
            cols = slice(j * TILE, (j + 1) * TILE)
            gh = gp[s, :, cols].astype(F32) * dot(grad, wd[cols, :], 1, 1)
            vg[6:7, cols] += row_sum(gh)
            gp[s, :, cols] = gh.astype(LOW)
        grad_hidden = gp[s]
        for j in range(width // TILE):
            put_part(s, j, dot(grad_hidden, wu[j * TILE : (j + 1) * TILE, :], 1, 1))

    def compute_g(s):
        grad_context = dot(whole(g1a, s), wo[...], 1, 1).astype(LOW)
        for j in range(pairs):
            cols = slice(j * 128, (j + 1) * 128)
            q, k, v = qkv[s, 0, :, cols], qkv[s, 1, :, cols], qkv[s, 2, :, cols]
            gc = grad_context[:, cols]
            dq = jnp.zeros((128, rows), F32)
            dk = jnp.zeros((rows, 128), F32)
            dv = jnp.zeros((rows, 128), F32)
            for h in range(2):
                gc_h = masked(gc, h)
                p = pt[s, 2 * j + h]
                wide = p.astype(F32)
                product = wide * dot(v, gc_h, 1, 1)
                ds = (product - wide * row_sum(product)).astype(LOW)
                dv = dv + dot(p, gc_h)
                dk = dk + dot(ds, masked(q, h))
                dq = dq + dot(masked(k, h).T, ds)
            dq = dq.T * (HD ** (-0.5))
            vg[7:8, cols] += row_sum(dq)
            vg[7:8, head_cols + j * 128 : head_cols + (j + 1) * 128] += row_sum(dv)
            qkv[s, 0, :, cols] = dq.astype(LOW)
            qkv[s, 1, :, cols] = dk.astype(LOW)
            qkv[s, 2, :, cols] = dv.astype(LOW)
        for j in range(width // TILE):
            at = slice(j * TILE, (j + 1) * TILE)
            total = dot(qkv[s, 0], wq[0, at, :], 1, 1)
            total = total + dot(qkv[s, 1], wq[1, at, :], 1, 1)
            total = total + dot(qkv[s, 2], wq[2, at, :], 1, 1)
            put_part(s, j, total)

    computes = (compute_a, compute_c, compute_e, compute_g)

    def reduced(p, s):
        rs_y(p, s).wait()
        rs_c(p, s).wait_send()
        return part[s, c, y].astype(F32) + rc[s, y].astype(F32) + ry[s].astype(F32)

    def send_on(p, s):
        ag_y(p, s, t).start()
        ag_c(p, s, t).start()

    def finish_a(s):
        z = xa[s, t].astype(F32) + (reduced(0, s) + vec(0))
        centred = z - row_mean(z)
        rstd = lax.rsqrt(row_mean(centred * centred) + EPSILON)
        hat = centred * rstd
        xh1[s] = hat
        rstd1[s] = jnp.broadcast_to(rstd, rstd1.shape[1:])
        ua[s, t] = (hat * vec(1) + vec(2)).astype(LOW)
        send_on(1, s)

    def finish_c(s):
        z = (xh1[s] * vec(1) + vec(2)) + (reduced(1, s) + vec(3))
        centred = z - row_mean(z)
        rstd = lax.rsqrt(row_mean(centred * centred) + EPSILON)
        hat = centred * rstd
        valid = t * block + lax.broadcasted_iota(jnp.int32, (block, width), 0) < lengths_ref[0, s]
        incoming = jnp.where(valid, cot[s].astype(F32), 0.0)
        scaled = incoming * vec(4)
        grad = rstd * (scaled - row_mean(scaled) - hat * row_mean(scaled * hat))
        resid[s] = grad
        g2a[s, t] = grad.astype(LOW)
        send_on(2, s)
        cot[s] = jnp.where(valid, hat * vec(4) + vec(5), 0.0).astype(LOW)
        store(s, cot.at[s], out_ref.at[s]).start()
        vg[3:4, :] += row_sum(grad)
        vg[4:5, :] += row_sum(incoming * hat)
        vg[5:6, :] += row_sum(incoming)

    def finish_e(s):
        gu = resid[s] + reduced(2, s)
        hat = xh1[s]
        scaled = gu * vec(1)
        grad = rstd1[s, :, :1] * (scaled - row_mean(scaled) - hat * row_mean(scaled * hat))
        resid[s] = grad
        g1a[s, t] = grad.astype(LOW)
        send_on(3, s)
        vg[0:1, :] += row_sum(grad)
        vg[1:2, :] += row_sum(gu * hat)
        vg[2:3, :] += row_sum(gu)

    def finish_g(s):
        store(s, cot.at[s], out_ref.at[s]).wait()
        cot[s] = (resid[s] + reduced(3, s)).astype(LOW)
        store(batches + s, cot.at[s], gin_ref.at[s]).start()

    finishes = (finish_a, finish_c, finish_e, finish_g)

    def forward_block(p, s):
        ag_y(p, s, t_y).wait_recv()
        ag_f(p, s, t_y).start()

    def gathered(p, s):
        ag_c(p, s, t_core).wait_recv()
        ag_f(p, s, t_far).wait_recv()

    def send_sums(p, s):
        rs_c(p, s).start()

    def pass_sums(p, s):
        rs_c(p, s).wait_recv()
        ys[s] = (part[s, c, 1 - y].astype(F32) + rc[s, 1 - y].astype(F32)).astype(LOW)
        rs_y(p, s).start()

    def tall(values):
        return values.reshape(batches * rows, -1)

    per_piece = TILE // UNIT
    down_pieces = hidden // TILE
    up_pieces = width // TILE
    early_pieces = down_pieces + up_pieces
    pieces = early_pieces + 1 + 3

    def piece(d):
        if d < down_pieces:
            cols = slice(d * TILE, (d + 1) * TILE)
            product = dot(tall(act[:, :, cols]), tall(g2a[...]), 0, 0)
        elif d < early_pieces:
            cols = slice((d - down_pieces) * TILE, (d - down_pieces + 1) * TILE)
            product = dot(tall(ua[:, :, :, cols]), tall(gp[...]), 0, 0)
        elif d == early_pieces:
            product = dot(tall(cc[...]), tall(g1a[...]), 0, 0)
        else:
            right = tall(qkv[:, d - early_pieces - 1])
            for j in range(per_piece):
                cols = slice(j * TILE, (j + 1) * TILE)
                product = dot(tall(xa[:, :, :, cols]), right, 0, 0).astype(LOW)
                for h in range(per_piece):
                    gb[d * per_piece + j, :, :, h * head_cols : (h + 1) * head_cols] = product[
                        h * UNIT : (h + 1) * UNIT
                    ].reshape(2, UNIT // 2, head_cols)
            return
        product = product.astype(LOW)
        for u in range(per_piece):
            gb[d * per_piece + u] = product[u * UNIT : (u + 1) * UNIT].reshape(2, UNIT // 2, width)

    def unit_stores(i, src):
        def make(n, src, dst):
            return pltpu.make_async_copy(src, dst, grad_sem.at[i, n])

        if i < down_pieces * per_piece:
            return [make(0, src, gdown_ref.at[i])]
        i_up = i - down_pieces * per_piece
        if i_up < up_pieces * per_piece:
            return [make(0, src, gup_ref.at[i_up])]
        i_out = i - early_pieces * per_piece
        if i_out < per_piece:
            return [make(0, src, gout_ref.at[i_out])]
        i_qkv = i_out - per_piece
        kind, j = i_qkv // per_piece, i_qkv % per_piece
        return [
            make(h, src.at[:, :, pl.ds(h * head_cols, head_cols)], gqkv_ref.at[kind, j * per_piece + h])
            for h in range(per_piece)
        ]

    unit_pairs = pieces * per_piece // 2

    def pair_stores(k):
        return unit_stores(2 * k, rx.at[k % RING]) + unit_stores(2 * k + 1, rb.at[k % RING])

    ticks = iter(range(-1, unit_pairs + STAGE_AT[-1] + STORE_TICKS + 1))

    def tick():
        now = next(ticks, None)
        if now is None:
            return False
        if 0 <= now - STAGE_AT[-1] - STORE_TICKS < unit_pairs:
            reducer.drain(now - STAGE_AT[-1] - STORE_TICKS)
            for cp in pair_stores(now - STAGE_AT[-1] - STORE_TICKS):
                cp.wait()
        k = now + 1
        if k < unit_pairs:
            if 2 * k % per_piece == 0:
                piece(2 * k // per_piece)
            reducer.start(k)
        for stage, at in zip(reducer.stages, STAGE_AT):
            if 0 <= now - at < unit_pairs:
                stage(reducer, now - at)
        if 0 <= now - STAGE_AT[-1] < unit_pairs:
            for cp in pair_stores(now - STAGE_AT[-1]):
                cp.start()
        return True

    def step(s, carry, p):
        gathered(p, s)
        computes[p](s)
        send_sums(p, s)
        pass_sums(p, s)
        if p > 0:

            @pl.when(s == 0)
            def _():
                finishes[p - 1](batches - 1)

        @pl.when(s > 0)
        def _():
            finishes[p](s - 1)

        @pl.when(s < batches - 1)
        def _():
            forward_block(p, s + 1)

        @pl.when(s == batches - 1)
        def _():
            forward_block(p + 1, 0)

        return carry

    forward_block(0, 0)
    for cp in loads:
        cp.wait()
    load_wq.wait()
    load_wo.wait()
    lax.fori_loop(0, batches, functools.partial(step, p=0), 0)
    load_wu.wait()
    load_wd.wait()
    load_cot.wait()
    lax.fori_loop(0, batches, functools.partial(step, p=1), 0)

    hops = iter(range(VECTOR_HOPS + 1))

    def vector_hop():
        hop = next(hops, None)
        if hop is None:
            return False
        if hop == 0:
            held[0] = vg[...]
        else:
            vectors.end(hop - 1)
        if hop < VECTOR_HOPS:
            vectors.begin(hop)
        return True

    actions = {
        "gather": gathered,
        "compute": lambda p, s: computes[p](s),
        "send": send_sums,
        "pass": pass_sums,
        "finish": lambda p, s: finishes[p](s),
        "forward": forward_block,
    }
    last = PHASES * batches - 1
    vectors_wait = {("compute", last), ("finish", last - 1)}
    for action in SCHEDULE:
        if action == TICK:
            if summed:
                if not vectors_wait:
                    vector_hop()
                tick()
        else:
            name, index = action
            actions[name](index // batches, index % batches)
            vectors_wait.discard(action)
    if summed:
        while tick():
            vector_hop()
        while vector_hop():
            pass
        vsum_ref[...] = held[VECTOR_HOPS - 1]
    else:
        stores = []
        for d in range(pieces):
            piece(d)
            for i in range(d * per_piece, (d + 1) * per_piece):
                stores += unit_stores(i, gb.at[i])
                for cp in unit_stores(i, gb.at[i]):
                    cp.start()
        vsum_ref[...] = vg[...]
        for cp in stores:
            cp.wait()
    for s in range(batches):
        store(batches + s, cot.at[s], gin_ref.at[s]).wait()

    def drain(i, carry):
        for p in range(PHASES):
            ag_y(p, i, t).wait_send()
            ag_c(p, i, t).wait_send()
            ag_f(p, i, t_y).wait_send()
        return carry

    lax.fori_loop(0, batches, drain, 0)


def run_layer(lengths, x, cot, wqkv, wout, wup, wdown, vectors, summed):
    batches, block, width = x.shape
    rows = 4 * block
    head_cols = wout.shape[0]
    heads = head_cols // HD
    hidden = wup.shape[1]
    half = UNIT // 2
    down, up, out = hidden // UNIT, width // UNIT, head_cols // UNIT
    units = down + up + out + 3 * out
    ring, short_ring = (RING, SHORT_RING) if summed else (1, 1)
    any_space = pl.BlockSpec(memory_space=pl.ANY)
    vmem = pl.BlockSpec(memory_space=pltpu.VMEM)
    dma = pltpu.SemaphoreType.DMA
    low = lambda *shape: pltpu.VMEM(shape, LOW)
    wide = lambda *shape: pltpu.VMEM(shape, F32)
    gathered = low(batches, 4, block, width)
    scratch = [
        gathered,
        low(3, width, head_cols),
        low(head_cols, width),
        low(width, hidden),
        low(hidden, width),
        low(batches, 3, rows, head_cols),
        low(batches, heads, rows, rows),
        low(batches, rows, head_cols),
        gathered,
        low(batches, rows, hidden),
        low(batches, rows, hidden),
        gathered,
        gathered,
        low(batches, 2, 2, block, width),
        low(batches, 2, block, width),
        low(batches, block, width),
        low(batches, block, width),
        wide(batches, block, width),
        wide(batches, block, 128),
        wide(batches, block, width),
        low(batches, block, width),
        low(units, 2, half, width),
        low(ring, 2, half, width),
        low(short_ring, half, width),
        low(short_ring, half, width),
        low(ring, 2, half, width),
        low(short_ring, half, width),
        low(short_ring, half, width),
        wide(VECTOR_HOPS, 8, width),
        wide(VECTOR_HOPS - 1, 8, width),
        wide(8, width),
        wide(8, width),
        dma((batches + 5,)),
        dma((2 * batches,)),
    ]
    scratch += [dma((PHASES, batches))] * 10 + [dma((HOPS, units // 2))] * 2 + [dma((VECTOR_HOPS,))] * 2
    scratch.append(dma((units, TILE // UNIT)))
    low_out = lambda *shape: jax.ShapeDtypeStruct(shape, LOW)
    return pl.pallas_call(
        functools.partial(layer_kernel, summed=summed),
        out_shape=(
            low_out(batches, block, width),
            low_out(batches, block, width),
            low_out(down, 2, half, width),
            low_out(up, 2, half, hidden),
            low_out(out, 2, half, width),
            low_out(3, width // UNIT, 2, half, head_cols),
            jax.ShapeDtypeStruct((8, width), F32),
        ),
        in_specs=[pl.BlockSpec(memory_space=pltpu.SMEM)] + [any_space] * 6 + [vmem] * 9,
        out_specs=(any_space,) * 6 + (vmem,),
        scratch_shapes=scratch,
        compiler_params=pltpu.CompilerParams(
            collective_id=0, has_side_effects=True, vmem_limit_bytes=63 << 20
        ),
        name="layer",
    )(lengths, x, cot, wqkv, wout, wup, wdown, *vectors)


def widen_kernel(
    down_ref, up_ref, out_ref, qkv_ref, sums_ref, rows_ref, gin_ref,
    down_wide, up_wide, out_wide, qkv_wide, *refs,
):
    vectors, (rows_copy, gin_copy, low, wide, low_qkv, wide_qkv, rows, load_sem, store_sem) = refs[:9], refs[9:]
    work = []

    def part(src, dst, held, made):
        n = len(work)
        get = pltpu.make_async_copy(src, held, load_sem.at[n])
        put = pltpu.make_async_copy(made, dst, store_sem.at[n])
        work.append((get, held, made, put))

    i = 0
    for src, dst in ((down_ref, down_wide), (up_ref, up_wide), (out_ref, out_wide)):
        for at in range(0, src.shape[0], TILE):
            part(src.at[pl.ds(at, TILE)], dst.at[pl.ds(at, TILE)], low.at[i], wide.at[i])
            i += 1
    for i in range(3):
        part(qkv_ref.at[i], qkv_wide.at[i], low_qkv.at[i], wide_qkv.at[i])
    for i, (src, dst) in enumerate(((rows_ref, rows_copy), (gin_ref, gin_copy))):
        block = rows.at[i]
        part(src, dst, block, block)
    for get, _, _, _ in work:
        get.start()
    head_cols = vectors[0].shape[0]
    vectors[0][...] = sums_ref[7, :head_cols]
    vectors[1][...] = sums_ref[7, head_cols : 2 * head_cols]
    for ref, row in zip(vectors[2:], (0, 1, 2, 6, 3, 4, 5)):
        ref[...] = sums_ref[row]
    for get, held, made, put in work:
        get.wait()
        if made is not held:
            made[...] = held[...].astype(F32)
        put.start()
    for _, _, _, put in work:
        put.wait()


def widen(down, up, out, qkv, sums, rows, gin):
    any_space = pl.BlockSpec(memory_space=pl.ANY)
    vmem = pl.BlockSpec(memory_space=pltpu.VMEM)
    dma = pltpu.SemaphoreType.DMA
    width = down.shape[1]
    pieces = (down.shape[0] + up.shape[0] + out.shape[0]) // TILE
    as_wide = lambda a: jax.ShapeDtypeStruct(a.shape, F32)
    vector = lambda n: jax.ShapeDtypeStruct((n,), F32)
    return pl.pallas_call(
        widen_kernel,
        out_shape=(
            *map(as_wide, (down, up, out, qkv)),
            *[vector(out.shape[0])] * 2,
            *[vector(width)] * 7,
            jax.ShapeDtypeStruct(rows.shape, rows.dtype),
            jax.ShapeDtypeStruct(gin.shape, gin.dtype),
        ),
        in_specs=[any_space] * 4 + [vmem] + [any_space] * 2,
        out_specs=(any_space,) * 4 + (vmem,) * 9 + (any_space,) * 2,
        scratch_shapes=[
            pltpu.VMEM((pieces, TILE, width), LOW),
            pltpu.VMEM((pieces, TILE, width), F32),
            pltpu.VMEM(qkv.shape, LOW),
            pltpu.VMEM(qkv.shape, F32),
            pltpu.VMEM((2, *rows.shape), LOW),
            dma((pieces + 5,)),
            dma((pieces + 5,)),
        ],
        compiler_params=pltpu.CompilerParams(vmem_limit_bytes=62 << 20),
        name="widen",
    )(down, up, out, qkv, sums, rows, gin)


def per_device(
    inputs,
    lengths,
    cotangent,
    w_qkv,
    b_query,
    b_value,
    w_out,
    b_out,
    ln1_gain,
    ln1_bias,
    w_up,
    b_up,
    w_down,
    b_down,
    ln2_gain,
    ln2_bias,
):
    width = inputs.shape[3]
    head_cols = w_out.shape[0]
    hidden = w_up.shape[1]
    summed = lax.axis_size("dp") == 8
    output, grad_inputs, grad_down, grad_up, grad_out, grad_qkv, sums = run_layer(
        lengths,
        inputs[0],
        cotangent[0],
        jnp.transpose(w_qkv, (1, 0, 2)),
        w_out,
        w_up,
        w_down,
        (b_out, ln1_gain, ln1_bias, b_down, ln2_gain, ln2_bias, b_up, b_query, b_value),
        summed,
    )
    if not summed:
        grad_down, grad_up, grad_out, grad_qkv, sums = lax.psum(
            (grad_down, grad_up, grad_out, grad_qkv, sums), "dp"
        )
        sums = jnp.concatenate([lax.psum(sums[:6], "tensor"), sums[6:]])
    grad_down, grad_up, grad_out, grad_qkv, *rest = widen(
        grad_down.reshape(hidden, width),
        grad_up.reshape(width, hidden),
        grad_out.reshape(head_cols, width),
        grad_qkv.reshape(3, width, head_cols),
        sums,
        output,
        grad_inputs,
    )
    gquery, gvalue, gbout, ggain1, gbias1, gbup, gbdown, ggain2, gbias2, output, grad_inputs = rest
    return (
        output[None],
        grad_inputs[None],
        jnp.transpose(grad_qkv, (1, 0, 2)),
        gquery,
        gvalue,
        grad_out,
        gbout,
        ggain1,
        gbias1,
        grad_up,
        gbup,
        grad_down,
        gbdown,
        ggain2,
        gbias2,
    )


def solution(mesh):
    return jax.shard_map(
        per_device,
        mesh=mesh,
        in_specs=(
            P("dp", None, "tensor", None),
            P("dp", None),
            P("dp", None, "tensor", None),
            P(None, None, "tensor"),
            P("tensor"),
            P("tensor"),
            P("tensor", None),
            P(),
            P(),
            P(),
            P(None, "tensor"),
            P("tensor"),
            P("tensor", None),
            P(),
            P(),
            P(),
        ),
        out_specs=(
            P("dp", None, "tensor", None),
            P("dp", None, "tensor", None),
            P(None, None, "tensor"),
            P("tensor"),
            P("tensor"),
            P("tensor", None),
            P(),
            P(),
            P(),
            P(None, "tensor"),
            P("tensor"),
            P("tensor", None),
            P(),
            P(),
            P(),
        ),
        check_vma=False,
    )
```

```python
import functools

import jax
import jax.numpy as jnp
from jax import lax
from jax.experimental import pallas as pl
from jax.experimental.pallas import tpu as pltpu
from jax.sharding import PartitionSpec as P

HD = 64
EPSILON = 1e-05
F32 = jnp.float32
LOW = jnp.bfloat16
MESH = pl.DeviceIdType.MESH
TILE = 256
PHASES = 4
UNIT = 64


def dot(left, right, left_dim=1, right_dim=0):
    return lax.dot_general(
        left, right, (((left_dim,), (right_dim,)), ((), ())), preferred_element_type=F32
    )


def row_sum(values):
    return jnp.sum(values, axis=0, keepdims=True)


def row_mean(values):
    return jnp.mean(values, axis=-1, keepdims=True)


def gelu_parts(h):
    t = 1.0 / (1.0 + 0.23164188 * jnp.abs(h))
    density = jnp.exp(-0.5 * h * h)
    series = t * (
        0.127414796
        + t * (-0.142248368 + t * (0.7107068705 + t * (-0.7265760135 + t * 0.5307027145)))
    )
    tail = series * density
    return jnp.where(h < 0.0, tail, 1.0 - tail), density * 0.3989422804014327


HOPS = 11
RING = 16
SHORT_RING = 8
STAGE_AT = (0, 1, 2, 3, 4, 6)
STORE_TICKS = 3
TICK = ("tick", 0)
SCHEDULE = (
    ("finish", 5),
    ("gather", 6),
    ("compute", 6),
    ("forward", 7),
    ("send", 6),
    ("gather", 7),
    ("compute", 7),
    ("pass", 6),
    ("forward", 8),
    ("gather", 8),
    TICK,
    ("send", 7),
    ("pass", 7),
    TICK,
    ("finish", 6),
    TICK,
    ("compute", 8),
    *[TICK] * 2,
    ("finish", 7),
    ("send", 8),
    ("forward", 9),
    TICK,
    ("gather", 9),
    ("pass", 8),
    TICK,
    ("compute", 9),
    TICK,
    ("forward", 10),
    TICK,
    ("finish", 8),
    ("send", 9),
    TICK,
    ("gather", 10),
    ("pass", 9),
    TICK,
    ("compute", 10),
    ("send", 10),
    TICK,
    ("forward", 11),
    ("pass", 10),
    TICK,
    ("gather", 11),
    ("compute", 11),
    TICK,
    ("send", 11),
    TICK,
    ("pass", 11),
    *[TICK] * 4,
    ("finish", 9),
    ("finish", 10),
    *[TICK] * 2,
    ("finish", 11),
    TICK,
)


class Reducer:
    def __init__(self, gb, rx, rz, rm, rb, rn, rq, send_sems, recv_sems):
        dp = lax.axis_index("dp")
        self.x = lax.rem(dp, 2)
        self.z = lax.div(dp, 2)
        self.side = lax.rem(self.z, 2)
        self.m = lax.div(self.z, 2)
        self.inner = self.side != self.m
        self.outer = self.side == self.m
        self.to_x = {"dp": self.z * 2 + (1 - self.x)}
        self.to_pair = {"dp": (self.z + 1 - 2 * self.side) * 2 + self.x}
        self.to_mid = {"dp": (3 - self.z) * 2 + self.x}
        self.gb, self.rx, self.rz, self.rm, self.rb, self.rn, self.rq = gb, rx, rz, rm, rb, rn, rq
        self.send_sems, self.recv_sems = send_sems, recv_sems

    def greet(self, extra=()):
        barrier = pltpu.get_barrier_semaphore()

        def signal(device):
            pl.semaphore_signal(barrier, inc=1, device_id=device, device_id_type=MESH)

        for device in (self.to_x, self.to_pair) + tuple(extra):
            signal(device)

        @pl.when(self.inner)
        def _():
            signal(self.to_mid)
            pl.semaphore_wait(barrier, 3 + len(extra))

        @pl.when(self.outer)
        def _():
            pl.semaphore_wait(barrier, 2 + len(extra))

    def copy(self, hop, k, src, dst, device):
        return pltpu.make_async_remote_copy(
            src_ref=src,
            dst_ref=dst,
            send_sem=self.send_sems.at[hop, k],
            recv_sem=self.recv_sems.at[hop, k],
            device_id=device,
            device_id_type=MESH,
        )

    def ax(self, k):
        return self.copy(0, k, self.gb.at[2 * k, 1 - self.x], self.rx.at[k % RING, 1 - self.x], self.to_x)

    def az(self, k):
        return self.copy(1, k, self.gb.at[2 * k, self.x], self.rz.at[k % SHORT_RING], self.to_pair)

    def am(self, k):
        return self.copy(2, k, self.gb.at[2 * k, self.x], self.rm.at[k % SHORT_RING], self.to_mid)

    def ao(self, k):
        return self.copy(3, k, self.rx.at[k % RING, self.x], self.rx.at[k % RING, self.x], self.to_pair)

    def ag(self, k):
        return self.copy(4, k, self.rx.at[k % RING, self.x], self.rx.at[k % RING, self.x], self.to_x)

    def bi(self, k):
        return self.copy(5, k, self.gb.at[2 * k + 1], self.rb.at[k % RING], self.to_pair)

    def bm(self, k):
        return self.copy(6, k, self.gb.at[2 * k + 1, 1 - self.m], self.rn.at[k % SHORT_RING], self.to_mid)

    def bx(self, k):
        return self.copy(7, k, self.gb.at[2 * k + 1, self.m], self.rq.at[k % SHORT_RING], self.to_x)

    def bg(self, k):
        return self.copy(8, k, self.rb.at[k % RING, self.m], self.rb.at[k % RING, self.m], self.to_mid)

    def bo(self, k):
        return self.copy(9, k, self.rb.at[k % RING, self.m], self.rb.at[k % RING, self.m], self.to_pair)

    def bp(self, k):
        return self.copy(10, k, self.rb.at[k % RING, 1 - self.m], self.rb.at[k % RING, 1 - self.m], self.to_pair)

    def add(self, out, left, right):
        out[...] = (left[...].astype(F32) + right[...].astype(F32)).astype(LOW)

    def start(self, k):
        self.ax(k).start()

        @pl.when(self.outer)
        def _():
            self.bi(k).start()

    def stage1(self, k):
        self.ax(k).wait()
        own = self.gb.at[2 * k, self.x]
        self.add(own, own, self.rx.at[k % RING, self.x])

        @pl.when(self.outer)
        def _():
            self.az(k).start()

    def stage2(self, k):
        @pl.when(self.inner)
        def _():
            self.bi(k).wait_recv()
            away = self.gb.at[2 * k + 1, 1 - self.m]
            self.add(away, away, self.rb.at[k % RING, 1 - self.m])
            self.bm(k).start()
            own = self.gb.at[2 * k + 1, self.m]
            self.add(own, own, self.rb.at[k % RING, self.m])
            self.az(k).wait_recv()
            own = self.gb.at[2 * k, self.x]
            self.add(own, own, self.rz.at[k % SHORT_RING])
            self.am(k).start()

    def stage3(self, k):
        @pl.when(self.inner)
        def _():
            self.bm(k).wait()
            own = self.gb.at[2 * k + 1, self.m]
            self.add(own, own, self.rn.at[k % SHORT_RING])
            self.bx(k).start()
            self.am(k).wait()
            self.add(self.rx.at[k % RING, self.x], self.gb.at[2 * k, self.x], self.rm.at[k % SHORT_RING])
            self.ao(k).start()
            self.ag(k).start()

    def stage4(self, k):
        @pl.when(self.inner)
        def _():
            self.bx(k).wait()
            self.add(self.rb.at[k % RING, self.m], self.gb.at[2 * k + 1, self.m], self.rq.at[k % SHORT_RING])
            self.bg(k).start()
            self.bo(k).start()

        @pl.when(self.outer)
        def _():
            self.ao(k).wait_recv()
            self.ag(k).start()

    def stage5(self, k):
        @pl.when(self.inner)
        def _():
            self.bg(k).wait_recv()
            self.bp(k).start()

        self.ag(k).wait_recv()

    def stage6(self, k):
        @pl.when(self.outer)
        def _():
            self.bo(k).wait_recv()
            self.bp(k).wait_recv()

    def drain(self, k):
        self.ag(k).wait_send()

        @pl.when(self.inner)
        def _():
            self.ao(k).wait_send()
            self.bg(k).wait_send()
            self.bo(k).wait_send()
            self.bp(k).wait_send()

        @pl.when(self.outer)
        def _():
            self.az(k).wait_send()
            self.bi(k).wait_send()

    stages = (stage1, stage2, stage3, stage4, stage5, stage6)


VECTOR_HOPS = 6


class VectorReducer:
    def __init__(self, reducer, held, landed, send_sem, recv_sem, shared):
        t = lax.axis_index("tensor")
        c = lax.rem(t, 2)
        y = lax.div(t, 2)
        self.r = reducer
        self.held, self.landed, self.send_sem, self.recv_sem = held, landed, send_sem, recv_sem
        self.shared = shared
        self.devices = (
            {"tensor": y * 2 + (1 - c)},
            {"tensor": (1 - y) * 2 + c},
            reducer.to_x,
            reducer.to_pair,
            reducer.to_mid,
            reducer.to_pair,
        )

    def copy(self, hop):
        src = self.held.at[5 if hop == 5 else hop]
        dst = self.held.at[5] if hop == 5 else self.landed.at[hop]
        return pltpu.make_async_remote_copy(
            src_ref=src,
            dst_ref=dst,
            send_sem=self.send_sem.at[hop],
            recv_sem=self.recv_sem.at[hop],
            device_id=self.devices[hop],
            device_id_type=MESH,
        )

    def begin(self, hop):
        if hop < 3:
            self.copy(hop).start()
        else:

            @pl.when(self.r.outer if hop == 3 else self.r.inner)
            def _():
                self.copy(hop).start()

    def end(self, hop):
        if hop < 3:
            self.copy(hop).wait()
            got = self.landed[hop]
            if hop < 2:
                row = lax.broadcasted_iota(jnp.int32, got.shape, 0)
                got = jnp.where(row < self.shared, got, 0.0)
            self.held[hop + 1] = self.held[hop] + got
        elif hop == 3:

            @pl.when(self.r.outer)
            def _():
                self.copy(3).wait_send()

            @pl.when(self.r.inner)
            def _():
                self.copy(3).wait_recv()
                self.held[4] = self.held[3] + self.landed[3]

        elif hop == 4:

            @pl.when(self.r.inner)
            def _():
                self.copy(4).wait()
                self.held[5] = self.held[4] + self.landed[4]

        else:

            @pl.when(self.r.inner)
            def _():
                self.copy(5).wait_send()

            @pl.when(self.r.outer)
            def _():
                self.copy(5).wait_recv()


def layer_kernel(
    lengths_ref,
    x_ref,
    cot_ref,
    wqkv_ref,
    wout_ref,
    wup_ref,
    wdown_ref,
    bout_ref,
    gain1_ref,
    bias1_ref,
    bdown_ref,
    gain2_ref,
    bias2_ref,
    bup_ref,
    bquery_ref,
    bvalue_ref,
    out_ref,
    gin_ref,
    gdown_ref,
    gup_ref,
    gout_ref,
    gqkv_ref,
    vsum_ref,
    xa,
    wq,
    wo,
    wu,
    wd,
    qkv,
    pt,
    cc,
    ua,
    act,
    gp,
    g2a,
    g1a,
    part,
    rc,
    ys,
    ry,
    xh1,
    rstd1,
    resid,
    cot,
    gb,
    rx,
    rz,
    rm,
    rb,
    rn,
    rq,
    held,
    landed,
    vg,
    vec_ref,
    grads,
    load_sem,
    store_sem,
    agy_send,
    agy_recv,
    agc_send,
    agc_recv,
    agf_send,
    agf_recv,
    rsc_send,
    rsc_recv,
    rsy_send,
    rsy_recv,
    hop_send,
    hop_recv,
    vec_send,
    vec_recv,
    grad_sem,
    *,
    summed,
):
    batches = x_ref.shape[0]
    block = x_ref.shape[1]
    width = x_ref.shape[2]
    head_cols = wo.shape[0]
    hidden = wu.shape[1]
    rows = 4 * block
    pairs = head_cols // 128
    t = lax.axis_index("tensor")
    c = lax.rem(t, 2)
    y = lax.div(t, 2)
    t_core = y * 2 + (1 - c)
    t_y = (1 - y) * 2 + c
    t_far = (1 - y) * 2 + (1 - c)
    core = {"tensor": t_core}
    across = {"tensor": t_y}

    gathers = (xa, ua, g2a, g1a)

    def remote(src, dst, send, recv, device):
        return pltpu.make_async_remote_copy(
            src_ref=src, dst_ref=dst, send_sem=send, recv_sem=recv, device_id=device, device_id_type=MESH
        )

    def ag_y(p, s, at, src=None):
        buf = gathers[p]
        return remote(
            buf.at[s, at] if src is None else src, buf.at[s, at], agy_send.at[p, s], agy_recv.at[p, s], across
        )

    def ag_c(p, s, at, src=None):
        buf = gathers[p]
        return remote(
            buf.at[s, at] if src is None else src, buf.at[s, at], agc_send.at[p, s], agc_recv.at[p, s], core
        )

    def ag_f(p, s, at):
        buf = gathers[p]
        return remote(buf.at[s, at], buf.at[s, at], agf_send.at[p, s], agf_recv.at[p, s], core)

    def rs_c(p, s):
        return remote(part.at[s, 1 - c], rc.at[s], rsc_send.at[p, s], rsc_recv.at[p, s], core)

    def rs_y(p, s):
        return remote(ys.at[s], ry.at[s], rsy_send.at[p, s], rsy_recv.at[p, s], across)

    def load(index, src, dst):
        return pltpu.make_async_copy(src, dst, load_sem.at[index])

    def store(index, src, dst):
        return pltpu.make_async_copy(src, dst, store_sem.at[index])

    loads = [load(s, x_ref.at[s], xa.at[s, t]) for s in range(batches)]
    n = batches
    load_wq = load(n, wqkv_ref, wq)
    load_wo = load(n + 1, wout_ref, wo)
    load_wu = load(n + 2, wup_ref, wu)
    load_wd = load(n + 3, wdown_ref, wd)
    load_cot = load(n + 4, cot_ref, cot)

    for cp in loads:
        cp.start()
    if summed:
        reducer = Reducer(gb, rx, rz, rm, rb, rn, rq, hop_send, hop_recv)
        vectors = VectorReducer(reducer, held, landed, vec_send, vec_recv, 6)
        reducer.greet((core, across))
    else:
        barrier = pltpu.get_barrier_semaphore()
        for device in (core, across):
            pl.semaphore_signal(barrier, inc=1, device_id=device, device_id_type=MESH)
        pl.semaphore_wait(barrier, 2)
    for s in range(batches):
        ag_y(0, s, t, x_ref.at[s]).start()
        ag_c(0, s, t, x_ref.at[s]).start()
    load_wq.start()
    load_wo.start()
    load_wu.start()
    load_wd.start()
    load_cot.start()

    vg[...] = jnp.zeros_like(vg)
    long_refs = (bout_ref, gain1_ref, bias1_ref, bdown_ref, gain2_ref, bias2_ref, bup_ref)
    for i, ref in enumerate(long_refs):
        vec_ref[i : i + 1, :] = ref[...].astype(F32).reshape(1, -1)
    for i, ref in enumerate((bquery_ref, bvalue_ref)):
        vec_ref[7:8, i * head_cols : (i + 1) * head_cols] = ref[...].astype(F32).reshape(1, -1)
    lane = lax.broadcasted_iota(jnp.int32, (rows, 128), 1)
    low_half = lane < HD
    empty = jnp.zeros((rows, 128), LOW)

    def masked(values, h):
        return jnp.where(low_half, values, empty) if h == 0 else jnp.where(low_half, empty, values)

    def vec(i):
        return vec_ref[i : i + 1, :]

    def whole(ref, s):
        return ref[s].reshape(rows, width)

    def put_part(s, j, values):
        values = values.astype(LOW)
        cols = pl.ds(pl.multiple_of(j * TILE, TILE), TILE)
        for b in range(4):
            part[s, b % 2, b // 2, :, cols] = values[b * block : (b + 1) * block]

    def compute_a(s):
        tokens = whole(xa, s)
        q = dot(tokens, wq[0]) + vec_ref[7:8, :head_cols]
        qkv[s, 0] = q.astype(LOW) * LOW(HD ** (-0.5))
        qkv[s, 1] = dot(tokens, wq[1]).astype(LOW)
        v = dot(tokens, wq[2]) + vec_ref[7:8, head_cols : 2 * head_cols]
        qkv[s, 2] = v.astype(LOW)
        keys_valid = lax.broadcasted_iota(jnp.int32, (rows, rows), 0) < lengths_ref[0, s]
        for j in range(pairs):
            cols = slice(j * 128, (j + 1) * 128)
            q, k, v = qkv[s, 0, :, cols], qkv[s, 1, :, cols], qkv[s, 2, :, cols]
            context = jnp.zeros((128, rows), F32)
            for h in range(2):
                scores = dot(k, masked(q, h), 1, 1)
                scores = jnp.where(keys_valid, scores, -1e30)
                weights = jnp.exp(scores - jnp.max(scores, axis=0, keepdims=True))
                p = (weights * (1.0 / row_sum(weights))).astype(LOW)
                pt[s, 2 * j + h] = p
                context = context + dot(masked(v, h).T, p)
            cc[s, :, cols] = context.T.astype(LOW)
        context = cc[s]
        for j in range(width // TILE):
            put_part(s, j, dot(context, wo[:, j * TILE : (j + 1) * TILE]))

    def compute_c(s):
        normed = whole(ua, s)
        for j in range(hidden // TILE):
            cols = slice(j * TILE, (j + 1) * TILE)
            h = dot(normed, wu[:, cols]) + vec_ref[6:7, cols]
            phi, density = gelu_parts(h)
            act[s, :, cols] = (h * phi).astype(LOW)
            gp[s, :, cols] = (phi + h * density).astype(LOW)
        activated = act[s]
        for j in range(width // TILE):
            put_part(s, j, dot(activated, wd[:, j * TILE : (j + 1) * TILE]))

    def compute_e(s):
        def tile(j, carry):
            cols = pl.ds(pl.multiple_of(j * TILE, TILE), TILE)
            gh = gp[s, :, cols].astype(F32) * dot(whole(g2a, s), wd[cols, :], 1, 1)
            vg[6:7, cols] += row_sum(gh)
            gp[s, :, cols] = gh.astype(LOW)
            return carry

        lax.fori_loop(0, hidden // TILE, tile, 0)

        def back(j, carry):
            rows_at = pl.ds(pl.multiple_of(j * TILE, TILE), TILE)
            put_part(s, j, dot(gp[s], wu[rows_at, :], 1, 1))
            return carry

        lax.fori_loop(0, width // TILE, back, 0)

    def compute_g(s):
        grads[...] = dot(whole(g1a, s), wo[...], 1, 1).astype(LOW)

        def pair(j, carry):
            cols = pl.ds(pl.multiple_of(j * 128, 128), 128)
            q, k, v = qkv[s, 0, :, cols], qkv[s, 1, :, cols], qkv[s, 2, :, cols]
            gc = grads[:, cols]
            dq = jnp.zeros((128, rows), F32)
            dk = jnp.zeros((rows, 128), F32)
            dv = jnp.zeros((rows, 128), F32)
            for h in range(2):
                gc_h = masked(gc, h)
                p = pt[s, 2 * j + h]
                wide = p.astype(F32)
                product = wide * dot(v, gc_h, 1, 1)
                ds = (product - wide * row_sum(product)).astype(LOW)
                dv = dv + dot(p, gc_h)
                dk = dk + dot(ds, masked(q, h))
                dq = dq + dot(masked(k, h).T, ds)
            dq = dq.T * (HD ** (-0.5))
            vg[7:8, cols] += row_sum(dq)
            vg[7:8, pl.ds(pl.multiple_of(head_cols + j * 128, 128), 128)] += row_sum(dv)
            qkv[s, 0, :, cols] = dq.astype(LOW)
            qkv[s, 1, :, cols] = dk.astype(LOW)
            qkv[s, 2, :, cols] = dv.astype(LOW)
            return carry

        lax.fori_loop(0, pairs, pair, 0)

        def back(j, carry):
            at = pl.ds(pl.multiple_of(j * TILE, TILE), TILE)
            total = dot(qkv[s, 0], wq[0, at, :], 1, 1)
            total = total + dot(qkv[s, 1], wq[1, at, :], 1, 1)
            total = total + dot(qkv[s, 2], wq[2, at, :], 1, 1)
            put_part(s, j, total)
            return carry

        lax.fori_loop(0, width // TILE, back, 0)

    computes = (compute_a, compute_c, compute_e, compute_g)

    def reduced(p, s):
        rs_y(p, s).wait()
        rs_c(p, s).wait_send()
        return part[s, c, y].astype(F32) + rc[s, y].astype(F32) + ry[s].astype(F32)

    def send_on(p, s):
        ag_y(p, s, t).start()
        ag_c(p, s, t).start()

    def finish_a(s):
        z = xa[s, t].astype(F32) + (reduced(0, s) + vec(0))
        centred = z - row_mean(z)
        rstd = lax.rsqrt(row_mean(centred * centred) + EPSILON)
        hat = centred * rstd
        xh1[s] = hat
        rstd1[s] = jnp.broadcast_to(rstd, rstd1.shape[1:])
        ua[s, t] = (hat * vec(1) + vec(2)).astype(LOW)
        send_on(1, s)

    def finish_c(s):
        z = (xh1[s] * vec(1) + vec(2)) + (reduced(1, s) + vec(3))
        centred = z - row_mean(z)
        rstd = lax.rsqrt(row_mean(centred * centred) + EPSILON)
        hat = centred * rstd
        valid = t * block + lax.broadcasted_iota(jnp.int32, (block, width), 0) < lengths_ref[0, s]
        incoming = jnp.where(valid, cot[s].astype(F32), 0.0)
        scaled = incoming * vec(4)
        grad = rstd * (scaled - row_mean(scaled) - hat * row_mean(scaled * hat))
        resid[s] = grad
        g2a[s, t] = grad.astype(LOW)
        send_on(2, s)
        cot[s] = jnp.where(valid, hat * vec(4) + vec(5), 0.0).astype(LOW)
        store(s, cot.at[s], out_ref.at[s]).start()
        vg[3:4, :] += row_sum(grad)
        vg[4:5, :] += row_sum(incoming * hat)
        vg[5:6, :] += row_sum(incoming)

    def finish_e(s):
        gu = resid[s] + reduced(2, s)
        hat = xh1[s]
        scaled = gu * vec(1)
        grad = rstd1[s, :, :1] * (scaled - row_mean(scaled) - hat * row_mean(scaled * hat))
        resid[s] = grad
        g1a[s, t] = grad.astype(LOW)
        send_on(3, s)
        vg[0:1, :] += row_sum(grad)
        vg[1:2, :] += row_sum(gu * hat)
        vg[2:3, :] += row_sum(gu)

    def finish_g(s):
        store(s, cot.at[s], out_ref.at[s]).wait()
        cot[s] = (resid[s] + reduced(3, s)).astype(LOW)
        store(batches + s, cot.at[s], gin_ref.at[s]).start()

    finishes = (finish_a, finish_c, finish_e, finish_g)

    def forward_block(p, s):
        ag_y(p, s, t_y).wait_recv()
        ag_f(p, s, t_y).start()

    def gathered(p, s):
        ag_c(p, s, t_core).wait_recv()
        ag_f(p, s, t_far).wait_recv()

    def send_sums(p, s):
        rs_c(p, s).start()

    def pass_sums(p, s):
        rs_c(p, s).wait_recv()
        ys[s] = (part[s, c, 1 - y].astype(F32) + rc[s, 1 - y].astype(F32)).astype(LOW)
        rs_y(p, s).start()

    def tall(values):
        return values.reshape(batches * rows, -1)

    per_piece = TILE // UNIT
    down_pieces = hidden // TILE
    up_pieces = width // TILE
    early_pieces = down_pieces + up_pieces
    pieces = early_pieces + 1 + 3

    def piece(d):
        if d < down_pieces:
            cols = slice(d * TILE, (d + 1) * TILE)
            product = dot(tall(act[:, :, cols]), tall(g2a[...]), 0, 0)
        elif d < early_pieces:
            cols = slice((d - down_pieces) * TILE, (d - down_pieces + 1) * TILE)
            product = dot(tall(ua[:, :, :, cols]), tall(gp[...]), 0, 0)
        elif d == early_pieces:
            product = dot(tall(cc[...]), tall(g1a[...]), 0, 0)
        else:
            right = tall(qkv[:, d - early_pieces - 1])
            for j in range(per_piece):
                cols = slice(j * TILE, (j + 1) * TILE)
                product = dot(tall(xa[:, :, :, cols]), right, 0, 0).astype(LOW)
                for h in range(per_piece):
                    gb[d * per_piece + j, :, :, h * head_cols : (h + 1) * head_cols] = product[
                        h * UNIT : (h + 1) * UNIT
                    ].reshape(2, UNIT // 2, head_cols)
            return
        product = product.astype(LOW)
        for u in range(per_piece):
            gb[d * per_piece + u] = product[u * UNIT : (u + 1) * UNIT].reshape(2, UNIT // 2, width)

    def unit_stores(i, src):
        def make(n, src, dst):
            return pltpu.make_async_copy(src, dst, grad_sem.at[i, n])

        if i < down_pieces * per_piece:
            return [make(0, src, gdown_ref.at[i])]
        i_up = i - down_pieces * per_piece
        if i_up < up_pieces * per_piece:
            return [make(0, src, gup_ref.at[i_up])]
        i_out = i - early_pieces * per_piece
        if i_out < per_piece:
            return [make(0, src, gout_ref.at[i_out])]
        i_qkv = i_out - per_piece
        kind, j = i_qkv // per_piece, i_qkv % per_piece
        return [
            make(h, src.at[:, :, pl.ds(h * head_cols, head_cols)], gqkv_ref.at[kind, j * per_piece + h])
            for h in range(per_piece)
        ]

    unit_pairs = pieces * per_piece // 2

    def pair_stores(k):
        return unit_stores(2 * k, rx.at[k % RING]) + unit_stores(2 * k + 1, rb.at[k % RING])

    ticks = iter(range(-1, unit_pairs + STAGE_AT[-1] + STORE_TICKS + 1))

    def tick():
        now = next(ticks, None)
        if now is None:
            return False
        if 0 <= now - STAGE_AT[-1] - STORE_TICKS < unit_pairs:
            reducer.drain(now - STAGE_AT[-1] - STORE_TICKS)
            for cp in pair_stores(now - STAGE_AT[-1] - STORE_TICKS):
                cp.wait()
        k = now + 1
        if k < unit_pairs:
            if 2 * k % per_piece == 0:
                piece(2 * k // per_piece)
            reducer.start(k)
        for stage, at in zip(reducer.stages, STAGE_AT):
            if 0 <= now - at < unit_pairs:
                stage(reducer, now - at)
        if 0 <= now - STAGE_AT[-1] < unit_pairs:
            for cp in pair_stores(now - STAGE_AT[-1]):
                cp.start()
        return True

    def step(s, carry, p):
        gathered(p, s)
        computes[p](s)
        send_sums(p, s)
        pass_sums(p, s)
        if p > 0:

            @pl.when(s == 0)
            def _():
                finishes[p - 1](batches - 1)

        @pl.when(s > 0)
        def _():
            finishes[p](s - 1)

        @pl.when(s < batches - 1)
        def _():
            forward_block(p, s + 1)

        @pl.when(s == batches - 1)
        def _():
            forward_block(p + 1, 0)

        return carry

    forward_block(0, 0)
    for cp in loads:
        cp.wait()
    load_wq.wait()
    load_wo.wait()
    lax.fori_loop(0, batches, functools.partial(step, p=0), 0)
    load_wu.wait()
    load_wd.wait()
    load_cot.wait()
    lax.fori_loop(0, batches, functools.partial(step, p=1), 0)

    hops = iter(range(VECTOR_HOPS + 1))

    def vector_hop():
        hop = next(hops, None)
        if hop is None:
            return False
        if hop == 0:
            held[0] = vg[...]
        else:
            vectors.end(hop - 1)
        if hop < VECTOR_HOPS:
            vectors.begin(hop)
        return True

    actions = {
        "gather": gathered,
        "compute": lambda p, s: computes[p](s),
        "send": send_sums,
        "pass": pass_sums,
        "finish": lambda p, s: finishes[p](s),
        "forward": forward_block,
    }
    last = PHASES * batches - 1
    vectors_wait = {("compute", last), ("finish", last - 1)}
    for action in SCHEDULE:
        if action == TICK:
            if summed:
                if not vectors_wait:
                    vector_hop()
                tick()
        else:
            name, index = action
            actions[name](index // batches, index % batches)
            vectors_wait.discard(action)
    if summed:
        while tick():
            vector_hop()
        while vector_hop():
            pass
        vsum_ref[...] = held[VECTOR_HOPS - 1]
    else:
        stores = []
        for d in range(pieces):
            piece(d)
            for i in range(d * per_piece, (d + 1) * per_piece):
                stores += unit_stores(i, gb.at[i])
                for cp in unit_stores(i, gb.at[i]):
                    cp.start()
        vsum_ref[...] = vg[...]
        for cp in stores:
            cp.wait()
    for s in range(batches):
        store(batches + s, cot.at[s], gin_ref.at[s]).wait()

    def drain(i, carry):
        for p in range(PHASES):
            ag_y(p, i, t).wait_send()
            ag_c(p, i, t).wait_send()
            ag_f(p, i, t_y).wait_send()
        return carry

    lax.fori_loop(0, batches, drain, 0)


def run_layer(lengths, x, cot, wqkv, wout, wup, wdown, vectors, summed):
    batches, block, width = x.shape
    rows = 4 * block
    head_cols = wout.shape[0]
    heads = head_cols // HD
    hidden = wup.shape[1]
    half = UNIT // 2
    down, up, out = hidden // UNIT, width // UNIT, head_cols // UNIT
    units = down + up + out + 3 * out
    ring, short_ring = (RING, SHORT_RING) if summed else (1, 1)
    any_space = pl.BlockSpec(memory_space=pl.ANY)
    vmem = pl.BlockSpec(memory_space=pltpu.VMEM)
    dma = pltpu.SemaphoreType.DMA
    low = lambda *shape: pltpu.VMEM(shape, LOW)
    wide = lambda *shape: pltpu.VMEM(shape, F32)
    gathered = low(batches, 4, block, width)
    scratch = [
        gathered,
        low(3, width, head_cols),
        low(head_cols, width),
        low(width, hidden),
        low(hidden, width),
        low(batches, 3, rows, head_cols),
        low(batches, heads, rows, rows),
        low(batches, rows, head_cols),
        gathered,
        low(batches, rows, hidden),
        low(batches, rows, hidden),
        gathered,
        gathered,
        low(batches, 2, 2, block, width),
        low(batches, 2, block, width),
        low(batches, block, width),
        low(batches, block, width),
        wide(batches, block, width),
        wide(batches, block, 128),
        wide(batches, block, width),
        low(batches, block, width),
        low(units, 2, half, width),
        low(ring, 2, half, width),
        low(short_ring, half, width),
        low(short_ring, half, width),
        low(ring, 2, half, width),
        low(short_ring, half, width),
        low(short_ring, half, width),
        wide(VECTOR_HOPS, 8, width),
        wide(VECTOR_HOPS - 1, 8, width),
        wide(8, width),
        wide(8, width),
        low(rows, head_cols),
        dma((batches + 5,)),
        dma((2 * batches,)),
    ]
    scratch += [dma((PHASES, batches))] * 10 + [dma((HOPS, units // 2))] * 2 + [dma((VECTOR_HOPS,))] * 2
    scratch.append(dma((units, TILE // UNIT)))
    low_out = lambda *shape: jax.ShapeDtypeStruct(shape, LOW)
    return pl.pallas_call(
        functools.partial(layer_kernel, summed=summed),
        out_shape=(
            low_out(batches, block, width),
            low_out(batches, block, width),
            low_out(down, 2, half, width),
            low_out(up, 2, half, hidden),
            low_out(out, 2, half, width),
            low_out(3, width // UNIT, 2, half, head_cols),
            jax.ShapeDtypeStruct((8, width), F32),
        ),
        in_specs=[pl.BlockSpec(memory_space=pltpu.SMEM)] + [any_space] * 6 + [vmem] * 9,
        out_specs=(any_space,) * 6 + (vmem,),
        scratch_shapes=scratch,
        compiler_params=pltpu.CompilerParams(
            collective_id=0, has_side_effects=True, vmem_limit_bytes=63 << 20
        ),
        name="layer",
    )(lengths, x, cot, wqkv, wout, wup, wdown, *vectors)


def widen_kernel(
    down_ref, up_ref, out_ref, qkv_ref, sums_ref, rows_ref, gin_ref,
    down_wide, up_wide, out_wide, qkv_wide, *refs,
):
    vectors, (rows_copy, gin_copy, low, wide, low_qkv, wide_qkv, rows, load_sem, store_sem) = refs[:9], refs[9:]
    work = []

    def part(src, dst, held, made):
        n = len(work)
        get = pltpu.make_async_copy(src, held, load_sem.at[n])
        put = pltpu.make_async_copy(made, dst, store_sem.at[n])
        work.append((get, held, made, put))

    i = 0
    for src, dst in ((down_ref, down_wide), (up_ref, up_wide), (out_ref, out_wide)):
        for at in range(0, src.shape[0], TILE):
            part(src.at[pl.ds(at, TILE)], dst.at[pl.ds(at, TILE)], low.at[i], wide.at[i])
            i += 1
    for i in range(3):
        part(qkv_ref.at[i], qkv_wide.at[i], low_qkv.at[i], wide_qkv.at[i])
    for i, (src, dst) in enumerate(((rows_ref, rows_copy), (gin_ref, gin_copy))):
        block = rows.at[i]
        part(src, dst, block, block)
    for get, _, _, _ in work:
        get.start()
    head_cols = vectors[0].shape[0]
    vectors[0][...] = sums_ref[7, :head_cols]
    vectors[1][...] = sums_ref[7, head_cols : 2 * head_cols]
    for ref, row in zip(vectors[2:], (0, 1, 2, 6, 3, 4, 5)):
        ref[...] = sums_ref[row]
    for get, held, made, put in work:
        get.wait()
        if made is not held:
            made[...] = held[...].astype(F32)
        put.start()
    for _, _, _, put in work:
        put.wait()


def widen(down, up, out, qkv, sums, rows, gin):
    any_space = pl.BlockSpec(memory_space=pl.ANY)
    vmem = pl.BlockSpec(memory_space=pltpu.VMEM)
    dma = pltpu.SemaphoreType.DMA
    width = down.shape[1]
    pieces = (down.shape[0] + up.shape[0] + out.shape[0]) // TILE
    as_wide = lambda a: jax.ShapeDtypeStruct(a.shape, F32)
    vector = lambda n: jax.ShapeDtypeStruct((n,), F32)
    return pl.pallas_call(
        widen_kernel,
        out_shape=(
            *map(as_wide, (down, up, out, qkv)),
            *[vector(out.shape[0])] * 2,
            *[vector(width)] * 7,
            jax.ShapeDtypeStruct(rows.shape, rows.dtype),
            jax.ShapeDtypeStruct(gin.shape, gin.dtype),
        ),
        in_specs=[any_space] * 4 + [vmem] + [any_space] * 2,
        out_specs=(any_space,) * 4 + (vmem,) * 9 + (any_space,) * 2,
        scratch_shapes=[
            pltpu.VMEM((pieces, TILE, width), LOW),
            pltpu.VMEM((pieces, TILE, width), F32),
            pltpu.VMEM(qkv.shape, LOW),
            pltpu.VMEM(qkv.shape, F32),
            pltpu.VMEM((2, *rows.shape), LOW),
            dma((pieces + 5,)),
            dma((pieces + 5,)),
        ],
        compiler_params=pltpu.CompilerParams(vmem_limit_bytes=62 << 20),
        name="widen",
    )(down, up, out, qkv, sums, rows, gin)


def per_device(
    inputs,
    lengths,
    cotangent,
    w_qkv,
    b_query,
    b_value,
    w_out,
    b_out,
    ln1_gain,
    ln1_bias,
    w_up,
    b_up,
    w_down,
    b_down,
    ln2_gain,
    ln2_bias,
):
    width = inputs.shape[3]
    head_cols = w_out.shape[0]
    hidden = w_up.shape[1]
    summed = lax.axis_size("dp") == 8
    output, grad_inputs, grad_down, grad_up, grad_out, grad_qkv, sums = run_layer(
        lengths,
        inputs[0],
        cotangent[0],
        jnp.transpose(w_qkv, (1, 0, 2)),
        w_out,
        w_up,
        w_down,
        (b_out, ln1_gain, ln1_bias, b_down, ln2_gain, ln2_bias, b_up, b_query, b_value),
        summed,
    )
    if not summed:
        grad_down, grad_up, grad_out, grad_qkv, sums = lax.psum(
            (grad_down, grad_up, grad_out, grad_qkv, sums), "dp"
        )
        sums = jnp.concatenate([lax.psum(sums[:6], "tensor"), sums[6:]])
    grad_down, grad_up, grad_out, grad_qkv, *rest = widen(
        grad_down.reshape(hidden, width),
        grad_up.reshape(width, hidden),
        grad_out.reshape(head_cols, width),
        grad_qkv.reshape(3, width, head_cols),
        sums,
        output,
        grad_inputs,
    )
    gquery, gvalue, gbout, ggain1, gbias1, gbup, gbdown, ggain2, gbias2, output, grad_inputs = rest
    return (
        output[None],
        grad_inputs[None],
        jnp.transpose(grad_qkv, (1, 0, 2)),
        gquery,
        gvalue,
        grad_out,
        gbout,
        ggain1,
        gbias1,
        grad_up,
        gbup,
        grad_down,
        gbdown,
        ggain2,
        gbias2,
    )


def solution(mesh):
    return jax.shard_map(
        per_device,
        mesh=mesh,
        in_specs=(
            P("dp", None, "tensor", None),
            P("dp", None),
            P("dp", None, "tensor", None),
            P(None, None, "tensor"),
            P("tensor"),
            P("tensor"),
            P("tensor", None),
            P(),
            P(),
            P(),
            P(None, "tensor"),
            P("tensor"),
            P("tensor", None),
            P(),
            P(),
            P(),
        ),
        out_specs=(
            P("dp", None, "tensor", None),
            P("dp", None, "tensor", None),
            P(None, None, "tensor"),
            P("tensor"),
            P("tensor"),
            P("tensor", None),
            P(),
            P(),
            P(),
            P(None, "tensor"),
            P("tensor"),
            P("tensor", None),
            P(),
            P(),
            P(),
        ),
        check_vma=False,
    )
```

```python
import functools

import jax
import jax.numpy as jnp
from jax import lax
from jax.experimental import pallas as pl
from jax.experimental.pallas import tpu as pltpu
from jax.sharding import PartitionSpec as P

HD = 64
EPSILON = 1e-05
F32 = jnp.float32
LOW = jnp.bfloat16
MESH = pl.DeviceIdType.MESH
TILE = 256
PHASES = 4
UNIT = 64


def dot(left, right, left_dim=1, right_dim=0):
    return lax.dot_general(
        left, right, (((left_dim,), (right_dim,)), ((), ())), preferred_element_type=F32
    )


def row_sum(values):
    return jnp.sum(values, axis=0, keepdims=True)


def row_mean(values):
    return jnp.mean(values, axis=-1, keepdims=True)


def gelu_parts(h):
    t = 1.0 / (1.0 + 0.23164188 * jnp.abs(h))
    density = jnp.exp(-0.5 * h * h)
    series = t * (
        0.127414796
        + t * (-0.142248368 + t * (0.7107068705 + t * (-0.7265760135 + t * 0.5307027145)))
    )
    tail = series * density
    return jnp.where(h < 0.0, tail, 1.0 - tail), density * 0.3989422804014327


HOPS = 11
RING = 16
SHORT_RING = 8
STAGE_AT = (0, 1, 2, 3, 4, 6)
STORE_TICKS = 3
TICK = ("tick", 0)
SCHEDULE = (
    ("gather", 6),
    ("finish", 5),
    ("forward", 7),
    ("compute", 6, 0),
    ("compute", 6, 1),
    ("send", 6),
    ("forward", 8),
    ("gather", 7),
    ("gather", 8),
    TICK,
    ("compute", 7, 0),
    ("pass", 6),
    TICK,
    ("compute", 8, 0),
    TICK,
    ("compute", 8, 1),
    ("compute", 7, 1),
    TICK,
    ("send", 7),
    TICK,
    ("send", 8),
    ("finish", 6),
    TICK,
    ("pass", 8),
    *[TICK] * 2,
    ("pass", 7),
    TICK,
    ("forward", 9),
    ("finish", 8),
    TICK,
    ("gather", 9),
    TICK,
    ("finish", 7),
    TICK,
    ("forward", 11),
    TICK,
    ("compute", 9, 0),
    TICK,
    ("forward", 10),
    ("compute", 9, 1),
    TICK,
    ("gather", 11),
    ("gather", 10),
    ("compute", 10, 0),
    TICK,
    ("compute", 10, 1),
    TICK,
    ("compute", 11, 0),
    TICK,
    ("compute", 11, 1),
    TICK,
    ("compute", 10, 2),
    ("send", 10),
    TICK,
    ("pass", 10),
    TICK,
    ("compute", 9, 2),
    ("send", 9),
    *[TICK] * 2,
    ("compute", 11, 2),
    TICK,
    ("pass", 9),
    TICK,
    ("send", 11),
    TICK,
    ("pass", 11),
    ("finish", 10),
    ("finish", 9),
    *[TICK] * 2,
    ("finish", 11),
)


class Reducer:
    def __init__(self, gb, rx, rz, rm, rb, rn, rq, send_sems, recv_sems):
        dp = lax.axis_index("dp")
        self.x = lax.rem(dp, 2)
        self.z = lax.div(dp, 2)
        self.side = lax.rem(self.z, 2)
        self.m = lax.div(self.z, 2)
        self.inner = self.side != self.m
        self.outer = self.side == self.m
        self.to_x = {"dp": self.z * 2 + (1 - self.x)}
        self.to_pair = {"dp": (self.z + 1 - 2 * self.side) * 2 + self.x}
        self.to_mid = {"dp": (3 - self.z) * 2 + self.x}
        self.gb, self.rx, self.rz, self.rm, self.rb, self.rn, self.rq = gb, rx, rz, rm, rb, rn, rq
        self.send_sems, self.recv_sems = send_sems, recv_sems

    def greet(self, extra=()):
        barrier = pltpu.get_barrier_semaphore()

        def signal(device):
            pl.semaphore_signal(barrier, inc=1, device_id=device, device_id_type=MESH)

        for device in (self.to_x, self.to_pair) + tuple(extra):
            signal(device)

        @pl.when(self.inner)
        def _():
            signal(self.to_mid)
            pl.semaphore_wait(barrier, 3 + len(extra))

        @pl.when(self.outer)
        def _():
            pl.semaphore_wait(barrier, 2 + len(extra))

    def copy(self, hop, k, src, dst, device):
        return pltpu.make_async_remote_copy(
            src_ref=src,
            dst_ref=dst,
            send_sem=self.send_sems.at[hop, k],
            recv_sem=self.recv_sems.at[hop, k],
            device_id=device,
            device_id_type=MESH,
        )

    def ax(self, k):
        return self.copy(0, k, self.gb.at[2 * k, 1 - self.x], self.rx.at[k % RING, 1 - self.x], self.to_x)

    def az(self, k):
        return self.copy(1, k, self.gb.at[2 * k, self.x], self.rz.at[k % SHORT_RING], self.to_pair)

    def am(self, k):
        return self.copy(2, k, self.gb.at[2 * k, self.x], self.rm.at[k % SHORT_RING], self.to_mid)

    def ao(self, k):
        return self.copy(3, k, self.rx.at[k % RING, self.x], self.rx.at[k % RING, self.x], self.to_pair)

    def ag(self, k):
        return self.copy(4, k, self.rx.at[k % RING, self.x], self.rx.at[k % RING, self.x], self.to_x)

    def bi(self, k):
        return self.copy(5, k, self.gb.at[2 * k + 1], self.rb.at[k % RING], self.to_pair)

    def bm(self, k):
        return self.copy(6, k, self.gb.at[2 * k + 1, 1 - self.m], self.rn.at[k % SHORT_RING], self.to_mid)

    def bx(self, k):
        return self.copy(7, k, self.gb.at[2 * k + 1, self.m], self.rq.at[k % SHORT_RING], self.to_x)

    def bg(self, k):
        return self.copy(8, k, self.rb.at[k % RING, self.m], self.rb.at[k % RING, self.m], self.to_mid)

    def bo(self, k):
        return self.copy(9, k, self.rb.at[k % RING, self.m], self.rb.at[k % RING, self.m], self.to_pair)

    def bp(self, k):
        return self.copy(10, k, self.rb.at[k % RING, 1 - self.m], self.rb.at[k % RING, 1 - self.m], self.to_pair)

    def add(self, out, left, right):
        out[...] = (left[...].astype(F32) + right[...].astype(F32)).astype(LOW)

    def start(self, k):
        self.ax(k).start()

        @pl.when(self.outer)
        def _():
            self.bi(k).start()

    def stage1(self, k):
        self.ax(k).wait()
        own = self.gb.at[2 * k, self.x]
        self.add(own, own, self.rx.at[k % RING, self.x])

        @pl.when(self.outer)
        def _():
            self.az(k).start()

    def stage2(self, k):
        @pl.when(self.inner)
        def _():
            self.bi(k).wait_recv()
            away = self.gb.at[2 * k + 1, 1 - self.m]
            self.add(away, away, self.rb.at[k % RING, 1 - self.m])
            self.bm(k).start()
            own = self.gb.at[2 * k + 1, self.m]
            self.add(own, own, self.rb.at[k % RING, self.m])
            self.az(k).wait_recv()
            own = self.gb.at[2 * k, self.x]
            self.add(own, own, self.rz.at[k % SHORT_RING])
            self.am(k).start()

    def stage3(self, k):
        @pl.when(self.inner)
        def _():
            self.bm(k).wait()
            own = self.gb.at[2 * k + 1, self.m]
            self.add(own, own, self.rn.at[k % SHORT_RING])
            self.bx(k).start()
            self.am(k).wait()
            self.add(self.rx.at[k % RING, self.x], self.gb.at[2 * k, self.x], self.rm.at[k % SHORT_RING])
            self.ao(k).start()
            self.ag(k).start()

    def stage4(self, k):
        @pl.when(self.inner)
        def _():
            self.bx(k).wait()
            self.add(self.rb.at[k % RING, self.m], self.gb.at[2 * k + 1, self.m], self.rq.at[k % SHORT_RING])
            self.bg(k).start()
            self.bo(k).start()

        @pl.when(self.outer)
        def _():
            self.ao(k).wait_recv()
            self.ag(k).start()

    def stage5(self, k):
        @pl.when(self.inner)
        def _():
            self.bg(k).wait_recv()
            self.bp(k).start()

        self.ag(k).wait_recv()

    def stage6(self, k):
        @pl.when(self.outer)
        def _():
            self.bo(k).wait_recv()
            self.bp(k).wait_recv()

    def drain(self, k):
        self.ag(k).wait_send()

        @pl.when(self.inner)
        def _():
            self.ao(k).wait_send()
            self.bg(k).wait_send()
            self.bo(k).wait_send()
            self.bp(k).wait_send()

        @pl.when(self.outer)
        def _():
            self.az(k).wait_send()
            self.bi(k).wait_send()

    stages = (stage1, stage2, stage3, stage4, stage5, stage6)


VECTOR_HOPS = 6


class VectorReducer:
    def __init__(self, reducer, held, landed, send_sem, recv_sem, shared):
        t = lax.axis_index("tensor")
        c = lax.rem(t, 2)
        y = lax.div(t, 2)
        self.r = reducer
        self.held, self.landed, self.send_sem, self.recv_sem = held, landed, send_sem, recv_sem
        self.shared = shared
        self.devices = (
            {"tensor": y * 2 + (1 - c)},
            {"tensor": (1 - y) * 2 + c},
            reducer.to_x,
            reducer.to_pair,
            reducer.to_mid,
            reducer.to_pair,
        )

    def copy(self, hop):
        src = self.held.at[5 if hop == 5 else hop]
        dst = self.held.at[5] if hop == 5 else self.landed.at[hop]
        return pltpu.make_async_remote_copy(
            src_ref=src,
            dst_ref=dst,
            send_sem=self.send_sem.at[hop],
            recv_sem=self.recv_sem.at[hop],
            device_id=self.devices[hop],
            device_id_type=MESH,
        )

    def begin(self, hop):
        if hop < 3:
            self.copy(hop).start()
        else:

            @pl.when(self.r.outer if hop == 3 else self.r.inner)
            def _():
                self.copy(hop).start()

    def end(self, hop):
        if hop < 3:
            self.copy(hop).wait()
            got = self.landed[hop]
            if hop < 2:
                row = lax.broadcasted_iota(jnp.int32, got.shape, 0)
                got = jnp.where(row < self.shared, got, 0.0)
            self.held[hop + 1] = self.held[hop] + got
        elif hop == 3:

            @pl.when(self.r.outer)
            def _():
                self.copy(3).wait_send()

            @pl.when(self.r.inner)
            def _():
                self.copy(3).wait_recv()
                self.held[4] = self.held[3] + self.landed[3]

        elif hop == 4:

            @pl.when(self.r.inner)
            def _():
                self.copy(4).wait()
                self.held[5] = self.held[4] + self.landed[4]

        else:

            @pl.when(self.r.inner)
            def _():
                self.copy(5).wait_send()

            @pl.when(self.r.outer)
            def _():
                self.copy(5).wait_recv()


def layer_kernel(
    lengths_ref,
    x_ref,
    cot_ref,
    wqkv_ref,
    wout_ref,
    wup_ref,
    wdown_ref,
    bout_ref,
    gain1_ref,
    bias1_ref,
    bdown_ref,
    gain2_ref,
    bias2_ref,
    bup_ref,
    bquery_ref,
    bvalue_ref,
    out_ref,
    gin_ref,
    gdown_ref,
    gup_ref,
    gout_ref,
    gqkv_ref,
    vsum_ref,
    xa,
    wq,
    wo,
    wu,
    wd,
    qkv,
    pt,
    cc,
    ua,
    act,
    gp,
    g2a,
    g1a,
    part,
    rc,
    ys,
    ry,
    xh1,
    rstd1,
    resid,
    cot,
    gb,
    rx,
    rz,
    rm,
    rb,
    rn,
    rq,
    held,
    landed,
    vg,
    vec_ref,
    grads,
    load_sem,
    store_sem,
    agy_send,
    agy_recv,
    agc_send,
    agc_recv,
    agf_send,
    agf_recv,
    rsc_send,
    rsc_recv,
    rsy_send,
    rsy_recv,
    hop_send,
    hop_recv,
    vec_send,
    vec_recv,
    grad_sem,
    *,
    summed,
):
    batches = x_ref.shape[0]
    block = x_ref.shape[1]
    width = x_ref.shape[2]
    head_cols = wo.shape[0]
    hidden = wu.shape[1]
    rows = 4 * block
    pairs = head_cols // 128
    t = lax.axis_index("tensor")
    c = lax.rem(t, 2)
    y = lax.div(t, 2)
    t_core = y * 2 + (1 - c)
    t_y = (1 - y) * 2 + c
    t_far = (1 - y) * 2 + (1 - c)
    core = {"tensor": t_core}
    across = {"tensor": t_y}

    gathers = (xa, ua, g2a, g1a)

    def remote(src, dst, send, recv, device):
        return pltpu.make_async_remote_copy(
            src_ref=src, dst_ref=dst, send_sem=send, recv_sem=recv, device_id=device, device_id_type=MESH
        )

    def ag_y(p, s, at, src=None):
        buf = gathers[p]
        return remote(
            buf.at[s, at] if src is None else src, buf.at[s, at], agy_send.at[p, s], agy_recv.at[p, s], across
        )

    def ag_c(p, s, at, src=None):
        buf = gathers[p]
        return remote(
            buf.at[s, at] if src is None else src, buf.at[s, at], agc_send.at[p, s], agc_recv.at[p, s], core
        )

    def ag_f(p, s, at):
        buf = gathers[p]
        return remote(buf.at[s, at], buf.at[s, at], agf_send.at[p, s], agf_recv.at[p, s], core)

    def rs_c(p, s):
        return remote(part.at[s, 1 - c], rc.at[s], rsc_send.at[p, s], rsc_recv.at[p, s], core)

    def rs_y(p, s):
        return remote(ys.at[s], ry.at[s], rsy_send.at[p, s], rsy_recv.at[p, s], across)

    def load(index, src, dst):
        return pltpu.make_async_copy(src, dst, load_sem.at[index])

    def store(index, src, dst):
        return pltpu.make_async_copy(src, dst, store_sem.at[index])

    loads = [load(s, x_ref.at[s], xa.at[s, t]) for s in range(batches)]
    n = batches
    load_wq = load(n, wqkv_ref, wq)
    load_wo = load(n + 1, wout_ref, wo)
    load_wu = load(n + 2, wup_ref, wu)
    load_wd = load(n + 3, wdown_ref, wd)
    load_cot = load(n + 4, cot_ref, cot)

    for cp in loads:
        cp.start()
    if summed:
        reducer = Reducer(gb, rx, rz, rm, rb, rn, rq, hop_send, hop_recv)
        vectors = VectorReducer(reducer, held, landed, vec_send, vec_recv, 6)
        reducer.greet((core, across))
    else:
        barrier = pltpu.get_barrier_semaphore()
        for device in (core, across):
            pl.semaphore_signal(barrier, inc=1, device_id=device, device_id_type=MESH)
        pl.semaphore_wait(barrier, 2)
    for s in range(batches):
        ag_y(0, s, t, x_ref.at[s]).start()
        ag_c(0, s, t, x_ref.at[s]).start()
    load_wq.start()
    load_wo.start()
    load_wu.start()
    load_wd.start()
    load_cot.start()

    vg[...] = jnp.zeros_like(vg)
    long_refs = (bout_ref, gain1_ref, bias1_ref, bdown_ref, gain2_ref, bias2_ref, bup_ref)
    for i, ref in enumerate(long_refs):
        vec_ref[i : i + 1, :] = ref[...].astype(F32).reshape(1, -1)
    for i, ref in enumerate((bquery_ref, bvalue_ref)):
        vec_ref[7:8, i * head_cols : (i + 1) * head_cols] = ref[...].astype(F32).reshape(1, -1)
    lane = lax.broadcasted_iota(jnp.int32, (rows, 128), 1)
    low_half = lane < HD
    empty = jnp.zeros((rows, 128), LOW)

    def masked(values, h):
        return jnp.where(low_half, values, empty) if h == 0 else jnp.where(low_half, empty, values)

    def vec(i):
        return vec_ref[i : i + 1, :]

    def whole(ref, s):
        return ref[s].reshape(rows, width)

    def put_part(s, j, values):
        values = values.astype(LOW)
        cols = pl.ds(pl.multiple_of(j * TILE, TILE), TILE)
        for b in range(4):
            part[s, b % 2, b // 2, :, cols] = values[b * block : (b + 1) * block]

    def compute_a(s):
        tokens = whole(xa, s)
        q = dot(tokens, wq[0]) + vec_ref[7:8, :head_cols]
        qkv[s, 0] = q.astype(LOW) * LOW(HD ** (-0.5))
        qkv[s, 1] = dot(tokens, wq[1]).astype(LOW)
        v = dot(tokens, wq[2]) + vec_ref[7:8, head_cols : 2 * head_cols]
        qkv[s, 2] = v.astype(LOW)
        keys_valid = lax.broadcasted_iota(jnp.int32, (rows, rows), 0) < lengths_ref[0, s]

        def pair(j, carry):
            cols = pl.ds(pl.multiple_of(j * 128, 128), 128)
            q, k, v = qkv[s, 0, :, cols], qkv[s, 1, :, cols], qkv[s, 2, :, cols]
            context = jnp.zeros((128, rows), F32)
            for h in range(2):
                scores = dot(k, masked(q, h), 1, 1)
                scores = jnp.where(keys_valid, scores, -1e30)
                weights = jnp.exp(scores - jnp.max(scores, axis=0, keepdims=True))
                p = (weights * (1.0 / row_sum(weights))).astype(LOW)
                pt[s, 2 * j + h] = p
                context = context + dot(masked(v, h).T, p)
            cc[s, :, cols] = context.T.astype(LOW)
            return carry

        lax.fori_loop(0, pairs, pair, 0)

        def out(j, carry):
            cols = pl.ds(pl.multiple_of(j * TILE, TILE), TILE)
            put_part(s, j, dot(cc[s], wo[:, cols]))
            return carry

        lax.fori_loop(0, width // TILE, out, 0)

    def compute_c(s):
        def tile(j, carry):
            cols = pl.ds(pl.multiple_of(j * TILE, TILE), TILE)
            h = dot(whole(ua, s), wu[:, cols]) + vec_ref[6:7, cols]
            phi, density = gelu_parts(h)
            act[s, :, cols] = (h * phi).astype(LOW)
            gp[s, :, cols] = (phi + h * density).astype(LOW)
            return carry

        lax.fori_loop(0, hidden // TILE, tile, 0)

        def down(j, carry):
            cols = pl.ds(pl.multiple_of(j * TILE, TILE), TILE)
            put_part(s, j, dot(act[s], wd[:, cols]))
            return carry

        lax.fori_loop(0, width // TILE, down, 0)

    def compute_e_hidden(s):
        def tile(j, carry):
            cols = pl.ds(pl.multiple_of(j * TILE, TILE), TILE)
            gh = gp[s, :, cols].astype(F32) * dot(whole(g2a, s), wd[cols, :], 1, 1)
            vg[6:7, cols] += row_sum(gh)
            gp[s, :, cols] = gh.astype(LOW)
            return carry

        lax.fori_loop(0, hidden // TILE, tile, 0)

    def compute_e_back(s):
        def back(j, carry):
            rows_at = pl.ds(pl.multiple_of(j * TILE, TILE), TILE)
            put_part(s, j, dot(gp[s], wu[rows_at, :], 1, 1))
            return carry

        lax.fori_loop(0, width // TILE, back, 0)

    def head_pair_back(s, j):
        cols = slice(j * 128, (j + 1) * 128)
        q, k, v = qkv[s, 0, :, cols], qkv[s, 1, :, cols], qkv[s, 2, :, cols]
        gc = grads[:, cols]
        dq = jnp.zeros((128, rows), F32)
        dk = jnp.zeros((rows, 128), F32)
        dv = jnp.zeros((rows, 128), F32)
        for h in range(2):
            gc_h = masked(gc, h)
            p = pt[s, 2 * j + h]
            wide = p.astype(F32)
            product = wide * dot(v, gc_h, 1, 1)
            ds = (product - wide * row_sum(product)).astype(LOW)
            dv = dv + dot(p, gc_h)
            dk = dk + dot(ds, masked(q, h))
            dq = dq + dot(masked(k, h).T, ds)
        dq = dq.T * (HD ** (-0.5))
        vg[7:8, cols] += row_sum(dq)
        vg[7:8, head_cols + j * 128 : head_cols + (j + 1) * 128] += row_sum(dv)
        qkv[s, 0, :, cols] = dq.astype(LOW)
        qkv[s, 1, :, cols] = dk.astype(LOW)
        qkv[s, 2, :, cols] = dv.astype(LOW)

    def compute_g_first(s):
        grads[...] = dot(whole(g1a, s), wo[...], 1, 1).astype(LOW)
        for j in range(pairs // 2):
            head_pair_back(s, j)

    def compute_g_second(s):
        for j in range(pairs // 2, pairs):
            head_pair_back(s, j)

    def compute_g_back(s):
        def back(j, carry):
            at = pl.ds(pl.multiple_of(j * TILE, TILE), TILE)
            total = dot(qkv[s, 0], wq[0, at, :], 1, 1)
            total = total + dot(qkv[s, 1], wq[1, at, :], 1, 1)
            total = total + dot(qkv[s, 2], wq[2, at, :], 1, 1)
            put_part(s, j, total)
            return carry

        lax.fori_loop(0, width // TILE, back, 0)

    computes = (
        (compute_a,),
        (compute_c,),
        (compute_e_hidden, compute_e_back),
        (compute_g_first, compute_g_second, compute_g_back),
    )

    def reduced(p, s):
        rs_y(p, s).wait()
        rs_c(p, s).wait_send()
        return part[s, c, y].astype(F32) + rc[s, y].astype(F32) + ry[s].astype(F32)

    def send_on(p, s):
        ag_y(p, s, t).start()
        ag_c(p, s, t).start()

    def finish_a(s):
        z = xa[s, t].astype(F32) + (reduced(0, s) + vec(0))
        centred = z - row_mean(z)
        rstd = lax.rsqrt(row_mean(centred * centred) + EPSILON)
        hat = centred * rstd
        xh1[s] = hat
        rstd1[s] = jnp.broadcast_to(rstd, rstd1.shape[1:])
        ua[s, t] = (hat * vec(1) + vec(2)).astype(LOW)
        send_on(1, s)

    def finish_c(s):
        z = (xh1[s] * vec(1) + vec(2)) + (reduced(1, s) + vec(3))
        centred = z - row_mean(z)
        rstd = lax.rsqrt(row_mean(centred * centred) + EPSILON)
        hat = centred * rstd
        valid = t * block + lax.broadcasted_iota(jnp.int32, (block, width), 0) < lengths_ref[0, s]
        incoming = jnp.where(valid, cot[s].astype(F32), 0.0)
        scaled = incoming * vec(4)
        grad = rstd * (scaled - row_mean(scaled) - hat * row_mean(scaled * hat))
        resid[s] = grad
        g2a[s, t] = grad.astype(LOW)
        send_on(2, s)
        cot[s] = jnp.where(valid, hat * vec(4) + vec(5), 0.0).astype(LOW)
        store(s, cot.at[s], out_ref.at[s]).start()
        vg[3:4, :] += row_sum(grad)
        vg[4:5, :] += row_sum(incoming * hat)
        vg[5:6, :] += row_sum(incoming)

    def finish_e(s):
        gu = resid[s] + reduced(2, s)
        hat = xh1[s]
        scaled = gu * vec(1)
        grad = rstd1[s, :, :1] * (scaled - row_mean(scaled) - hat * row_mean(scaled * hat))
        resid[s] = grad
        g1a[s, t] = grad.astype(LOW)
        send_on(3, s)
        vg[0:1, :] += row_sum(grad)
        vg[1:2, :] += row_sum(gu * hat)
        vg[2:3, :] += row_sum(gu)

    def finish_g(s):
        store(s, cot.at[s], out_ref.at[s]).wait()
        cot[s] = (resid[s] + reduced(3, s)).astype(LOW)
        store(batches + s, cot.at[s], gin_ref.at[s]).start()

    finishes = (finish_a, finish_c, finish_e, finish_g)

    def forward_block(p, s):
        ag_y(p, s, t_y).wait_recv()
        ag_f(p, s, t_y).start()

    def gathered(p, s):
        ag_c(p, s, t_core).wait_recv()
        ag_f(p, s, t_far).wait_recv()

    def send_sums(p, s):
        rs_c(p, s).start()

    def pass_sums(p, s):
        rs_c(p, s).wait_recv()
        ys[s] = (part[s, c, 1 - y].astype(F32) + rc[s, 1 - y].astype(F32)).astype(LOW)
        rs_y(p, s).start()

    def tall(values):
        return values.reshape(batches * rows, -1)

    per_piece = TILE // UNIT
    down_pieces = hidden // TILE
    up_pieces = width // TILE
    early_pieces = down_pieces + up_pieces
    pieces = early_pieces + 1 + 3

    def piece(d):
        if d < early_pieces:
            if d < down_pieces:
                cols = slice(d * TILE, (d + 1) * TILE)
                left, right = tall(act[:, :, cols]), g2a
            else:
                cols = slice((d - down_pieces) * TILE, (d - down_pieces + 1) * TILE)
                left, right = tall(ua[:, :, :, cols]), gp
        elif d == early_pieces:
            left, right = tall(cc[...]), g1a
        else:
            right = tall(qkv[:, d - early_pieces - 1])
            for j in range(per_piece):
                cols = slice(j * TILE, (j + 1) * TILE)
                product = dot(tall(xa[:, :, :, cols]), right, 0, 0).astype(LOW)
                for h in range(per_piece):
                    gb[d * per_piece + j, :, :, h * head_cols : (h + 1) * head_cols] = product[
                        h * UNIT : (h + 1) * UNIT
                    ].reshape(2, UNIT // 2, head_cols)
            return

        def half(j, carry):
            cols = pl.ds(pl.multiple_of(j * (width // 2), width // 2), width // 2)
            columns = right[:, :, cols] if len(right.shape) == 3 else right[:, :, :, cols]
            product = dot(left, tall(columns), 0, 0).astype(LOW)
            for u in range(per_piece):
                gb[d * per_piece + u, :, :, cols] = product[u * UNIT : (u + 1) * UNIT].reshape(
                    2, UNIT // 2, width // 2
                )
            return carry

        lax.fori_loop(0, 2, half, 0)

    def unit_stores(i, src):
        def make(n, src, dst):
            return pltpu.make_async_copy(src, dst, grad_sem.at[i, n])

        if i < down_pieces * per_piece:
            return [make(0, src, gdown_ref.at[i])]
        i_up = i - down_pieces * per_piece
        if i_up < up_pieces * per_piece:
            return [make(0, src, gup_ref.at[i_up])]
        i_out = i - early_pieces * per_piece
        if i_out < per_piece:
            return [make(0, src, gout_ref.at[i_out])]
        i_qkv = i_out - per_piece
        kind, j = i_qkv // per_piece, i_qkv % per_piece
        return [
            make(h, src.at[:, :, pl.ds(h * head_cols, head_cols)], gqkv_ref.at[kind, j * per_piece + h])
            for h in range(per_piece)
        ]

    unit_pairs = pieces * per_piece // 2

    def pair_stores(k):
        return unit_stores(2 * k, rx.at[k % RING]) + unit_stores(2 * k + 1, rb.at[k % RING])

    ticks = iter(range(-1, unit_pairs + STAGE_AT[-1] + STORE_TICKS + 1))

    def tick():
        now = next(ticks, None)
        if now is None:
            return False
        if 0 <= now - STAGE_AT[-1] - STORE_TICKS < unit_pairs:
            reducer.drain(now - STAGE_AT[-1] - STORE_TICKS)
            for cp in pair_stores(now - STAGE_AT[-1] - STORE_TICKS):
                cp.wait()
        k = now + 1
        if k < unit_pairs:
            if 2 * k % per_piece == 0:
                piece(2 * k // per_piece)
            reducer.start(k)
        for stage, at in zip(reducer.stages, STAGE_AT):
            if 0 <= now - at < unit_pairs:
                stage(reducer, now - at)
        if 0 <= now - STAGE_AT[-1] < unit_pairs:
            for cp in pair_stores(now - STAGE_AT[-1]):
                cp.start()
        return True

    def step(s, carry, p):
        gathered(p, s)
        for compute in computes[p]:
            compute(s)
        send_sums(p, s)
        pass_sums(p, s)
        if p > 0:

            @pl.when(s == 0)
            def _():
                finishes[p - 1](batches - 1)

        @pl.when(s > 0)
        def _():
            finishes[p](s - 1)

        @pl.when(s < batches - 1)
        def _():
            forward_block(p, s + 1)

        @pl.when(s == batches - 1)
        def _():
            forward_block(p + 1, 0)

        return carry

    forward_block(0, 0)
    for cp in loads:
        cp.wait()
    load_wq.wait()
    load_wo.wait()
    lax.fori_loop(0, batches, functools.partial(step, p=0), 0)
    load_wu.wait()
    load_wd.wait()
    load_cot.wait()
    lax.fori_loop(0, batches, functools.partial(step, p=1), 0)

    hops = iter(range(VECTOR_HOPS + 1))

    def vector_hop():
        hop = next(hops, None)
        if hop is None:
            return False
        if hop == 0:
            held[0] = vg[...]
        else:
            vectors.end(hop - 1)
        if hop < VECTOR_HOPS:
            vectors.begin(hop)
        return True

    actions = {
        "gather": gathered,
        "compute": lambda p, s, part: computes[p][part](s),
        "send": send_sums,
        "pass": pass_sums,
        "finish": lambda p, s: finishes[p](s),
        "forward": forward_block,
    }
    last = PHASES * batches - 1
    vectors_wait = {("compute", last, 1), ("finish", last - batches)}
    for action in SCHEDULE:
        if action == TICK:
            if summed:
                if not vectors_wait:
                    vector_hop()
                tick()
        else:
            name, index, *which = action
            actions[name](index // batches, index % batches, *which)
            vectors_wait.discard(action)
    if summed:
        while tick():
            vector_hop()
        while vector_hop():
            pass
        vsum_ref[...] = held[VECTOR_HOPS - 1]
    else:
        stores = []
        for d in range(pieces):
            piece(d)
            for i in range(d * per_piece, (d + 1) * per_piece):
                stores += unit_stores(i, gb.at[i])
                for cp in unit_stores(i, gb.at[i]):
                    cp.start()
        vsum_ref[...] = vg[...]
        for cp in stores:
            cp.wait()
    for s in range(batches):
        store(batches + s, cot.at[s], gin_ref.at[s]).wait()

    def drain(i, carry):
        for p in range(PHASES):
            ag_y(p, i, t).wait_send()
            ag_c(p, i, t).wait_send()
            ag_f(p, i, t_y).wait_send()
        return carry

    lax.fori_loop(0, batches, drain, 0)


def run_layer(lengths, x, cot, wqkv, wout, wup, wdown, vectors, summed):
    batches, block, width = x.shape
    rows = 4 * block
    head_cols = wout.shape[0]
    heads = head_cols // HD
    hidden = wup.shape[1]
    half = UNIT // 2
    down, up, out = hidden // UNIT, width // UNIT, head_cols // UNIT
    units = down + up + out + 3 * out
    ring, short_ring = (RING, SHORT_RING) if summed else (1, 1)
    any_space = pl.BlockSpec(memory_space=pl.ANY)
    vmem = pl.BlockSpec(memory_space=pltpu.VMEM)
    dma = pltpu.SemaphoreType.DMA
    low = lambda *shape: pltpu.VMEM(shape, LOW)
    wide = lambda *shape: pltpu.VMEM(shape, F32)
    gathered = low(batches, 4, block, width)
    scratch = [
        gathered,
        low(3, width, head_cols),
        low(head_cols, width),
        low(width, hidden),
        low(hidden, width),
        low(batches, 3, rows, head_cols),
        low(batches, heads, rows, rows),
        low(batches, rows, head_cols),
        gathered,
        low(batches, rows, hidden),
        low(batches, rows, hidden),
        gathered,
        gathered,
        low(batches, 2, 2, block, width),
        low(batches, 2, block, width),
        low(batches, block, width),
        low(batches, block, width),
        wide(batches, block, width),
        wide(batches, block, 128),
        wide(batches, block, width),
        low(batches, block, width),
        low(units, 2, half, width),
        low(ring, 2, half, width),
        low(short_ring, half, width),
        low(short_ring, half, width),
        low(ring, 2, half, width),
        low(short_ring, half, width),
        low(short_ring, half, width),
        wide(VECTOR_HOPS, 8, width),
        wide(VECTOR_HOPS - 1, 8, width),
        wide(8, width),
        wide(8, width),
        low(rows, head_cols),
        dma((batches + 5,)),
        dma((2 * batches,)),
    ]
    scratch += [dma((PHASES, batches))] * 10 + [dma((HOPS, units // 2))] * 2 + [dma((VECTOR_HOPS,))] * 2
    scratch.append(dma((units, TILE // UNIT)))
    low_out = lambda *shape: jax.ShapeDtypeStruct(shape, LOW)
    return pl.pallas_call(
        functools.partial(layer_kernel, summed=summed),
        out_shape=(
            low_out(batches, block, width),
            low_out(batches, block, width),
            low_out(down, 2, half, width),
            low_out(up, 2, half, hidden),
            low_out(out, 2, half, width),
            low_out(3, width // UNIT, 2, half, head_cols),
            jax.ShapeDtypeStruct((8, width), F32),
        ),
        in_specs=[pl.BlockSpec(memory_space=pltpu.SMEM)] + [any_space] * 6 + [vmem] * 9,
        out_specs=(any_space,) * 6 + (vmem,),
        scratch_shapes=scratch,
        compiler_params=pltpu.CompilerParams(
            collective_id=0, has_side_effects=True, vmem_limit_bytes=63 << 20
        ),
        name="layer",
    )(lengths, x, cot, wqkv, wout, wup, wdown, *vectors)


def widen_kernel(
    down_ref, up_ref, out_ref, qkv_ref, sums_ref, rows_ref, gin_ref,
    down_wide, up_wide, out_wide, qkv_wide, *refs,
):
    vectors, (rows_copy, gin_copy, low, wide, low_qkv, wide_qkv, rows, load_sem, store_sem) = refs[:9], refs[9:]
    work = []

    def part(src, dst, held, made):
        n = len(work)
        get = pltpu.make_async_copy(src, held, load_sem.at[n])
        put = pltpu.make_async_copy(made, dst, store_sem.at[n])
        work.append((get, held, made, put))

    i = 0
    for src, dst in ((down_ref, down_wide), (up_ref, up_wide), (out_ref, out_wide)):
        for at in range(0, src.shape[0], TILE):
            part(src.at[pl.ds(at, TILE)], dst.at[pl.ds(at, TILE)], low.at[i], wide.at[i])
            i += 1
    for i in range(3):
        part(qkv_ref.at[i], qkv_wide.at[i], low_qkv.at[i], wide_qkv.at[i])
    for i, (src, dst) in enumerate(((rows_ref, rows_copy), (gin_ref, gin_copy))):
        block = rows.at[i]
        part(src, dst, block, block)
    for get, _, _, _ in work:
        get.start()
    head_cols = vectors[0].shape[0]
    vectors[0][...] = sums_ref[7, :head_cols]
    vectors[1][...] = sums_ref[7, head_cols : 2 * head_cols]
    for ref, row in zip(vectors[2:], (0, 1, 2, 6, 3, 4, 5)):
        ref[...] = sums_ref[row]
    for get, held, made, put in work:
        get.wait()
        if made is not held:
            made[...] = held[...].astype(F32)
        put.start()
    for _, _, _, put in work:
        put.wait()


def widen(down, up, out, qkv, sums, rows, gin):
    any_space = pl.BlockSpec(memory_space=pl.ANY)
    vmem = pl.BlockSpec(memory_space=pltpu.VMEM)
    dma = pltpu.SemaphoreType.DMA
    width = down.shape[1]
    pieces = (down.shape[0] + up.shape[0] + out.shape[0]) // TILE
    as_wide = lambda a: jax.ShapeDtypeStruct(a.shape, F32)
    vector = lambda n: jax.ShapeDtypeStruct((n,), F32)
    return pl.pallas_call(
        widen_kernel,
        out_shape=(
            *map(as_wide, (down, up, out, qkv)),
            *[vector(out.shape[0])] * 2,
            *[vector(width)] * 7,
            jax.ShapeDtypeStruct(rows.shape, rows.dtype),
            jax.ShapeDtypeStruct(gin.shape, gin.dtype),
        ),
        in_specs=[any_space] * 4 + [vmem] + [any_space] * 2,
        out_specs=(any_space,) * 4 + (vmem,) * 9 + (any_space,) * 2,
        scratch_shapes=[
            pltpu.VMEM((pieces, TILE, width), LOW),
            pltpu.VMEM((pieces, TILE, width), F32),
            pltpu.VMEM(qkv.shape, LOW),
            pltpu.VMEM(qkv.shape, F32),
            pltpu.VMEM((2, *rows.shape), LOW),
            dma((pieces + 5,)),
            dma((pieces + 5,)),
        ],
        compiler_params=pltpu.CompilerParams(vmem_limit_bytes=62 << 20),
        name="widen",
    )(down, up, out, qkv, sums, rows, gin)


def per_device(
    inputs,
    lengths,
    cotangent,
    w_qkv,
    b_query,
    b_value,
    w_out,
    b_out,
    ln1_gain,
    ln1_bias,
    w_up,
    b_up,
    w_down,
    b_down,
    ln2_gain,
    ln2_bias,
):
    width = inputs.shape[3]
    head_cols = w_out.shape[0]
    hidden = w_up.shape[1]
    summed = lax.axis_size("dp") == 8
    output, grad_inputs, grad_down, grad_up, grad_out, grad_qkv, sums = run_layer(
        lengths,
        inputs[0],
        cotangent[0],
        jnp.transpose(w_qkv, (1, 0, 2)),
        w_out,
        w_up,
        w_down,
        (b_out, ln1_gain, ln1_bias, b_down, ln2_gain, ln2_bias, b_up, b_query, b_value),
        summed,
    )
    if not summed:
        grad_down, grad_up, grad_out, grad_qkv, sums = lax.psum(
            (grad_down, grad_up, grad_out, grad_qkv, sums), "dp"
        )
        sums = jnp.concatenate([lax.psum(sums[:6], "tensor"), sums[6:]])
    grad_down, grad_up, grad_out, grad_qkv, *rest = widen(
        grad_down.reshape(hidden, width),
        grad_up.reshape(width, hidden),
        grad_out.reshape(head_cols, width),
        grad_qkv.reshape(3, width, head_cols),
        sums,
        output,
        grad_inputs,
    )
    gquery, gvalue, gbout, ggain1, gbias1, gbup, gbdown, ggain2, gbias2, output, grad_inputs = rest
    return (
        output[None],
        grad_inputs[None],
        jnp.transpose(grad_qkv, (1, 0, 2)),
        gquery,
        gvalue,
        grad_out,
        gbout,
        ggain1,
        gbias1,
        grad_up,
        gbup,
        grad_down,
        gbdown,
        ggain2,
        gbias2,
    )


def solution(mesh):
    return jax.shard_map(
        per_device,
        mesh=mesh,
        in_specs=(
            P("dp", None, "tensor", None),
            P("dp", None),
            P("dp", None, "tensor", None),
            P(None, None, "tensor"),
            P("tensor"),
            P("tensor"),
            P("tensor", None),
            P(),
            P(),
            P(),
            P(None, "tensor"),
            P("tensor"),
            P("tensor", None),
            P(),
            P(),
            P(),
        ),
        out_specs=(
            P("dp", None, "tensor", None),
            P("dp", None, "tensor", None),
            P(None, None, "tensor"),
            P("tensor"),
            P("tensor"),
            P("tensor", None),
            P(),
            P(),
            P(),
            P(None, "tensor"),
            P("tensor"),
            P("tensor", None),
            P(),
            P(),
            P(),
        ),
        check_vma=False,
    )
```

```python
import functools

import jax
import jax.numpy as jnp
from jax import lax
from jax.experimental import pallas as pl
from jax.experimental.pallas import tpu as pltpu
from jax.sharding import PartitionSpec as P

HD = 64
EPSILON = 1e-05
F32 = jnp.float32
LOW = jnp.bfloat16
MESH = pl.DeviceIdType.MESH
TILE = 256
PHASES = 4
UNIT = 64


def dot(left, right, left_dim=1, right_dim=0):
    return lax.dot_general(
        left, right, (((left_dim,), (right_dim,)), ((), ())), preferred_element_type=F32
    )


def row_sum(values):
    return jnp.sum(values, axis=0, keepdims=True)


def row_mean(values):
    return jnp.mean(values, axis=-1, keepdims=True)


def gelu_parts(h):
    t = 1.0 / (1.0 + 0.23164188 * jnp.abs(h))
    density = jnp.exp(-0.5 * h * h)
    series = t * (
        0.127414796
        + t * (-0.142248368 + t * (0.7107068705 + t * (-0.7265760135 + t * 0.5307027145)))
    )
    tail = series * density
    return jnp.where(h < 0.0, tail, 1.0 - tail), density * 0.3989422804014327


HOPS = 11
RING = 16
SHORT_RING = 8
STAGE_AT = (0, 1, 2, 3, 4, 6)
STORE_TICKS = 3
LOADS_AHEAD = 16
TICK = ("tick", 0)
SCHEDULE = (
    ("gather", 6),
    ("finish", 5),
    ("forward", 7),
    ("compute", 6, 0),
    ("compute", 6, 1),
    ("send", 6),
    ("forward", 8),
    ("gather", 7),
    ("gather", 8),
    TICK,
    ("compute", 7, 0),
    ("pass", 6),
    TICK,
    ("compute", 8, 0),
    TICK,
    ("compute", 8, 1),
    ("compute", 7, 1),
    TICK,
    ("send", 7),
    TICK,
    ("send", 8),
    ("finish", 6),
    TICK,
    ("pass", 8),
    *[TICK] * 2,
    ("pass", 7),
    TICK,
    ("forward", 9),
    ("finish", 8),
    TICK,
    ("gather", 9),
    TICK,
    ("finish", 7),
    TICK,
    ("forward", 11),
    TICK,
    ("compute", 9, 0),
    TICK,
    ("forward", 10),
    ("compute", 9, 1),
    TICK,
    ("gather", 11),
    ("gather", 10),
    ("compute", 10, 0),
    TICK,
    ("compute", 10, 1),
    TICK,
    ("compute", 11, 0),
    TICK,
    ("compute", 11, 1),
    TICK,
    ("compute", 10, 2),
    ("send", 10),
    TICK,
    ("pass", 10),
    TICK,
    ("compute", 9, 2),
    ("send", 9),
    *[TICK] * 2,
    ("compute", 11, 2),
    TICK,
    ("pass", 9),
    TICK,
    ("send", 11),
    TICK,
    ("pass", 11),
    ("finish", 10),
    ("finish", 9),
    *[TICK] * 2,
    ("finish", 11),
)


class Reducer:
    def __init__(self, gb, rx, rz, rm, rb, rn, rq, send_sems, recv_sems):
        dp = lax.axis_index("dp")
        self.x = lax.rem(dp, 2)
        self.z = lax.div(dp, 2)
        self.side = lax.rem(self.z, 2)
        self.m = lax.div(self.z, 2)
        self.inner = self.side != self.m
        self.outer = self.side == self.m
        self.to_x = {"dp": self.z * 2 + (1 - self.x)}
        self.to_pair = {"dp": (self.z + 1 - 2 * self.side) * 2 + self.x}
        self.to_mid = {"dp": (3 - self.z) * 2 + self.x}
        self.gb, self.rx, self.rz, self.rm, self.rb, self.rn, self.rq = gb, rx, rz, rm, rb, rn, rq
        self.send_sems, self.recv_sems = send_sems, recv_sems

    def greet(self, extra=()):
        barrier = pltpu.get_barrier_semaphore()

        def signal(device):
            pl.semaphore_signal(barrier, inc=1, device_id=device, device_id_type=MESH)

        for device in (self.to_x, self.to_pair) + tuple(extra):
            signal(device)

        @pl.when(self.inner)
        def _():
            signal(self.to_mid)
            pl.semaphore_wait(barrier, 3 + len(extra))

        @pl.when(self.outer)
        def _():
            pl.semaphore_wait(barrier, 2 + len(extra))

    def copy(self, hop, k, src, dst, device):
        return pltpu.make_async_remote_copy(
            src_ref=src,
            dst_ref=dst,
            send_sem=self.send_sems.at[hop, k],
            recv_sem=self.recv_sems.at[hop, k],
            device_id=device,
            device_id_type=MESH,
        )

    def ax(self, k):
        return self.copy(0, k, self.gb.at[2 * k, 1 - self.x], self.rx.at[k % RING, 1 - self.x], self.to_x)

    def az(self, k):
        return self.copy(1, k, self.gb.at[2 * k, self.x], self.rz.at[k % SHORT_RING], self.to_pair)

    def am(self, k):
        return self.copy(2, k, self.gb.at[2 * k, self.x], self.rm.at[k % SHORT_RING], self.to_mid)

    def ao(self, k):
        return self.copy(3, k, self.rx.at[k % RING, self.x], self.rx.at[k % RING, self.x], self.to_pair)

    def ag(self, k):
        return self.copy(4, k, self.rx.at[k % RING, self.x], self.rx.at[k % RING, self.x], self.to_x)

    def bi(self, k):
        return self.copy(5, k, self.gb.at[2 * k + 1], self.rb.at[k % RING], self.to_pair)

    def bm(self, k):
        return self.copy(6, k, self.gb.at[2 * k + 1, 1 - self.m], self.rn.at[k % SHORT_RING], self.to_mid)

    def bx(self, k):
        return self.copy(7, k, self.gb.at[2 * k + 1, self.m], self.rq.at[k % SHORT_RING], self.to_x)

    def bg(self, k):
        return self.copy(8, k, self.rb.at[k % RING, self.m], self.rb.at[k % RING, self.m], self.to_mid)

    def bo(self, k):
        return self.copy(9, k, self.rb.at[k % RING, self.m], self.rb.at[k % RING, self.m], self.to_pair)

    def bp(self, k):
        return self.copy(10, k, self.rb.at[k % RING, 1 - self.m], self.rb.at[k % RING, 1 - self.m], self.to_pair)

    def add(self, out, left, right):
        out[...] = (left[...].astype(F32) + right[...].astype(F32)).astype(LOW)

    def start(self, k):
        self.ax(k).start()

        @pl.when(self.outer)
        def _():
            self.bi(k).start()

    def stage1(self, k):
        self.ax(k).wait()
        own = self.gb.at[2 * k, self.x]
        self.add(own, own, self.rx.at[k % RING, self.x])

        @pl.when(self.outer)
        def _():
            self.az(k).start()

    def stage2(self, k):
        @pl.when(self.inner)
        def _():
            self.bi(k).wait_recv()
            away = self.gb.at[2 * k + 1, 1 - self.m]
            self.add(away, away, self.rb.at[k % RING, 1 - self.m])
            self.bm(k).start()
            own = self.gb.at[2 * k + 1, self.m]
            self.add(own, own, self.rb.at[k % RING, self.m])
            self.az(k).wait_recv()
            own = self.gb.at[2 * k, self.x]
            self.add(own, own, self.rz.at[k % SHORT_RING])
            self.am(k).start()

    def stage3(self, k):
        @pl.when(self.inner)
        def _():
            self.bm(k).wait()
            own = self.gb.at[2 * k + 1, self.m]
            self.add(own, own, self.rn.at[k % SHORT_RING])
            self.bx(k).start()
            self.am(k).wait()
            self.add(self.rx.at[k % RING, self.x], self.gb.at[2 * k, self.x], self.rm.at[k % SHORT_RING])
            self.ao(k).start()
            self.ag(k).start()

    def stage4(self, k):
        @pl.when(self.inner)
        def _():
            self.bx(k).wait()
            self.add(self.rb.at[k % RING, self.m], self.gb.at[2 * k + 1, self.m], self.rq.at[k % SHORT_RING])
            self.bg(k).start()
            self.bo(k).start()

        @pl.when(self.outer)
        def _():
            self.ao(k).wait_recv()
            self.ag(k).start()

    def stage5(self, k):
        @pl.when(self.inner)
        def _():
            self.bg(k).wait_recv()
            self.bp(k).start()

        self.ag(k).wait_recv()

    def stage6(self, k):
        @pl.when(self.outer)
        def _():
            self.bo(k).wait_recv()
            self.bp(k).wait_recv()

    def drain(self, k):
        self.ag(k).wait_send()

        @pl.when(self.inner)
        def _():
            self.ao(k).wait_send()
            self.bg(k).wait_send()
            self.bo(k).wait_send()
            self.bp(k).wait_send()

        @pl.when(self.outer)
        def _():
            self.az(k).wait_send()
            self.bi(k).wait_send()

    stages = (stage1, stage2, stage3, stage4, stage5, stage6)


VECTOR_HOPS = 6


class VectorReducer:
    def __init__(self, reducer, held, landed, send_sem, recv_sem, shared):
        t = lax.axis_index("tensor")
        c = lax.rem(t, 2)
        y = lax.div(t, 2)
        self.r = reducer
        self.held, self.landed, self.send_sem, self.recv_sem = held, landed, send_sem, recv_sem
        self.shared = shared
        self.devices = (
            {"tensor": y * 2 + (1 - c)},
            {"tensor": (1 - y) * 2 + c},
            reducer.to_x,
            reducer.to_pair,
            reducer.to_mid,
            reducer.to_pair,
        )

    def copy(self, hop):
        src = self.held.at[5 if hop == 5 else hop]
        dst = self.held.at[5] if hop == 5 else self.landed.at[hop]
        return pltpu.make_async_remote_copy(
            src_ref=src,
            dst_ref=dst,
            send_sem=self.send_sem.at[hop],
            recv_sem=self.recv_sem.at[hop],
            device_id=self.devices[hop],
            device_id_type=MESH,
        )

    def begin(self, hop):
        if hop < 3:
            self.copy(hop).start()
        else:

            @pl.when(self.r.outer if hop == 3 else self.r.inner)
            def _():
                self.copy(hop).start()

    def end(self, hop):
        if hop < 3:
            self.copy(hop).wait()
            got = self.landed[hop]
            if hop < 2:
                row = lax.broadcasted_iota(jnp.int32, got.shape, 0)
                got = jnp.where(row < self.shared, got, 0.0)
            self.held[hop + 1] = self.held[hop] + got
        elif hop == 3:

            @pl.when(self.r.outer)
            def _():
                self.copy(3).wait_send()

            @pl.when(self.r.inner)
            def _():
                self.copy(3).wait_recv()
                self.held[4] = self.held[3] + self.landed[3]

        elif hop == 4:

            @pl.when(self.r.inner)
            def _():
                self.copy(4).wait()
                self.held[5] = self.held[4] + self.landed[4]

        else:

            @pl.when(self.r.inner)
            def _():
                self.copy(5).wait_send()

            @pl.when(self.r.outer)
            def _():
                self.copy(5).wait_recv()


def layer_kernel(
    lengths_in,
    x_ref,
    cot_ref,
    wqkv_ref,
    wout_ref,
    wup_ref,
    wdown_ref,
    bout_in,
    gain1_in,
    bias1_in,
    bdown_in,
    gain2_in,
    bias2_in,
    bup_in,
    bquery_in,
    bvalue_in,
    out_ref,
    gin_ref,
    gdown_ref,
    gup_ref,
    gout_ref,
    gqkv_ref,
    vsum_ref,
    xa,
    wq,
    wo,
    wu,
    wd,
    qkv,
    pt,
    cc,
    ua,
    act,
    gp,
    g2a,
    g1a,
    part,
    rc,
    ys,
    ry,
    xh1,
    rstd1,
    resid,
    cot,
    gb,
    rx,
    rz,
    rm,
    rb,
    rn,
    rq,
    held,
    landed,
    vg,
    vec_ref,
    grads,
    lengths_ref,
    load_sem,
    store_sem,
    agy_send,
    agy_recv,
    agc_send,
    agc_recv,
    agf_send,
    agf_recv,
    rsc_send,
    rsc_recv,
    rsy_send,
    rsy_recv,
    hop_send,
    hop_recv,
    vec_send,
    vec_recv,
    grad_sem,
    *small_refs,
    summed,
):
    batches = x_ref.shape[0]
    block = x_ref.shape[1]
    width = x_ref.shape[2]
    head_cols = wo.shape[0]
    hidden = wu.shape[1]
    rows = 4 * block
    pairs = head_cols // 128
    t = lax.axis_index("tensor")
    c = lax.rem(t, 2)
    y = lax.div(t, 2)
    t_core = y * 2 + (1 - c)
    t_y = (1 - y) * 2 + c
    t_far = (1 - y) * 2 + (1 - c)
    core = {"tensor": t_core}
    across = {"tensor": t_y}

    gathers = (xa, ua, g2a, g1a)

    def remote(src, dst, send, recv, device):
        return pltpu.make_async_remote_copy(
            src_ref=src, dst_ref=dst, send_sem=send, recv_sem=recv, device_id=device, device_id_type=MESH
        )

    def ag_y(p, s, at, src=None):
        buf = gathers[p]
        return remote(
            buf.at[s, at] if src is None else src, buf.at[s, at], agy_send.at[p, s], agy_recv.at[p, s], across
        )

    def ag_c(p, s, at, src=None):
        buf = gathers[p]
        return remote(
            buf.at[s, at] if src is None else src, buf.at[s, at], agc_send.at[p, s], agc_recv.at[p, s], core
        )

    def ag_f(p, s, at):
        buf = gathers[p]
        return remote(buf.at[s, at], buf.at[s, at], agf_send.at[p, s], agf_recv.at[p, s], core)

    def rs_c(p, s):
        return remote(part.at[s, 1 - c], rc.at[s], rsc_send.at[p, s], rsc_recv.at[p, s], core)

    def rs_y(p, s):
        return remote(ys.at[s], ry.at[s], rsy_send.at[p, s], rsy_recv.at[p, s], across)

    def load(index, src, dst):
        return pltpu.make_async_copy(src, dst, load_sem.at[index])

    def store(index, src, dst):
        return pltpu.make_async_copy(src, dst, store_sem.at[index])

    loads = [load(s, x_ref.at[s], xa.at[s, t]) for s in range(batches)]
    n = batches
    load_wq = load(n, wqkv_ref, wq)
    load_wo = load(n + 1, wout_ref, wo)
    load_wu = load(n + 2, wup_ref, wu)
    load_wd = load(n + 3, wdown_ref, wd)
    load_cot = load(n + 4, cot_ref, cot)

    for cp in loads:
        cp.start()
    if summed:
        reducer = Reducer(gb, rx, rz, rm, rb, rn, rq, hop_send, hop_recv)
        vectors = VectorReducer(reducer, held, landed, vec_send, vec_recv, 6)
        reducer.greet((core, across))
    else:
        barrier = pltpu.get_barrier_semaphore()
        for device in (core, across):
            pl.semaphore_signal(barrier, inc=1, device_id=device, device_id_type=MESH)
        pl.semaphore_wait(barrier, 2)
    for s in range(batches):
        ag_y(0, s, t, x_ref.at[s]).start()
        ag_c(0, s, t, x_ref.at[s]).start()
    load_wq.start()
    load_wo.start()
    load_wu.start()
    load_wd.start()
    load_cot.start()

    vg[...] = jnp.zeros_like(vg)
    small_ins = (bout_in, gain1_in, bias1_in, bdown_in, gain2_in, bias2_in, bup_in, bquery_in, bvalue_in)
    small = [load(n + 5, lengths_in, lengths_ref)]
    small += [load(n + 6 + i, ref, held_ref) for i, (ref, held_ref) in enumerate(zip(small_ins, small_refs))]
    for cp in small:
        cp.start()
    for cp in small:
        cp.wait()
    for i, ref in enumerate(small_refs[:7]):
        vec_ref[i : i + 1, :] = ref[...].astype(F32).reshape(1, -1)
    for i, ref in enumerate(small_refs[7:]):
        vec_ref[7:8, i * head_cols : (i + 1) * head_cols] = ref[...].astype(F32).reshape(1, -1)
    lane = lax.broadcasted_iota(jnp.int32, (rows, 128), 1)
    low_half = lane < HD
    empty = jnp.zeros((rows, 128), LOW)

    def masked(values, h):
        return jnp.where(low_half, values, empty) if h == 0 else jnp.where(low_half, empty, values)

    def vec(i):
        return vec_ref[i : i + 1, :]

    def whole(ref, s):
        return ref[s].reshape(rows, width)

    def put_part(s, j, values):
        values = values.astype(LOW)
        cols = pl.ds(pl.multiple_of(j * TILE, TILE), TILE)
        for b in range(4):
            part[s, b % 2, b // 2, :, cols] = values[b * block : (b + 1) * block]

    def compute_a(s):
        tokens = whole(xa, s)
        q = dot(tokens, wq[0]) + vec_ref[7:8, :head_cols]
        qkv[s, 0] = q.astype(LOW) * LOW(HD ** (-0.5))
        qkv[s, 1] = dot(tokens, wq[1]).astype(LOW)
        v = dot(tokens, wq[2]) + vec_ref[7:8, head_cols : 2 * head_cols]
        qkv[s, 2] = v.astype(LOW)
        keys_valid = lax.broadcasted_iota(jnp.int32, (rows, rows), 0) < lengths_ref[0, s]

        def pair(j, carry):
            cols = pl.ds(pl.multiple_of(j * 128, 128), 128)
            q, k, v = qkv[s, 0, :, cols], qkv[s, 1, :, cols], qkv[s, 2, :, cols]
            context = jnp.zeros((128, rows), F32)
            for h in range(2):
                scores = dot(k, masked(q, h), 1, 1)
                scores = jnp.where(keys_valid, scores, -1e30)
                weights = jnp.exp(scores - jnp.max(scores, axis=0, keepdims=True))
                p = (weights * (1.0 / row_sum(weights))).astype(LOW)
                pt[s, 2 * j + h] = p
                context = context + dot(masked(v, h).T, p)
            cc[s, :, cols] = context.T.astype(LOW)
            return carry

        lax.fori_loop(0, pairs, pair, 0)

        def out(j, carry):
            cols = pl.ds(pl.multiple_of(j * TILE, TILE), TILE)
            put_part(s, j, dot(cc[s], wo[:, cols]))
            return carry

        lax.fori_loop(0, width // TILE, out, 0)

    def compute_c(s):
        def tile(j, carry):
            cols = pl.ds(pl.multiple_of(j * TILE, TILE), TILE)
            h = dot(whole(ua, s), wu[:, cols]) + vec_ref[6:7, cols]
            phi, density = gelu_parts(h)
            act[s, :, cols] = (h * phi).astype(LOW)
            gp[s, :, cols] = (phi + h * density).astype(LOW)
            return carry

        lax.fori_loop(0, hidden // TILE, tile, 0)

        def down(j, carry):
            cols = pl.ds(pl.multiple_of(j * TILE, TILE), TILE)
            put_part(s, j, dot(act[s], wd[:, cols]))
            return carry

        lax.fori_loop(0, width // TILE, down, 0)

    def compute_e_hidden(s):
        def tile(j, carry):
            cols = pl.ds(pl.multiple_of(j * TILE, TILE), TILE)
            gh = gp[s, :, cols].astype(F32) * dot(whole(g2a, s), wd[cols, :], 1, 1)
            vg[6:7, cols] += row_sum(gh)
            gp[s, :, cols] = gh.astype(LOW)
            return carry

        lax.fori_loop(0, hidden // TILE, tile, 0)

    def compute_e_back(s):
        def back(j, carry):
            rows_at = pl.ds(pl.multiple_of(j * TILE, TILE), TILE)
            put_part(s, j, dot(gp[s], wu[rows_at, :], 1, 1))
            return carry

        lax.fori_loop(0, width // TILE, back, 0)

    def head_pair_back(s, j):
        cols = slice(j * 128, (j + 1) * 128)
        q, k, v = qkv[s, 0, :, cols], qkv[s, 1, :, cols], qkv[s, 2, :, cols]
        gc = grads[:, cols]
        dq = jnp.zeros((128, rows), F32)
        dk = jnp.zeros((rows, 128), F32)
        dv = jnp.zeros((rows, 128), F32)
        for h in range(2):
            gc_h = masked(gc, h)
            p = pt[s, 2 * j + h]
            wide = p.astype(F32)
            product = wide * dot(v, gc_h, 1, 1)
            ds = (product - wide * row_sum(product)).astype(LOW)
            dv = dv + dot(p, gc_h)
            dk = dk + dot(ds, masked(q, h))
            dq = dq + dot(masked(k, h).T, ds)
        dq = dq.T * (HD ** (-0.5))
        vg[7:8, cols] += row_sum(dq)
        vg[7:8, head_cols + j * 128 : head_cols + (j + 1) * 128] += row_sum(dv)
        qkv[s, 0, :, cols] = dq.astype(LOW)
        qkv[s, 1, :, cols] = dk.astype(LOW)
        qkv[s, 2, :, cols] = dv.astype(LOW)

    def compute_g_first(s):
        grads[...] = dot(whole(g1a, s), wo[...], 1, 1).astype(LOW)
        for j in range(pairs // 2):
            head_pair_back(s, j)

    def compute_g_second(s):
        for j in range(pairs // 2, pairs):
            head_pair_back(s, j)

    def compute_g_back(s):
        def back(j, carry):
            at = pl.ds(pl.multiple_of(j * TILE, TILE), TILE)
            total = dot(qkv[s, 0], wq[0, at, :], 1, 1)
            total = total + dot(qkv[s, 1], wq[1, at, :], 1, 1)
            total = total + dot(qkv[s, 2], wq[2, at, :], 1, 1)
            put_part(s, j, total)
            return carry

        lax.fori_loop(0, width // TILE, back, 0)

    computes = (
        (compute_a,),
        (compute_c,),
        (compute_e_hidden, compute_e_back),
        (compute_g_first, compute_g_second, compute_g_back),
    )

    def reduced(p, s):
        rs_y(p, s).wait()
        rs_c(p, s).wait_send()
        return part[s, c, y].astype(F32) + rc[s, y].astype(F32) + ry[s].astype(F32)

    def send_on(p, s):
        ag_y(p, s, t).start()
        ag_c(p, s, t).start()

    def finish_a(s):
        z = xa[s, t].astype(F32) + (reduced(0, s) + vec(0))
        centred = z - row_mean(z)
        rstd = lax.rsqrt(row_mean(centred * centred) + EPSILON)
        hat = centred * rstd
        xh1[s] = hat
        rstd1[s] = jnp.broadcast_to(rstd, rstd1.shape[1:])
        ua[s, t] = (hat * vec(1) + vec(2)).astype(LOW)
        send_on(1, s)

    def finish_c(s):
        z = (xh1[s] * vec(1) + vec(2)) + (reduced(1, s) + vec(3))
        centred = z - row_mean(z)
        rstd = lax.rsqrt(row_mean(centred * centred) + EPSILON)
        hat = centred * rstd
        valid = t * block + lax.broadcasted_iota(jnp.int32, (block, width), 0) < lengths_ref[0, s]
        incoming = jnp.where(valid, cot[s].astype(F32), 0.0)
        scaled = incoming * vec(4)
        grad = rstd * (scaled - row_mean(scaled) - hat * row_mean(scaled * hat))
        resid[s] = grad
        g2a[s, t] = grad.astype(LOW)
        send_on(2, s)
        cot[s] = jnp.where(valid, hat * vec(4) + vec(5), 0.0).astype(LOW)
        store(s, cot.at[s], out_ref.at[s]).start()
        vg[3:4, :] += row_sum(grad)
        vg[4:5, :] += row_sum(incoming * hat)
        vg[5:6, :] += row_sum(incoming)

    def finish_e(s):
        gu = resid[s] + reduced(2, s)
        hat = xh1[s]
        scaled = gu * vec(1)
        grad = rstd1[s, :, :1] * (scaled - row_mean(scaled) - hat * row_mean(scaled * hat))
        resid[s] = grad
        g1a[s, t] = grad.astype(LOW)
        send_on(3, s)
        vg[0:1, :] += row_sum(grad)
        vg[1:2, :] += row_sum(gu * hat)
        vg[2:3, :] += row_sum(gu)

    def finish_g(s):
        store(s, cot.at[s], out_ref.at[s]).wait()
        cot[s] = (resid[s] + reduced(3, s)).astype(LOW)
        store(batches + s, cot.at[s], gin_ref.at[s]).start()

    finishes = (finish_a, finish_c, finish_e, finish_g)

    def forward_block(p, s):
        ag_y(p, s, t_y).wait_recv()
        ag_f(p, s, t_y).start()

    def gathered(p, s):
        ag_c(p, s, t_core).wait_recv()
        ag_f(p, s, t_far).wait_recv()

    def send_sums(p, s):
        rs_c(p, s).start()

    def pass_sums(p, s):
        rs_c(p, s).wait_recv()
        ys[s] = (part[s, c, 1 - y].astype(F32) + rc[s, 1 - y].astype(F32)).astype(LOW)
        rs_y(p, s).start()

    def tall(values):
        return values.reshape(batches * rows, -1)

    per_piece = TILE // UNIT
    down_pieces = hidden // TILE
    up_pieces = width // TILE
    early_pieces = down_pieces + up_pieces
    pieces = early_pieces + 1 + 3

    def piece(d):
        if d < early_pieces:
            if d < down_pieces:
                cols = slice(d * TILE, (d + 1) * TILE)
                left, right = tall(act[:, :, cols]), g2a
            else:
                cols = slice((d - down_pieces) * TILE, (d - down_pieces + 1) * TILE)
                left, right = tall(ua[:, :, :, cols]), gp
        elif d == early_pieces:
            left, right = tall(cc[...]), g1a
        else:
            right = tall(qkv[:, d - early_pieces - 1])
            for j in range(per_piece):
                cols = slice(j * TILE, (j + 1) * TILE)
                product = dot(tall(xa[:, :, :, cols]), right, 0, 0).astype(LOW)
                for h in range(per_piece):
                    gb[d * per_piece + j, :, :, h * head_cols : (h + 1) * head_cols] = product[
                        h * UNIT : (h + 1) * UNIT
                    ].reshape(2, UNIT // 2, head_cols)
            return

        def half(j, carry):
            cols = pl.ds(pl.multiple_of(j * (width // 2), width // 2), width // 2)
            columns = right[:, :, cols] if len(right.shape) == 3 else right[:, :, :, cols]
            product = dot(left, tall(columns), 0, 0).astype(LOW)
            for u in range(per_piece):
                gb[d * per_piece + u, :, :, cols] = product[u * UNIT : (u + 1) * UNIT].reshape(
                    2, UNIT // 2, width // 2
                )
            return carry

        lax.fori_loop(0, 2, half, 0)

    def unit_stores(i, src):
        def make(n, src, dst):
            return pltpu.make_async_copy(src, dst, grad_sem.at[i, n])

        if i < down_pieces * per_piece:
            return [make(0, src, gdown_ref.at[i])]
        i_up = i - down_pieces * per_piece
        if i_up < up_pieces * per_piece:
            return [make(0, src, gup_ref.at[i_up])]
        i_out = i - early_pieces * per_piece
        if i_out < per_piece:
            return [make(0, src, gout_ref.at[i_out])]
        i_qkv = i_out - per_piece
        kind, j = i_qkv // per_piece, i_qkv % per_piece
        return [
            make(h, src.at[:, :, pl.ds(h * head_cols, head_cols)], gqkv_ref.at[kind, j * per_piece + h])
            for h in range(per_piece)
        ]

    unit_pairs = pieces * per_piece // 2

    def pair_stores(k):
        return unit_stores(2 * k, rx.at[k % RING]) + unit_stores(2 * k + 1, rb.at[k % RING])

    ticks = iter(range(-1, unit_pairs + STAGE_AT[-1] + STORE_TICKS + 1))

    def tick():
        now = next(ticks, None)
        if now is None:
            return False
        if 0 <= now - STAGE_AT[-1] - STORE_TICKS < unit_pairs:
            reducer.drain(now - STAGE_AT[-1] - STORE_TICKS)
            for cp in pair_stores(now - STAGE_AT[-1] - STORE_TICKS):
                cp.wait()
        k = now + 1
        if k < unit_pairs:
            if 2 * k % per_piece == 0:
                piece(2 * k // per_piece)
            reducer.start(k)
        for stage, at in zip(reducer.stages, STAGE_AT):
            if 0 <= now - at < unit_pairs:
                stage(reducer, now - at)
        if 0 <= now - STAGE_AT[-1] < unit_pairs:
            for cp in pair_stores(now - STAGE_AT[-1]):
                cp.start()
        return True

    def step(s, carry, p):
        gathered(p, s)
        for compute in computes[p]:
            compute(s)
        send_sums(p, s)
        pass_sums(p, s)
        if p > 0:

            @pl.when(s == 0)
            def _():
                finishes[p - 1](batches - 1)

        @pl.when(s > 0)
        def _():
            finishes[p](s - 1)

        @pl.when(s < batches - 1)
        def _():
            forward_block(p, s + 1)

        @pl.when(s == batches - 1)
        def _():
            forward_block(p + 1, 0)

        return carry

    forward_block(0, 0)
    for cp in loads:
        cp.wait()
    load_wq.wait()
    load_wo.wait()
    lax.fori_loop(0, batches, functools.partial(step, p=0), 0)
    load_wu.wait()
    load_wd.wait()
    load_cot.wait()
    lax.fori_loop(0, batches, functools.partial(step, p=1), 0)

    hops = iter(range(VECTOR_HOPS + 1))

    def vector_hop():
        hop = next(hops, None)
        if hop is None:
            return False
        if hop == 0:
            held[0] = vg[...]
        else:
            vectors.end(hop - 1)
        if hop < VECTOR_HOPS:
            vectors.begin(hop)
        return True

    actions = {
        "gather": gathered,
        "compute": lambda p, s, part: computes[p][part](s),
        "send": send_sums,
        "pass": pass_sums,
        "finish": lambda p, s: finishes[p](s),
        "forward": forward_block,
    }
    last = PHASES * batches - 1
    vectors_wait = {("compute", last, 1), ("finish", last - batches)}
    for action in SCHEDULE:
        if action == TICK:
            if summed:
                if not vectors_wait:
                    vector_hop()
                tick()
        else:
            name, index, *which = action
            actions[name](index // batches, index % batches, *which)
            vectors_wait.discard(action)
    if summed:
        while tick():
            vector_hop()
        while vector_hop():
            pass
        store_sums = store(2 * batches, held.at[VECTOR_HOPS - 1], vsum_ref)
        store_sums.start()
    else:
        stores = []
        for d in range(pieces):
            piece(d)
            for i in range(d * per_piece, (d + 1) * per_piece):
                stores += unit_stores(i, gb.at[i])
                for cp in unit_stores(i, gb.at[i]):
                    cp.start()
        store_sums = store(2 * batches, vg, vsum_ref)
        store_sums.start()
        for cp in stores:
            cp.wait()
    for s in range(batches):
        store(batches + s, cot.at[s], gin_ref.at[s]).wait()
    store_sums.wait()

    def drain(i, carry):
        for p in range(PHASES):
            ag_y(p, i, t).wait_send()
            ag_c(p, i, t).wait_send()
            ag_f(p, i, t_y).wait_send()
        return carry

    lax.fori_loop(0, batches, drain, 0)


def run_layer(lengths, x, cot, wqkv, wout, wup, wdown, vectors, summed):
    batches, block, width = x.shape
    rows = 4 * block
    head_cols = wout.shape[0]
    heads = head_cols // HD
    hidden = wup.shape[1]
    half = UNIT // 2
    down, up, out = hidden // UNIT, width // UNIT, head_cols // UNIT
    units = down + up + out + 3 * out
    ring, short_ring = (RING, SHORT_RING) if summed else (1, 1)
    any_space = pl.BlockSpec(memory_space=pl.ANY)
    dma = pltpu.SemaphoreType.DMA
    low = lambda *shape: pltpu.VMEM(shape, LOW)
    wide = lambda *shape: pltpu.VMEM(shape, F32)
    gathered = low(batches, 4, block, width)
    scratch = [
        gathered,
        low(3, width, head_cols),
        low(head_cols, width),
        low(width, hidden),
        low(hidden, width),
        low(batches, 3, rows, head_cols),
        low(batches, heads, rows, rows),
        low(batches, rows, head_cols),
        gathered,
        low(batches, rows, hidden),
        low(batches, rows, hidden),
        gathered,
        gathered,
        low(batches, 2, 2, block, width),
        low(batches, 2, block, width),
        low(batches, block, width),
        low(batches, block, width),
        wide(batches, block, width),
        wide(batches, block, 128),
        wide(batches, block, width),
        low(batches, block, width),
        low(units, 2, half, width),
        low(ring, 2, half, width),
        low(short_ring, half, width),
        low(short_ring, half, width),
        low(ring, 2, half, width),
        low(short_ring, half, width),
        low(short_ring, half, width),
        wide(VECTOR_HOPS, 8, width),
        wide(VECTOR_HOPS - 1, 8, width),
        wide(8, width),
        wide(8, width),
        low(rows, head_cols),
        pltpu.SMEM(lengths.shape, jnp.int32),
        dma((batches + 15,)),
        dma((2 * batches + 1,)),
    ]
    scratch += [dma((PHASES, batches))] * 10 + [dma((HOPS, units // 2))] * 2 + [dma((VECTOR_HOPS,))] * 2
    scratch.append(dma((units, TILE // UNIT)))
    scratch += [low(width)] * 7 + [low(head_cols)] * 2
    low_out = lambda *shape: jax.ShapeDtypeStruct(shape, LOW)
    return pl.pallas_call(
        functools.partial(layer_kernel, summed=summed),
        out_shape=(
            low_out(batches, block, width),
            low_out(batches, block, width),
            low_out(down, 2, half, width),
            low_out(up, 2, half, hidden),
            low_out(out, 2, half, width),
            low_out(3, width // UNIT, 2, half, head_cols),
            jax.ShapeDtypeStruct((8, width), F32),
        ),
        in_specs=[any_space] * 16,
        out_specs=(any_space,) * 7,
        scratch_shapes=scratch,
        compiler_params=pltpu.CompilerParams(
            collective_id=0, has_side_effects=True, vmem_limit_bytes=63 << 20
        ),
        name="layer",
    )(lengths, x, cot, wqkv, wout, wup, wdown, *vectors)


def widen_kernel(
    down_ref, up_ref, out_ref, qkv_ref, sums_ref, rows_ref, gin_ref,
    down_wide, up_wide, out_wide, qkv_wide, *refs,
):
    vectors, refs = refs[:9], refs[9:]
    rows_copy, gin_copy, low, wide, low_qkv, wide_qkv, rows, sums, load_sem, store_sem, vec_sem, *made_vectors = refs
    work = []

    def part(src, dst, held, made):
        n = len(work)
        get = pltpu.make_async_copy(src, held, load_sem.at[n])
        put = pltpu.make_async_copy(made, dst, store_sem.at[n])
        work.append((get, held, made, put))

    i = 0
    for src, dst in ((down_ref, down_wide), (up_ref, up_wide), (out_ref, out_wide)):
        for at in range(0, src.shape[0], TILE):
            part(src.at[pl.ds(at, TILE)], dst.at[pl.ds(at, TILE)], low.at[i], wide.at[i])
            i += 1
    for i in range(3):
        part(qkv_ref.at[i], qkv_wide.at[i], low_qkv.at[i], wide_qkv.at[i])
    for i, (src, dst) in enumerate(((rows_ref, rows_copy), (gin_ref, gin_copy))):
        block = rows.at[i]
        part(src, dst, block, block)
    load_sums = pltpu.make_async_copy(sums_ref, sums, vec_sem.at[0])
    for get, _, _, _ in work[:LOADS_AHEAD]:
        get.start()
    load_sums.start()
    for n, (get, held, made, put) in enumerate(work):
        get.wait()
        if n + LOADS_AHEAD < len(work):
            work[n + LOADS_AHEAD][0].start()
        if made is not held:
            made[...] = held[...].astype(F32)
        put.start()
    load_sums.wait()
    head_cols = out_ref.shape[0]
    for i in range(2):
        made_vectors[i][...] = sums[7, i * head_cols : (i + 1) * head_cols]
    for ref, row in zip(made_vectors[2:], (0, 1, 2, 6, 3, 4, 5)):
        ref[...] = sums[row]
    puts = [
        pltpu.make_async_copy(src, dst, vec_sem.at[1 + i])
        for i, (src, dst) in enumerate(zip(made_vectors, vectors))
    ]
    for cp in puts:
        cp.start()
    for cp in puts:
        cp.wait()
    for _, _, _, put in work:
        put.wait()


def widen(down, up, out, qkv, sums, rows, gin):
    any_space = pl.BlockSpec(memory_space=pl.ANY)
    dma = pltpu.SemaphoreType.DMA
    width = down.shape[1]
    pieces = (down.shape[0] + up.shape[0] + out.shape[0]) // TILE
    as_wide = lambda a: jax.ShapeDtypeStruct(a.shape, F32)
    vector = lambda n: jax.ShapeDtypeStruct((n,), F32)
    return pl.pallas_call(
        widen_kernel,
        out_shape=(
            *map(as_wide, (down, up, out, qkv)),
            *[vector(out.shape[0])] * 2,
            *[vector(width)] * 7,
            jax.ShapeDtypeStruct(rows.shape, rows.dtype),
            jax.ShapeDtypeStruct(gin.shape, gin.dtype),
        ),
        in_specs=[any_space] * 7,
        out_specs=(any_space,) * 15,
        scratch_shapes=[
            pltpu.VMEM((pieces, TILE, width), LOW),
            pltpu.VMEM((pieces, TILE, width), F32),
            pltpu.VMEM(qkv.shape, LOW),
            pltpu.VMEM(qkv.shape, F32),
            pltpu.VMEM((2, *rows.shape), LOW),
            pltpu.VMEM(sums.shape, F32),
            dma((pieces + 5,)),
            dma((pieces + 5,)),
            dma((10,)),
            *[pltpu.VMEM((out.shape[0],), F32)] * 2,
            *[pltpu.VMEM((width,), F32)] * 7,
        ],
        compiler_params=pltpu.CompilerParams(vmem_limit_bytes=62 << 20),
        name="widen",
    )(down, up, out, qkv, sums, rows, gin)


def per_device(
    inputs,
    lengths,
    cotangent,
    w_qkv,
    b_query,
    b_value,
    w_out,
    b_out,
    ln1_gain,
    ln1_bias,
    w_up,
    b_up,
    w_down,
    b_down,
    ln2_gain,
    ln2_bias,
):
    width = inputs.shape[3]
    head_cols = w_out.shape[0]
    hidden = w_up.shape[1]
    summed = lax.axis_size("dp") == 8
    output, grad_inputs, grad_down, grad_up, grad_out, grad_qkv, sums = run_layer(
        lengths,
        inputs[0],
        cotangent[0],
        jnp.transpose(w_qkv, (1, 0, 2)),
        w_out,
        w_up,
        w_down,
        (b_out, ln1_gain, ln1_bias, b_down, ln2_gain, ln2_bias, b_up, b_query, b_value),
        summed,
    )
    if not summed:
        grad_down, grad_up, grad_out, grad_qkv, sums = lax.psum(
            (grad_down, grad_up, grad_out, grad_qkv, sums), "dp"
        )
        sums = jnp.concatenate([lax.psum(sums[:6], "tensor"), sums[6:]])
    grad_down, grad_up, grad_out, grad_qkv, *rest = widen(
        grad_down.reshape(hidden, width),
        grad_up.reshape(width, hidden),
        grad_out.reshape(head_cols, width),
        grad_qkv.reshape(3, width, head_cols),
        sums,
        output,
        grad_inputs,
    )
    gquery, gvalue, gbout, ggain1, gbias1, gbup, gbdown, ggain2, gbias2, output, grad_inputs = rest
    return (
        output[None],
        grad_inputs[None],
        jnp.transpose(grad_qkv, (1, 0, 2)),
        gquery,
        gvalue,
        grad_out,
        gbout,
        ggain1,
        gbias1,
        grad_up,
        gbup,
        grad_down,
        gbdown,
        ggain2,
        gbias2,
    )


def solution(mesh):
    return jax.shard_map(
        per_device,
        mesh=mesh,
        in_specs=(
            P("dp", None, "tensor", None),
            P("dp", None),
            P("dp", None, "tensor", None),
            P(None, None, "tensor"),
            P("tensor"),
            P("tensor"),
            P("tensor", None),
            P(),
            P(),
            P(),
            P(None, "tensor"),
            P("tensor"),
            P("tensor", None),
            P(),
            P(),
            P(),
        ),
        out_specs=(
            P("dp", None, "tensor", None),
            P("dp", None, "tensor", None),
            P(None, None, "tensor"),
            P("tensor"),
            P("tensor"),
            P("tensor", None),
            P(),
            P(),
            P(),
            P(None, "tensor"),
            P("tensor"),
            P("tensor", None),
            P(),
            P(),
            P(),
        ),
        check_vma=False,
    )
```

```python
import functools

import jax
import jax.numpy as jnp
from jax import lax
from jax.experimental import pallas as pl
from jax.experimental.pallas import tpu as pltpu
from jax.sharding import PartitionSpec as P

HD = 64
EPSILON = 1e-05
F32 = jnp.float32
LOW = jnp.bfloat16
MESH = pl.DeviceIdType.MESH
TILE = 256
PHASES = 4
UNIT = 64


def dot(left, right, left_dim=1, right_dim=0):
    return lax.dot_general(
        left, right, (((left_dim,), (right_dim,)), ((), ())), preferred_element_type=F32
    )


def row_sum(values):
    return jnp.sum(values, axis=0, keepdims=True)


def row_mean(values):
    return jnp.mean(values, axis=-1, keepdims=True)


def gelu_parts(h):
    t = 1.0 / (1.0 + 0.23164188 * jnp.abs(h))
    density = jnp.exp(-0.5 * h * h)
    series = t * (
        0.127414796
        + t * (-0.142248368 + t * (0.7107068705 + t * (-0.7265760135 + t * 0.5307027145)))
    )
    tail = series * density
    return jnp.where(h < 0.0, tail, 1.0 - tail), density * 0.3989422804014327


HOPS = 11
RING = 16
SHORT_RING = 8
STAGE_AT = (0, 1, 2, 3, 4, 6)
STORE_TICKS = 3
LOADS_AHEAD = 16
TICK = ("tick", 0)
SCHEDULE = (
    ("gather", 6),
    ("finish", 5),
    ("forward", 7),
    ("compute", 6, 0),
    ("compute", 6, 1),
    ("send", 6),
    ("forward", 8),
    ("gather", 7),
    ("gather", 8),
    TICK,
    ("compute", 7, 0),
    ("pass", 6),
    TICK,
    ("compute", 8, 0),
    TICK,
    ("compute", 8, 1),
    ("compute", 7, 1),
    TICK,
    ("send", 7),
    TICK,
    ("send", 8),
    ("finish", 6),
    TICK,
    ("pass", 8),
    *[TICK] * 2,
    ("pass", 7),
    TICK,
    ("forward", 9),
    ("finish", 8),
    TICK,
    ("gather", 9),
    TICK,
    ("finish", 7),
    TICK,
    ("forward", 11),
    TICK,
    ("compute", 9, 0),
    TICK,
    ("forward", 10),
    ("compute", 9, 1),
    TICK,
    ("gather", 11),
    ("gather", 10),
    ("compute", 10, 0),
    TICK,
    ("compute", 10, 1),
    TICK,
    ("compute", 11, 0),
    TICK,
    ("compute", 11, 1),
    TICK,
    ("compute", 10, 2),
    ("send", 10),
    TICK,
    ("pass", 10),
    TICK,
    ("compute", 9, 2),
    ("send", 9),
    *[TICK] * 2,
    ("compute", 11, 2),
    TICK,
    ("pass", 9),
    TICK,
    ("send", 11),
    TICK,
    ("pass", 11),
    ("finish", 10),
    ("finish", 9),
    *[TICK] * 2,
    ("finish", 11),
)


class Reducer:
    def __init__(self, gb, rx, rz, rm, rb, rn, rq, send_sems, recv_sems):
        dp = lax.axis_index("dp")
        self.x = lax.rem(dp, 2)
        self.z = lax.div(dp, 2)
        self.side = lax.rem(self.z, 2)
        self.m = lax.div(self.z, 2)
        self.inner = self.side != self.m
        self.outer = self.side == self.m
        self.to_x = {"dp": self.z * 2 + (1 - self.x)}
        self.to_pair = {"dp": (self.z + 1 - 2 * self.side) * 2 + self.x}
        self.to_mid = {"dp": (3 - self.z) * 2 + self.x}
        self.gb, self.rx, self.rz, self.rm, self.rb, self.rn, self.rq = gb, rx, rz, rm, rb, rn, rq
        self.send_sems, self.recv_sems = send_sems, recv_sems

    def greet(self, extra=()):
        barrier = pltpu.get_barrier_semaphore()

        def signal(device):
            pl.semaphore_signal(barrier, inc=1, device_id=device, device_id_type=MESH)

        for device in (self.to_x, self.to_pair) + tuple(extra):
            signal(device)

        @pl.when(self.inner)
        def _():
            signal(self.to_mid)
            pl.semaphore_wait(barrier, 3 + len(extra))

        @pl.when(self.outer)
        def _():
            pl.semaphore_wait(barrier, 2 + len(extra))

    def copy(self, hop, k, src, dst, device):
        return pltpu.make_async_remote_copy(
            src_ref=src,
            dst_ref=dst,
            send_sem=self.send_sems.at[hop, k],
            recv_sem=self.recv_sems.at[hop, k],
            device_id=device,
            device_id_type=MESH,
        )

    def ax(self, k):
        return self.copy(0, k, self.gb.at[2 * k, 1 - self.x], self.rx.at[k % RING, 1 - self.x], self.to_x)

    def az(self, k):
        return self.copy(1, k, self.gb.at[2 * k, self.x], self.rz.at[k % SHORT_RING], self.to_pair)

    def am(self, k):
        return self.copy(2, k, self.gb.at[2 * k, self.x], self.rm.at[k % SHORT_RING], self.to_mid)

    def ao(self, k):
        return self.copy(3, k, self.rx.at[k % RING, self.x], self.rx.at[k % RING, self.x], self.to_pair)

    def ag(self, k):
        return self.copy(4, k, self.rx.at[k % RING, self.x], self.rx.at[k % RING, self.x], self.to_x)

    def bi(self, k):
        return self.copy(5, k, self.gb.at[2 * k + 1], self.rb.at[k % RING], self.to_pair)

    def bm(self, k):
        return self.copy(6, k, self.gb.at[2 * k + 1, 1 - self.m], self.rn.at[k % SHORT_RING], self.to_mid)

    def bx(self, k):
        return self.copy(7, k, self.gb.at[2 * k + 1, self.m], self.rq.at[k % SHORT_RING], self.to_x)

    def bg(self, k):
        return self.copy(8, k, self.rb.at[k % RING, self.m], self.rb.at[k % RING, self.m], self.to_mid)

    def bo(self, k):
        return self.copy(9, k, self.rb.at[k % RING, self.m], self.rb.at[k % RING, self.m], self.to_pair)

    def bp(self, k):
        return self.copy(10, k, self.rb.at[k % RING, 1 - self.m], self.rb.at[k % RING, 1 - self.m], self.to_pair)

    def add(self, out, left, right):
        out[...] = (left[...].astype(F32) + right[...].astype(F32)).astype(LOW)

    def start(self, k):
        self.ax(k).start()

        @pl.when(self.outer)
        def _():
            self.bi(k).start()

    def stage1(self, k):
        self.ax(k).wait()
        own = self.gb.at[2 * k, self.x]
        self.add(own, own, self.rx.at[k % RING, self.x])

        @pl.when(self.outer)
        def _():
            self.az(k).start()

    def stage2(self, k):
        @pl.when(self.inner)
        def _():
            self.bi(k).wait_recv()
            away = self.gb.at[2 * k + 1, 1 - self.m]
            self.add(away, away, self.rb.at[k % RING, 1 - self.m])
            self.bm(k).start()
            own = self.gb.at[2 * k + 1, self.m]
            self.add(own, own, self.rb.at[k % RING, self.m])
            self.az(k).wait_recv()
            own = self.gb.at[2 * k, self.x]
            self.add(own, own, self.rz.at[k % SHORT_RING])
            self.am(k).start()

    def stage3(self, k):
        @pl.when(self.inner)
        def _():
            self.bm(k).wait()
            own = self.gb.at[2 * k + 1, self.m]
            self.add(own, own, self.rn.at[k % SHORT_RING])
            self.bx(k).start()
            self.am(k).wait()
            self.add(self.rx.at[k % RING, self.x], self.gb.at[2 * k, self.x], self.rm.at[k % SHORT_RING])
            self.ao(k).start()
            self.ag(k).start()

    def stage4(self, k):
        @pl.when(self.inner)
        def _():
            self.bx(k).wait()
            self.add(self.rb.at[k % RING, self.m], self.gb.at[2 * k + 1, self.m], self.rq.at[k % SHORT_RING])
            self.bg(k).start()
            self.bo(k).start()

        @pl.when(self.outer)
        def _():
            self.ao(k).wait_recv()
            self.ag(k).start()

    def stage5(self, k):
        @pl.when(self.inner)
        def _():
            self.bg(k).wait_recv()
            self.bp(k).start()

        self.ag(k).wait_recv()

    def stage6(self, k):
        @pl.when(self.outer)
        def _():
            self.bo(k).wait_recv()
            self.bp(k).wait_recv()

    def drain(self, k):
        self.ag(k).wait_send()

        @pl.when(self.inner)
        def _():
            self.ao(k).wait_send()
            self.bg(k).wait_send()
            self.bo(k).wait_send()
            self.bp(k).wait_send()

        @pl.when(self.outer)
        def _():
            self.az(k).wait_send()
            self.bi(k).wait_send()

    stages = (stage1, stage2, stage3, stage4, stage5, stage6)


VECTOR_HOPS = 6


class VectorReducer:
    def __init__(self, reducer, held, landed, send_sem, recv_sem, shared):
        t = lax.axis_index("tensor")
        c = lax.rem(t, 2)
        y = lax.div(t, 2)
        self.r = reducer
        self.held, self.landed, self.send_sem, self.recv_sem = held, landed, send_sem, recv_sem
        self.shared = shared
        self.devices = (
            {"tensor": y * 2 + (1 - c)},
            {"tensor": (1 - y) * 2 + c},
            reducer.to_x,
            reducer.to_pair,
            reducer.to_mid,
            reducer.to_pair,
        )

    def copy(self, hop):
        src = self.held.at[5 if hop == 5 else hop]
        dst = self.held.at[5] if hop == 5 else self.landed.at[hop]
        return pltpu.make_async_remote_copy(
            src_ref=src,
            dst_ref=dst,
            send_sem=self.send_sem.at[hop],
            recv_sem=self.recv_sem.at[hop],
            device_id=self.devices[hop],
            device_id_type=MESH,
        )

    def begin(self, hop):
        if hop < 3:
            self.copy(hop).start()
        else:

            @pl.when(self.r.outer if hop == 3 else self.r.inner)
            def _():
                self.copy(hop).start()

    def end(self, hop):
        if hop < 3:
            self.copy(hop).wait()
            got = self.landed[hop]
            if hop < 2:
                row = lax.broadcasted_iota(jnp.int32, got.shape, 0)
                got = jnp.where(row < self.shared, got, 0.0)
            self.held[hop + 1] = self.held[hop] + got
        elif hop == 3:

            @pl.when(self.r.outer)
            def _():
                self.copy(3).wait_send()

            @pl.when(self.r.inner)
            def _():
                self.copy(3).wait_recv()
                self.held[4] = self.held[3] + self.landed[3]

        elif hop == 4:

            @pl.when(self.r.inner)
            def _():
                self.copy(4).wait()
                self.held[5] = self.held[4] + self.landed[4]

        else:

            @pl.when(self.r.inner)
            def _():
                self.copy(5).wait_send()

            @pl.when(self.r.outer)
            def _():
                self.copy(5).wait_recv()


def layer_kernel(
    lengths_in,
    x_ref,
    cot_ref,
    wqkv_ref,
    wout_ref,
    wup_ref,
    wdown_ref,
    bout_in,
    gain1_in,
    bias1_in,
    bdown_in,
    gain2_in,
    bias2_in,
    bup_in,
    bquery_in,
    bvalue_in,
    out_ref,
    gin_ref,
    gdown_ref,
    gup_ref,
    gout_ref,
    gqkv_ref,
    vsum_ref,
    xa,
    wq,
    wo,
    wu,
    wd,
    qkv,
    pt,
    cc,
    ua,
    act,
    gp,
    g2a,
    g1a,
    part,
    rc,
    ys,
    ry,
    xh1,
    rstd1,
    resid,
    cot,
    gb,
    rx,
    rz,
    rm,
    rb,
    rn,
    rq,
    held,
    landed,
    vg,
    vec_ref,
    grads,
    lengths_ref,
    load_sem,
    store_sem,
    agy_send,
    agy_recv,
    agc_send,
    agc_recv,
    agf_send,
    agf_recv,
    rsc_send,
    rsc_recv,
    rsy_send,
    rsy_recv,
    hop_send,
    hop_recv,
    vec_send,
    vec_recv,
    grad_sem,
    *small_refs,
    summed,
):
    batches = x_ref.shape[0]
    block = x_ref.shape[1]
    width = x_ref.shape[2]
    head_cols = wo.shape[0]
    hidden = wu.shape[1]
    rows = 4 * block
    pairs = head_cols // 128
    t = lax.axis_index("tensor")
    c = lax.rem(t, 2)
    y = lax.div(t, 2)
    t_core = y * 2 + (1 - c)
    t_y = (1 - y) * 2 + c
    t_far = (1 - y) * 2 + (1 - c)
    core = {"tensor": t_core}
    across = {"tensor": t_y}

    gathers = (xa, ua, g2a, g1a)

    def remote(src, dst, send, recv, device):
        return pltpu.make_async_remote_copy(
            src_ref=src, dst_ref=dst, send_sem=send, recv_sem=recv, device_id=device, device_id_type=MESH
        )

    def ag_y(p, s, at, src=None):
        buf = gathers[p]
        return remote(
            buf.at[s, at] if src is None else src, buf.at[s, at], agy_send.at[p, s], agy_recv.at[p, s], across
        )

    def ag_c(p, s, at, src=None):
        buf = gathers[p]
        return remote(
            buf.at[s, at] if src is None else src, buf.at[s, at], agc_send.at[p, s], agc_recv.at[p, s], core
        )

    def ag_f(p, s, at):
        buf = gathers[p]
        return remote(buf.at[s, at], buf.at[s, at], agf_send.at[p, s], agf_recv.at[p, s], core)

    def rs_c(p, s):
        return remote(part.at[s, 1 - c], rc.at[s], rsc_send.at[p, s], rsc_recv.at[p, s], core)

    def rs_y(p, s):
        return remote(ys.at[s], ry.at[s], rsy_send.at[p, s], rsy_recv.at[p, s], across)

    def load(index, src, dst):
        return pltpu.make_async_copy(src, dst, load_sem.at[index])

    def store(index, src, dst):
        return pltpu.make_async_copy(src, dst, store_sem.at[index])

    loads = [load(s, x_ref.at[s], xa.at[s, t]) for s in range(batches)]
    n = batches
    load_wq = load(n, wqkv_ref, wq)
    load_wo = load(n + 1, wout_ref, wo)
    load_wu = load(n + 2, wup_ref, wu)
    load_wd = load(n + 3, wdown_ref, wd)
    load_cot = load(n + 4, cot_ref, cot)

    for cp in loads:
        cp.start()
    if summed:
        reducer = Reducer(gb, rx, rz, rm, rb, rn, rq, hop_send, hop_recv)
        vectors = VectorReducer(reducer, held, landed, vec_send, vec_recv, 6)
        reducer.greet((core, across))
    else:
        barrier = pltpu.get_barrier_semaphore()
        for device in (core, across):
            pl.semaphore_signal(barrier, inc=1, device_id=device, device_id_type=MESH)
        pl.semaphore_wait(barrier, 2)
    for s in range(batches):
        ag_y(0, s, t, x_ref.at[s]).start()
        ag_c(0, s, t, x_ref.at[s]).start()
    load_wq.start()
    load_wo.start()
    load_wu.start()
    load_wd.start()
    load_cot.start()

    vg[...] = jnp.zeros_like(vg)
    small_ins = (bout_in, gain1_in, bias1_in, bdown_in, gain2_in, bias2_in, bup_in, bquery_in, bvalue_in)
    small = [load(n + 5, lengths_in, lengths_ref)]
    small += [load(n + 6 + i, ref, held_ref) for i, (ref, held_ref) in enumerate(zip(small_ins, small_refs))]
    for cp in small:
        cp.start()
    for cp in small:
        cp.wait()
    for i, ref in enumerate(small_refs[:7]):
        vec_ref[i : i + 1, :] = ref[...].astype(F32).reshape(1, -1)
    for i, ref in enumerate(small_refs[7:]):
        vec_ref[7:8, i * head_cols : (i + 1) * head_cols] = ref[...].astype(F32).reshape(1, -1)
    lane = lax.broadcasted_iota(jnp.int32, (rows, 128), 1)
    low_half = lane < HD
    empty = jnp.zeros((rows, 128), LOW)

    def masked(values, h):
        return jnp.where(low_half, values, empty) if h == 0 else jnp.where(low_half, empty, values)

    def vec(i):
        return vec_ref[i : i + 1, :]

    def whole(ref, s):
        return ref[s].reshape(rows, width)

    def put_part(s, j, values):
        values = values.astype(LOW)
        cols = pl.ds(pl.multiple_of(j * TILE, TILE), TILE)
        for b in range(4):
            part[s, b % 2, b // 2, :, cols] = values[b * block : (b + 1) * block]

    def compute_a(s):
        tokens = whole(xa, s)
        q = dot(tokens, wq[0]) + vec_ref[7:8, :head_cols]
        qkv[s, 0] = q.astype(LOW) * LOW(HD ** (-0.5))
        qkv[s, 1] = dot(tokens, wq[1]).astype(LOW)
        v = dot(tokens, wq[2]) + vec_ref[7:8, head_cols : 2 * head_cols]
        qkv[s, 2] = v.astype(LOW)
        keys_valid = lax.broadcasted_iota(jnp.int32, (rows, rows), 0) < lengths_ref[0, s]

        def pair(j, carry):
            cols = pl.ds(pl.multiple_of(j * 128, 128), 128)
            q, k, v = qkv[s, 0, :, cols], qkv[s, 1, :, cols], qkv[s, 2, :, cols]
            context = jnp.zeros((128, rows), F32)
            for h in range(2):
                scores = dot(k, masked(q, h), 1, 1)
                scores = jnp.where(keys_valid, scores, -1e30)
                weights = jnp.exp(scores - jnp.max(scores, axis=0, keepdims=True))
                p = (weights * (1.0 / row_sum(weights))).astype(LOW)
                pt[s, 2 * j + h] = p
                context = context + dot(masked(v, h).T, p)
            cc[s, :, cols] = context.T.astype(LOW)
            return carry

        lax.fori_loop(0, pairs, pair, 0)

        def out(j, carry):
            cols = pl.ds(pl.multiple_of(j * TILE, TILE), TILE)
            put_part(s, j, dot(cc[s], wo[:, cols]))
            return carry

        lax.fori_loop(0, width // TILE, out, 0)

    def compute_c(s):
        def tile(j, carry):
            cols = pl.ds(pl.multiple_of(j * TILE, TILE), TILE)
            h = dot(whole(ua, s), wu[:, cols]) + vec_ref[6:7, cols]
            phi, density = gelu_parts(h)
            act[s, :, cols] = (h * phi).astype(LOW)
            gp[s, :, cols] = (phi + h * density).astype(LOW)
            return carry

        lax.fori_loop(0, hidden // TILE, tile, 0)

        def down(j, carry):
            cols = pl.ds(pl.multiple_of(j * TILE, TILE), TILE)
            put_part(s, j, dot(act[s], wd[:, cols]))
            return carry

        lax.fori_loop(0, width // TILE, down, 0)

    def compute_e_hidden(s):
        def tile(j, carry):
            cols = pl.ds(pl.multiple_of(j * TILE, TILE), TILE)
            gh = gp[s, :, cols].astype(F32) * dot(whole(g2a, s), wd[cols, :], 1, 1)
            vg[6:7, cols] += row_sum(gh)
            gp[s, :, cols] = gh.astype(LOW)
            return carry

        lax.fori_loop(0, hidden // TILE, tile, 0)

    def compute_e_back(s):
        def back(j, carry):
            rows_at = pl.ds(pl.multiple_of(j * TILE, TILE), TILE)
            put_part(s, j, dot(gp[s], wu[rows_at, :], 1, 1))
            return carry

        lax.fori_loop(0, width // TILE, back, 0)

    def head_pair_back(s, j):
        cols = slice(j * 128, (j + 1) * 128)
        q, k, v = qkv[s, 0, :, cols], qkv[s, 1, :, cols], qkv[s, 2, :, cols]
        gc = grads[:, cols]
        dq = jnp.zeros((128, rows), F32)
        dk = jnp.zeros((rows, 128), F32)
        dv = jnp.zeros((rows, 128), F32)
        for h in range(2):
            gc_h = masked(gc, h)
            p = pt[s, 2 * j + h]
            wide = p.astype(F32)
            product = wide * dot(v, gc_h, 1, 1)
            ds = (product - wide * row_sum(product)).astype(LOW)
            dv = dv + dot(p, gc_h)
            dk = dk + dot(ds, masked(q, h))
            dq = dq + dot(masked(k, h).T, ds)
        dq = dq.T * (HD ** (-0.5))
        vg[7:8, cols] += row_sum(dq)
        vg[7:8, head_cols + j * 128 : head_cols + (j + 1) * 128] += row_sum(dv)
        qkv[s, 0, :, cols] = dq.astype(LOW)
        qkv[s, 1, :, cols] = dk.astype(LOW)
        qkv[s, 2, :, cols] = dv.astype(LOW)

    def compute_g_first(s):
        grads[...] = dot(whole(g1a, s), wo[...], 1, 1).astype(LOW)
        for j in range(pairs // 2):
            head_pair_back(s, j)

    def compute_g_second(s):
        for j in range(pairs // 2, pairs):
            head_pair_back(s, j)

    def compute_g_back(s):
        def back(j, carry):
            at = pl.ds(pl.multiple_of(j * TILE, TILE), TILE)
            total = dot(qkv[s, 0], wq[0, at, :], 1, 1)
            total = total + dot(qkv[s, 1], wq[1, at, :], 1, 1)
            total = total + dot(qkv[s, 2], wq[2, at, :], 1, 1)
            put_part(s, j, total)
            return carry

        lax.fori_loop(0, width // TILE, back, 0)

    computes = (
        (compute_a,),
        (compute_c,),
        (compute_e_hidden, compute_e_back),
        (compute_g_first, compute_g_second, compute_g_back),
    )

    def reduced(p, s):
        rs_y(p, s).wait()
        rs_c(p, s).wait_send()
        return part[s, c, y].astype(F32) + rc[s, y].astype(F32) + ry[s].astype(F32)

    def send_on(p, s):
        ag_y(p, s, t).start()
        ag_c(p, s, t).start()

    def finish_a(s):
        z = xa[s, t].astype(F32) + (reduced(0, s) + vec(0))
        centred = z - row_mean(z)
        rstd = lax.rsqrt(row_mean(centred * centred) + EPSILON)
        hat = centred * rstd
        xh1[s] = hat
        rstd1[s] = jnp.broadcast_to(rstd, rstd1.shape[1:])
        ua[s, t] = (hat * vec(1) + vec(2)).astype(LOW)
        send_on(1, s)

    def finish_c(s):
        z = (xh1[s] * vec(1) + vec(2)) + (reduced(1, s) + vec(3))
        centred = z - row_mean(z)
        rstd = lax.rsqrt(row_mean(centred * centred) + EPSILON)
        hat = centred * rstd
        valid = t * block + lax.broadcasted_iota(jnp.int32, (block, width), 0) < lengths_ref[0, s]
        incoming = jnp.where(valid, cot[s].astype(F32), 0.0)
        scaled = incoming * vec(4)
        grad = rstd * (scaled - row_mean(scaled) - hat * row_mean(scaled * hat))
        resid[s] = grad
        g2a[s, t] = grad.astype(LOW)
        send_on(2, s)
        cot[s] = jnp.where(valid, hat * vec(4) + vec(5), 0.0).astype(LOW)
        store(s, cot.at[s], out_ref.at[s]).start()
        vg[3:4, :] += row_sum(grad)
        vg[4:5, :] += row_sum(incoming * hat)
        vg[5:6, :] += row_sum(incoming)

    def finish_e(s):
        gu = resid[s] + reduced(2, s)
        hat = xh1[s]
        scaled = gu * vec(1)
        grad = rstd1[s, :, :1] * (scaled - row_mean(scaled) - hat * row_mean(scaled * hat))
        resid[s] = grad
        g1a[s, t] = grad.astype(LOW)
        send_on(3, s)
        vg[0:1, :] += row_sum(grad)
        vg[1:2, :] += row_sum(gu * hat)
        vg[2:3, :] += row_sum(gu)

    def finish_g(s):
        store(s, cot.at[s], out_ref.at[s]).wait()
        cot[s] = (resid[s] + reduced(3, s)).astype(LOW)
        store(batches + s, cot.at[s], gin_ref.at[s]).start()

    finishes = (finish_a, finish_c, finish_e, finish_g)

    def forward_block(p, s):
        ag_y(p, s, t_y).wait_recv()
        ag_f(p, s, t_y).start()

    def gathered(p, s):
        ag_c(p, s, t_core).wait_recv()
        ag_f(p, s, t_far).wait_recv()

    def send_sums(p, s):
        rs_c(p, s).start()

    def pass_sums(p, s):
        rs_c(p, s).wait_recv()
        ys[s] = (part[s, c, 1 - y].astype(F32) + rc[s, 1 - y].astype(F32)).astype(LOW)
        rs_y(p, s).start()

    def tall(values):
        return values.reshape(batches * rows, -1)

    per_piece = TILE // UNIT
    down_pieces = hidden // TILE
    up_pieces = width // TILE
    early_pieces = down_pieces + up_pieces
    pieces = early_pieces + 1 + 3

    def piece(d):
        if d < early_pieces:
            if d < down_pieces:
                cols = slice(d * TILE, (d + 1) * TILE)
                left, right = tall(act[:, :, cols]), g2a
            else:
                cols = slice((d - down_pieces) * TILE, (d - down_pieces + 1) * TILE)
                left, right = tall(ua[:, :, :, cols]), gp
        elif d == early_pieces:
            left, right = tall(cc[...]), g1a
        else:
            right = tall(qkv[:, d - early_pieces - 1])
            for j in range(per_piece):
                cols = slice(j * TILE, (j + 1) * TILE)
                product = dot(tall(xa[:, :, :, cols]), right, 0, 0).astype(LOW)
                for h in range(per_piece):
                    gb[d * per_piece + j, :, :, h * head_cols : (h + 1) * head_cols] = product[
                        h * UNIT : (h + 1) * UNIT
                    ].reshape(2, UNIT // 2, head_cols)
            return

        def half(j, carry):
            cols = pl.ds(pl.multiple_of(j * (width // 2), width // 2), width // 2)
            columns = right[:, :, cols] if len(right.shape) == 3 else right[:, :, :, cols]
            product = dot(left, tall(columns), 0, 0).astype(LOW)
            for u in range(per_piece):
                gb[d * per_piece + u, :, :, cols] = product[u * UNIT : (u + 1) * UNIT].reshape(
                    2, UNIT // 2, width // 2
                )
            return carry

        lax.fori_loop(0, 2, half, 0)

    def unit_store(i, src):
        at = i
        for ref in (gdown_ref, gup_ref, gout_ref, gqkv_ref):
            if at < ref.shape[0]:
                break
            at -= ref.shape[0]
        return pltpu.make_async_copy(src, ref.at[at], grad_sem.at[i])

    unit_pairs = pieces * per_piece // 2

    def pair_stores(k):
        return unit_store(2 * k, rx.at[k % RING]), unit_store(2 * k + 1, rb.at[k % RING])

    ticks = iter(range(-1, unit_pairs + STAGE_AT[-1] + STORE_TICKS + 1))

    def tick():
        now = next(ticks, None)
        if now is None:
            return False
        k = now + 1
        if k < unit_pairs:
            if 2 * k % per_piece == 0:
                piece(2 * k // per_piece)
            reducer.start(k)
        for stage, at in zip(reducer.stages, STAGE_AT):
            if 0 <= now - at < unit_pairs:
                stage(reducer, now - at)
        if 0 <= now - STAGE_AT[-1] < unit_pairs:
            for cp in pair_stores(now - STAGE_AT[-1]):
                cp.start()
        if 0 <= now - STAGE_AT[-1] - STORE_TICKS < unit_pairs:
            reducer.drain(now - STAGE_AT[-1] - STORE_TICKS)
            for cp in pair_stores(now - STAGE_AT[-1] - STORE_TICKS):
                cp.wait()
        return True

    def step(s, carry, p):
        gathered(p, s)
        for compute in computes[p]:
            compute(s)
        send_sums(p, s)
        pass_sums(p, s)
        if p > 0:

            @pl.when(s == 0)
            def _():
                finishes[p - 1](batches - 1)

        @pl.when(s > 0)
        def _():
            finishes[p](s - 1)

        @pl.when(s < batches - 1)
        def _():
            forward_block(p, s + 1)

        @pl.when(s == batches - 1)
        def _():
            forward_block(p + 1, 0)

        return carry

    forward_block(0, 0)
    for cp in loads:
        cp.wait()
    load_wq.wait()
    load_wo.wait()
    lax.fori_loop(0, batches, functools.partial(step, p=0), 0)
    load_wu.wait()
    load_wd.wait()
    load_cot.wait()
    lax.fori_loop(0, batches, functools.partial(step, p=1), 0)

    hops = iter(range(VECTOR_HOPS + 1))

    def vector_hop():
        hop = next(hops, None)
        if hop is None:
            return False
        if hop == 0:
            held[0] = vg[...]
        else:
            vectors.end(hop - 1)
        if hop < VECTOR_HOPS:
            vectors.begin(hop)
        return True

    actions = {
        "gather": gathered,
        "compute": lambda p, s, part: computes[p][part](s),
        "send": send_sums,
        "pass": pass_sums,
        "finish": lambda p, s: finishes[p](s),
        "forward": forward_block,
    }
    last = PHASES * batches - 1
    vectors_wait = {("compute", last, 1), ("finish", last - batches)}
    for action in SCHEDULE:
        if action == TICK:
            if summed:
                if not vectors_wait:
                    vector_hop()
                tick()
        else:
            name, index, *which = action
            actions[name](index // batches, index % batches, *which)
            vectors_wait.discard(action)
    if summed:
        while tick():
            vector_hop()
        while vector_hop():
            pass
        store_sums = store(2 * batches, held.at[VECTOR_HOPS - 1], vsum_ref)
        store_sums.start()
    else:
        stores = []
        for d in range(pieces):
            piece(d)
            for i in range(d * per_piece, (d + 1) * per_piece):
                stores.append(unit_store(i, gb.at[i]))
                stores[-1].start()
        store_sums = store(2 * batches, vg, vsum_ref)
        store_sums.start()
        for cp in stores:
            cp.wait()
    for s in range(batches):
        store(batches + s, cot.at[s], gin_ref.at[s]).wait()
    store_sums.wait()

    def drain(i, carry):
        for p in range(PHASES):
            ag_y(p, i, t).wait_send()
            ag_c(p, i, t).wait_send()
            ag_f(p, i, t_y).wait_send()
        return carry

    lax.fori_loop(0, batches, drain, 0)


def run_layer(lengths, x, cot, wqkv, wout, wup, wdown, vectors, summed):
    batches, block, width = x.shape
    rows = 4 * block
    head_cols = wout.shape[0]
    heads = head_cols // HD
    hidden = wup.shape[1]
    half = UNIT // 2
    down, up, out = hidden // UNIT, width // UNIT, head_cols // UNIT
    units = down + up + out + 3 * out
    ring, short_ring = (RING, SHORT_RING) if summed else (1, 1)
    any_space = pl.BlockSpec(memory_space=pl.ANY)
    dma = pltpu.SemaphoreType.DMA
    low = lambda *shape: pltpu.VMEM(shape, LOW)
    wide = lambda *shape: pltpu.VMEM(shape, F32)
    gathered = low(batches, 4, block, width)
    scratch = [
        gathered,
        low(3, width, head_cols),
        low(head_cols, width),
        low(width, hidden),
        low(hidden, width),
        low(batches, 3, rows, head_cols),
        low(batches, heads, rows, rows),
        low(batches, rows, head_cols),
        gathered,
        low(batches, rows, hidden),
        low(batches, rows, hidden),
        gathered,
        gathered,
        low(batches, 2, 2, block, width),
        low(batches, 2, block, width),
        low(batches, block, width),
        low(batches, block, width),
        wide(batches, block, width),
        wide(batches, block, 128),
        wide(batches, block, width),
        low(batches, block, width),
        low(units, 2, half, width),
        low(ring, 2, half, width),
        low(short_ring, half, width),
        low(short_ring, half, width),
        low(ring, 2, half, width),
        low(short_ring, half, width),
        low(short_ring, half, width),
        wide(VECTOR_HOPS, 8, width),
        wide(VECTOR_HOPS - 1, 8, width),
        wide(8, width),
        wide(8, width),
        low(rows, head_cols),
        pltpu.SMEM(lengths.shape, jnp.int32),
        dma((batches + 15,)),
        dma((2 * batches + 1,)),
    ]
    scratch += [dma((PHASES, batches))] * 10 + [dma((HOPS, units // 2))] * 2 + [dma((VECTOR_HOPS,))] * 2
    scratch.append(dma((units,)))
    scratch += [low(width)] * 7 + [low(head_cols)] * 2
    low_out = lambda *shape: jax.ShapeDtypeStruct(shape, LOW)
    return pl.pallas_call(
        functools.partial(layer_kernel, summed=summed),
        out_shape=(
            low_out(batches, block, width),
            low_out(batches, block, width),
            low_out(down, 2, half, width),
            low_out(up, 2, half, hidden),
            low_out(out, 2, half, width),
            low_out(3 * out, 2, half, width),
            jax.ShapeDtypeStruct((8, width), F32),
        ),
        in_specs=[any_space] * 16,
        out_specs=(any_space,) * 7,
        scratch_shapes=scratch,
        compiler_params=pltpu.CompilerParams(
            collective_id=0, has_side_effects=True, vmem_limit_bytes=63 << 20
        ),
        name="layer",
    )(lengths, x, cot, wqkv, wout, wup, wdown, *vectors)


def widen_kernel(
    down_ref, up_ref, out_ref, qkv_ref, sums_ref, rows_ref, gin_ref,
    down_wide, up_wide, out_wide, qkv_wide, *refs,
):
    vectors, refs = refs[:9], refs[9:]
    rows_copy, gin_copy, low, wide, low_qkv, wide_qkv, rows, sums, load_sem, store_sem, vec_sem, *made_vectors = refs
    work = []

    def part(src, dst, held, made):
        n = len(work)
        get = pltpu.make_async_copy(src, held, load_sem.at[n])
        put = pltpu.make_async_copy(made, dst, store_sem.at[n])
        work.append((get, held, made, put))

    i = 0
    for src, dst in ((down_ref, down_wide), (up_ref, up_wide), (out_ref, out_wide)):
        for at in range(0, src.shape[0], TILE):
            part(src.at[pl.ds(at, TILE)], dst.at[pl.ds(at, TILE)], low.at[i], wide.at[i])
            i += 1
    for i in range(3):
        part(qkv_ref.at[i], qkv_wide.at[i], low_qkv.at[i], wide_qkv.at[i])
    fold = low_qkv.shape[3] // wide_qkv.shape[2]
    for i, (src, dst) in enumerate(((rows_ref, rows_copy), (gin_ref, gin_copy))):
        block = rows.at[i]
        part(src, dst, block, block)
    load_sums = pltpu.make_async_copy(sums_ref, sums, vec_sem.at[0])
    for get, _, _, _ in work[:LOADS_AHEAD]:
        get.start()
    load_sums.start()
    for n, (get, held, made, put) in enumerate(work):
        get.wait()
        if n + LOADS_AHEAD < len(work):
            work[n + LOADS_AHEAD][0].start()
        if len(held.shape) == 3 and made is not held:
            cols = made.shape[1]
            for j in range(held.shape[0]):
                for h in range(fold):
                    at = (j * fold + h) * UNIT
                    made[at : at + UNIT, :] = held[j, :, h * cols : (h + 1) * cols].astype(F32)
        elif made is not held:
            made[...] = held[...].astype(F32)
        put.start()
    load_sums.wait()
    head_cols = out_ref.shape[0]
    for i in range(2):
        made_vectors[i][...] = sums[7, i * head_cols : (i + 1) * head_cols]
    for ref, row in zip(made_vectors[2:], (0, 1, 2, 6, 3, 4, 5)):
        ref[...] = sums[row]
    puts = [
        pltpu.make_async_copy(src, dst, vec_sem.at[1 + i])
        for i, (src, dst) in enumerate(zip(made_vectors, vectors))
    ]
    for cp in puts:
        cp.start()
    for cp in puts:
        cp.wait()
    for _, _, _, put in work:
        put.wait()


def widen(down, up, out, qkv, sums, rows, gin):
    any_space = pl.BlockSpec(memory_space=pl.ANY)
    dma = pltpu.SemaphoreType.DMA
    width = down.shape[1]
    pieces = (down.shape[0] + up.shape[0] + out.shape[0]) // TILE
    as_wide = lambda a: jax.ShapeDtypeStruct(a.shape, F32)
    vector = lambda n: jax.ShapeDtypeStruct((n,), F32)
    return pl.pallas_call(
        widen_kernel,
        out_shape=(
            *map(as_wide, (down, up, out)),
            jax.ShapeDtypeStruct((3, width, out.shape[0]), F32),
            *[vector(out.shape[0])] * 2,
            *[vector(width)] * 7,
            jax.ShapeDtypeStruct(rows.shape, rows.dtype),
            jax.ShapeDtypeStruct(gin.shape, gin.dtype),
        ),
        in_specs=[any_space] * 7,
        out_specs=(any_space,) * 15,
        scratch_shapes=[
            pltpu.VMEM((pieces, TILE, width), LOW),
            pltpu.VMEM((pieces, TILE, width), F32),
            pltpu.VMEM(qkv.shape, LOW),
            pltpu.VMEM((3, width, out.shape[0]), F32),
            pltpu.VMEM((2, *rows.shape), LOW),
            pltpu.VMEM(sums.shape, F32),
            dma((pieces + 5,)),
            dma((pieces + 5,)),
            dma((10,)),
            *[pltpu.VMEM((out.shape[0],), F32)] * 2,
            *[pltpu.VMEM((width,), F32)] * 7,
        ],
        compiler_params=pltpu.CompilerParams(vmem_limit_bytes=62 << 20),
        name="widen",
    )(down, up, out, qkv, sums, rows, gin)


def per_device(
    inputs,
    lengths,
    cotangent,
    w_qkv,
    b_query,
    b_value,
    w_out,
    b_out,
    ln1_gain,
    ln1_bias,
    w_up,
    b_up,
    w_down,
    b_down,
    ln2_gain,
    ln2_bias,
):
    width = inputs.shape[3]
    head_cols = w_out.shape[0]
    hidden = w_up.shape[1]
    summed = lax.axis_size("dp") == 8
    output, grad_inputs, grad_down, grad_up, grad_out, grad_qkv, sums = run_layer(
        lengths,
        inputs[0],
        cotangent[0],
        jnp.transpose(w_qkv, (1, 0, 2)),
        w_out,
        w_up,
        w_down,
        (b_out, ln1_gain, ln1_bias, b_down, ln2_gain, ln2_bias, b_up, b_query, b_value),
        summed,
    )
    if not summed:
        grad_down, grad_up, grad_out, grad_qkv, sums = lax.psum(
            (grad_down, grad_up, grad_out, grad_qkv, sums), "dp"
        )
        sums = jnp.concatenate([lax.psum(sums[:6], "tensor"), sums[6:]])
    grad_down, grad_up, grad_out, grad_qkv, *rest = widen(
        grad_down.reshape(hidden, width),
        grad_up.reshape(width, hidden),
        grad_out.reshape(head_cols, width),
        grad_qkv.reshape(3, -1, UNIT, width),
        sums,
        output,
        grad_inputs,
    )
    gquery, gvalue, gbout, ggain1, gbias1, gbup, gbdown, ggain2, gbias2, output, grad_inputs = rest
    return (
        output[None],
        grad_inputs[None],
        jnp.transpose(grad_qkv, (1, 0, 2)),
        gquery,
        gvalue,
        grad_out,
        gbout,
        ggain1,
        gbias1,
        grad_up,
        gbup,
        grad_down,
        gbdown,
        ggain2,
        gbias2,
    )


def solution(mesh):
    return jax.shard_map(
        per_device,
        mesh=mesh,
        in_specs=(
            P("dp", None, "tensor", None),
            P("dp", None),
            P("dp", None, "tensor", None),
            P(None, None, "tensor"),
            P("tensor"),
            P("tensor"),
            P("tensor", None),
            P(),
            P(),
            P(),
            P(None, "tensor"),
            P("tensor"),
            P("tensor", None),
            P(),
            P(),
            P(),
        ),
        out_specs=(
            P("dp", None, "tensor", None),
            P("dp", None, "tensor", None),
            P(None, None, "tensor"),
            P("tensor"),
            P("tensor"),
            P("tensor", None),
            P(),
            P(),
            P(),
            P(None, "tensor"),
            P("tensor"),
            P("tensor", None),
            P(),
            P(),
            P(),
        ),
        check_vma=False,
    )
```

```python
import functools

import jax
import jax.numpy as jnp
from jax import lax
from jax.experimental import pallas as pl
from jax.experimental.pallas import tpu as pltpu
from jax.sharding import PartitionSpec as P

HD = 64
EPSILON = 1e-05
F32 = jnp.float32
LOW = jnp.bfloat16
MESH = pl.DeviceIdType.MESH
TILE = 256
PHASES = 4
UNIT = 64


def dot(left, right, left_dim=1, right_dim=0):
    return lax.dot_general(
        left, right, (((left_dim,), (right_dim,)), ((), ())), preferred_element_type=F32
    )


def row_sum(values):
    return jnp.sum(values, axis=0, keepdims=True)


def row_mean(values):
    return jnp.mean(values, axis=-1, keepdims=True)


def gelu_parts(h):
    t = 1.0 / (1.0 + 0.23164188 * jnp.abs(h))
    density = jnp.exp(-0.5 * h * h)
    series = t * (
        0.127414796
        + t * (-0.142248368 + t * (0.7107068705 + t * (-0.7265760135 + t * 0.5307027145)))
    )
    tail = series * density
    return jnp.where(h < 0.0, tail, 1.0 - tail), density * 0.3989422804014327


HOPS = 11
RING = 16
SHORT_RING = 8
STAGE_AT = (0, 1, 2, 3, 4, 6)
STORE_TICKS = 3
LOADS_AHEAD = 16
TICK = ("tick", 0)
SCHEDULE = (
    ("gather", 6),
    ("finish", 5),
    ("forward", 7),
    ("compute", 6, 0),
    ("compute", 6, 1),
    ("send", 6),
    ("forward", 8),
    ("gather", 7),
    ("gather", 8),
    TICK,
    ("compute", 7, 0),
    ("pass", 6),
    TICK,
    ("compute", 8, 0),
    TICK,
    ("compute", 8, 1),
    ("compute", 7, 1),
    TICK,
    ("send", 7),
    TICK,
    ("send", 8),
    ("finish", 6),
    TICK,
    ("pass", 8),
    *[TICK] * 2,
    ("pass", 7),
    TICK,
    ("forward", 9),
    ("finish", 8),
    TICK,
    ("gather", 9),
    TICK,
    ("finish", 7),
    TICK,
    ("forward", 11),
    TICK,
    ("compute", 9, 0),
    TICK,
    ("forward", 10),
    ("compute", 9, 1),
    TICK,
    ("gather", 11),
    ("gather", 10),
    ("compute", 10, 0),
    TICK,
    ("compute", 10, 1),
    TICK,
    ("compute", 11, 0),
    TICK,
    ("compute", 11, 1),
    TICK,
    ("compute", 10, 2),
    ("send", 10),
    TICK,
    ("pass", 10),
    TICK,
    ("compute", 9, 2),
    ("send", 9),
    *[TICK] * 2,
    ("compute", 11, 2),
    TICK,
    ("pass", 9),
    TICK,
    ("send", 11),
    TICK,
    ("pass", 11),
    ("finish", 10),
    ("finish", 9),
    *[TICK] * 2,
    ("finish", 11),
)


class Reducer:
    def __init__(self, gb, rx, rz, rm, rb, rn, rq, send_sems, recv_sems):
        dp = lax.axis_index("dp")
        self.x = lax.rem(dp, 2)
        self.z = lax.div(dp, 2)
        self.side = lax.rem(self.z, 2)
        self.m = lax.div(self.z, 2)
        self.inner = self.side != self.m
        self.outer = self.side == self.m
        self.to_x = {"dp": self.z * 2 + (1 - self.x)}
        self.to_pair = {"dp": (self.z + 1 - 2 * self.side) * 2 + self.x}
        self.to_mid = {"dp": (3 - self.z) * 2 + self.x}
        self.inside = None
        self.gb, self.rx, self.rz, self.rm, self.rb, self.rn, self.rq = gb, rx, rz, rm, rb, rn, rq
        self.send_sems, self.recv_sems = send_sems, recv_sems

    def greet(self, extra=()):
        barrier = pltpu.get_barrier_semaphore()

        def signal(device):
            pl.semaphore_signal(barrier, inc=1, device_id=device, device_id_type=MESH)

        for device in (self.to_x, self.to_pair) + tuple(extra):
            signal(device)

        @self.when(True)
        def _():
            signal(self.to_mid)
            pl.semaphore_wait(barrier, 3 + len(extra))

        @self.when(False)
        def _():
            pl.semaphore_wait(barrier, 2 + len(extra))

    def when(self, inner):
        if self.inside is None:
            return pl.when(self.inner if inner else self.outer)

        def run(step):
            if inner == self.inside:
                step()

        return run

    def copy(self, hop, k, src, dst, device):
        return pltpu.make_async_remote_copy(
            src_ref=src,
            dst_ref=dst,
            send_sem=self.send_sems.at[hop, k],
            recv_sem=self.recv_sems.at[hop, k],
            device_id=device,
            device_id_type=MESH,
        )

    def ax(self, k):
        return self.copy(0, k, self.gb.at[2 * k, 1 - self.x], self.rx.at[k % RING, 1 - self.x], self.to_x)

    def az(self, k):
        return self.copy(1, k, self.gb.at[2 * k, self.x], self.rz.at[k % SHORT_RING], self.to_pair)

    def am(self, k):
        return self.copy(2, k, self.gb.at[2 * k, self.x], self.rm.at[k % SHORT_RING], self.to_mid)

    def ao(self, k):
        return self.copy(3, k, self.rx.at[k % RING, self.x], self.rx.at[k % RING, self.x], self.to_pair)

    def ag(self, k):
        return self.copy(4, k, self.rx.at[k % RING, self.x], self.rx.at[k % RING, self.x], self.to_x)

    def bi(self, k):
        return self.copy(5, k, self.gb.at[2 * k + 1], self.rb.at[k % RING], self.to_pair)

    def bm(self, k):
        return self.copy(6, k, self.gb.at[2 * k + 1, 1 - self.m], self.rn.at[k % SHORT_RING], self.to_mid)

    def bx(self, k):
        return self.copy(7, k, self.gb.at[2 * k + 1, self.m], self.rq.at[k % SHORT_RING], self.to_x)

    def bg(self, k):
        return self.copy(8, k, self.rb.at[k % RING, self.m], self.rb.at[k % RING, self.m], self.to_mid)

    def bo(self, k):
        return self.copy(9, k, self.rb.at[k % RING, self.m], self.rb.at[k % RING, self.m], self.to_pair)

    def bp(self, k):
        return self.copy(10, k, self.rb.at[k % RING, 1 - self.m], self.rb.at[k % RING, 1 - self.m], self.to_pair)

    def add(self, out, left, right):
        out[...] = (left[...].astype(F32) + right[...].astype(F32)).astype(LOW)

    def start(self, k):
        self.ax(k).start()

        @self.when(False)
        def _():
            self.bi(k).start()

    def stage1(self, k):
        self.ax(k).wait()
        own = self.gb.at[2 * k, self.x]
        self.add(own, own, self.rx.at[k % RING, self.x])

        @self.when(False)
        def _():
            self.az(k).start()

    def stage2(self, k):
        @self.when(True)
        def _():
            self.bi(k).wait_recv()
            away = self.gb.at[2 * k + 1, 1 - self.m]
            self.add(away, away, self.rb.at[k % RING, 1 - self.m])
            self.bm(k).start()
            own = self.gb.at[2 * k + 1, self.m]
            self.add(own, own, self.rb.at[k % RING, self.m])
            self.az(k).wait_recv()
            own = self.gb.at[2 * k, self.x]
            self.add(own, own, self.rz.at[k % SHORT_RING])
            self.am(k).start()

    def stage3(self, k):
        @self.when(True)
        def _():
            self.bm(k).wait()
            own = self.gb.at[2 * k + 1, self.m]
            self.add(own, own, self.rn.at[k % SHORT_RING])
            self.bx(k).start()
            self.am(k).wait()
            self.add(self.rx.at[k % RING, self.x], self.gb.at[2 * k, self.x], self.rm.at[k % SHORT_RING])
            self.ao(k).start()
            self.ag(k).start()

    def stage4(self, k):
        @self.when(True)
        def _():
            self.bx(k).wait()
            self.add(self.rb.at[k % RING, self.m], self.gb.at[2 * k + 1, self.m], self.rq.at[k % SHORT_RING])
            self.bg(k).start()
            self.bo(k).start()

        @self.when(False)
        def _():
            self.ao(k).wait_recv()
            self.ag(k).start()

    def stage5(self, k):
        @self.when(True)
        def _():
            self.bg(k).wait_recv()
            self.bp(k).start()

        self.ag(k).wait_recv()

    def stage6(self, k):
        @self.when(False)
        def _():
            self.bo(k).wait_recv()
            self.bp(k).wait_recv()

    def drain(self, k):
        self.ag(k).wait_send()

        @self.when(True)
        def _():
            self.ao(k).wait_send()
            self.bg(k).wait_send()
            self.bo(k).wait_send()
            self.bp(k).wait_send()

        @self.when(False)
        def _():
            self.az(k).wait_send()
            self.bi(k).wait_send()

    stages = (stage1, stage2, stage3, stage4, stage5, stage6)


VECTOR_HOPS = 6


class VectorReducer:
    def __init__(self, reducer, held, landed, send_sem, recv_sem, shared):
        t = lax.axis_index("tensor")
        c = lax.rem(t, 2)
        y = lax.div(t, 2)
        self.r = reducer
        self.held, self.landed, self.send_sem, self.recv_sem = held, landed, send_sem, recv_sem
        self.shared = shared
        self.devices = (
            {"tensor": y * 2 + (1 - c)},
            {"tensor": (1 - y) * 2 + c},
            reducer.to_x,
            reducer.to_pair,
            reducer.to_mid,
            reducer.to_pair,
        )

    def copy(self, hop):
        src = self.held.at[5 if hop == 5 else hop]
        dst = self.held.at[5] if hop == 5 else self.landed.at[hop]
        return pltpu.make_async_remote_copy(
            src_ref=src,
            dst_ref=dst,
            send_sem=self.send_sem.at[hop],
            recv_sem=self.recv_sem.at[hop],
            device_id=self.devices[hop],
            device_id_type=MESH,
        )

    def begin(self, hop):
        if hop < 3:
            self.copy(hop).start()
        else:

            @pl.when(self.r.outer if hop == 3 else self.r.inner)
            def _():
                self.copy(hop).start()

    def end(self, hop):
        if hop < 3:
            self.copy(hop).wait()
            got = self.landed[hop]
            if hop < 2:
                row = lax.broadcasted_iota(jnp.int32, got.shape, 0)
                got = jnp.where(row < self.shared, got, 0.0)
            self.held[hop + 1] = self.held[hop] + got
        elif hop == 3:

            @pl.when(self.r.outer)
            def _():
                self.copy(3).wait_send()

            @pl.when(self.r.inner)
            def _():
                self.copy(3).wait_recv()
                self.held[4] = self.held[3] + self.landed[3]

        elif hop == 4:

            @pl.when(self.r.inner)
            def _():
                self.copy(4).wait()
                self.held[5] = self.held[4] + self.landed[4]

        else:

            @pl.when(self.r.inner)
            def _():
                self.copy(5).wait_send()

            @pl.when(self.r.outer)
            def _():
                self.copy(5).wait_recv()


def layer_kernel(
    lengths_in,
    x_ref,
    cot_ref,
    wqkv_ref,
    wout_ref,
    wup_ref,
    wdown_ref,
    bout_in,
    gain1_in,
    bias1_in,
    bdown_in,
    gain2_in,
    bias2_in,
    bup_in,
    bquery_in,
    bvalue_in,
    out_ref,
    gin_ref,
    gdown_ref,
    gup_ref,
    gout_ref,
    gqkv_ref,
    vsum_ref,
    xa,
    wq,
    wo,
    wu,
    wd,
    qkv,
    pt,
    cc,
    ua,
    act,
    gp,
    g2a,
    g1a,
    part,
    rc,
    ys,
    ry,
    xh1,
    rstd1,
    resid,
    cot,
    gb,
    rx,
    rz,
    rm,
    rb,
    rn,
    rq,
    held,
    landed,
    vg,
    vec_ref,
    grads,
    lengths_ref,
    load_sem,
    store_sem,
    agy_send,
    agy_recv,
    agc_send,
    agc_recv,
    agf_send,
    agf_recv,
    rsc_send,
    rsc_recv,
    rsy_send,
    rsy_recv,
    hop_send,
    hop_recv,
    vec_send,
    vec_recv,
    grad_sem,
    *small_refs,
    summed,
):
    batches = x_ref.shape[0]
    block = x_ref.shape[1]
    width = x_ref.shape[2]
    head_cols = wo.shape[0]
    hidden = wu.shape[1]
    rows = 4 * block
    pairs = head_cols // 128
    t = lax.axis_index("tensor")
    c = lax.rem(t, 2)
    y = lax.div(t, 2)
    t_core = y * 2 + (1 - c)
    t_y = (1 - y) * 2 + c
    t_far = (1 - y) * 2 + (1 - c)
    core = {"tensor": t_core}
    across = {"tensor": t_y}

    gathers = (xa, ua, g2a, g1a)

    def remote(src, dst, send, recv, device):
        return pltpu.make_async_remote_copy(
            src_ref=src, dst_ref=dst, send_sem=send, recv_sem=recv, device_id=device, device_id_type=MESH
        )

    def ag_y(p, s, at, src=None):
        buf = gathers[p]
        return remote(
            buf.at[s, at] if src is None else src, buf.at[s, at], agy_send.at[p, s], agy_recv.at[p, s], across
        )

    def ag_c(p, s, at, src=None):
        buf = gathers[p]
        return remote(
            buf.at[s, at] if src is None else src, buf.at[s, at], agc_send.at[p, s], agc_recv.at[p, s], core
        )

    def ag_f(p, s, at):
        buf = gathers[p]
        return remote(buf.at[s, at], buf.at[s, at], agf_send.at[p, s], agf_recv.at[p, s], core)

    def rs_c(p, s):
        return remote(part.at[s, 1 - c], rc.at[s], rsc_send.at[p, s], rsc_recv.at[p, s], core)

    def rs_y(p, s):
        return remote(ys.at[s], ry.at[s], rsy_send.at[p, s], rsy_recv.at[p, s], across)

    def load(index, src, dst):
        return pltpu.make_async_copy(src, dst, load_sem.at[index])

    def store(index, src, dst):
        return pltpu.make_async_copy(src, dst, store_sem.at[index])

    loads = [load(s, x_ref.at[s], xa.at[s, t]) for s in range(batches)]
    n = batches
    load_wq = load(n, wqkv_ref, wq)
    load_wo = load(n + 1, wout_ref, wo)
    load_wu = load(n + 2, wup_ref, wu)
    load_wd = load(n + 3, wdown_ref, wd)
    load_cot = load(n + 4, cot_ref, cot)

    for cp in loads:
        cp.start()
    if summed:
        reducer = Reducer(gb, rx, rz, rm, rb, rn, rq, hop_send, hop_recv)
        vectors = VectorReducer(reducer, held, landed, vec_send, vec_recv, 6)
        reducer.greet((core, across))
    else:
        barrier = pltpu.get_barrier_semaphore()
        for device in (core, across):
            pl.semaphore_signal(barrier, inc=1, device_id=device, device_id_type=MESH)
        pl.semaphore_wait(barrier, 2)
    for s in range(batches):
        ag_y(0, s, t, x_ref.at[s]).start()
        ag_c(0, s, t, x_ref.at[s]).start()
    load_wq.start()
    load_wo.start()
    load_wu.start()
    load_wd.start()
    load_cot.start()

    vg[...] = jnp.zeros_like(vg)
    small_ins = (bout_in, gain1_in, bias1_in, bdown_in, gain2_in, bias2_in, bup_in, bquery_in, bvalue_in)
    small = [load(n + 5, lengths_in, lengths_ref)]
    small += [load(n + 6 + i, ref, held_ref) for i, (ref, held_ref) in enumerate(zip(small_ins, small_refs))]
    for cp in small:
        cp.start()
    for cp in small:
        cp.wait()
    for i, ref in enumerate(small_refs[:7]):
        vec_ref[i : i + 1, :] = ref[...].astype(F32).reshape(1, -1)
    for i, ref in enumerate(small_refs[7:]):
        vec_ref[7:8, i * head_cols : (i + 1) * head_cols] = ref[...].astype(F32).reshape(1, -1)
    lane = lax.broadcasted_iota(jnp.int32, (rows, 128), 1)
    low_half = lane < HD
    empty = jnp.zeros((rows, 128), LOW)

    def masked(values, h):
        return jnp.where(low_half, values, empty) if h == 0 else jnp.where(low_half, empty, values)

    def vec(i):
        return vec_ref[i : i + 1, :]

    def whole(ref, s):
        return ref[s].reshape(rows, width)

    def put_part(s, j, values):
        values = values.astype(LOW)
        cols = pl.ds(pl.multiple_of(j * TILE, TILE), TILE)
        for b in range(4):
            part[s, b % 2, b // 2, :, cols] = values[b * block : (b + 1) * block]

    def compute_a(s):
        tokens = whole(xa, s)
        q = dot(tokens, wq[0]) + vec_ref[7:8, :head_cols]
        qkv[s, 0] = q.astype(LOW) * LOW(HD ** (-0.5))
        qkv[s, 1] = dot(tokens, wq[1]).astype(LOW)
        v = dot(tokens, wq[2]) + vec_ref[7:8, head_cols : 2 * head_cols]
        qkv[s, 2] = v.astype(LOW)
        keys_valid = lax.broadcasted_iota(jnp.int32, (rows, rows), 0) < lengths_ref[0, s]

        def pair(j, carry):
            cols = pl.ds(pl.multiple_of(j * 128, 128), 128)
            q, k, v = qkv[s, 0, :, cols], qkv[s, 1, :, cols], qkv[s, 2, :, cols]
            context = jnp.zeros((128, rows), F32)
            for h in range(2):
                scores = dot(k, masked(q, h), 1, 1)
                scores = jnp.where(keys_valid, scores, -1e30)
                weights = jnp.exp(scores - jnp.max(scores, axis=0, keepdims=True))
                p = (weights * (1.0 / row_sum(weights))).astype(LOW)
                pt[s, 2 * j + h] = p
                context = context + dot(masked(v, h).T, p)
            cc[s, :, cols] = context.T.astype(LOW)
            return carry

        lax.fori_loop(0, pairs, pair, 0)

        def out(j, carry):
            cols = pl.ds(pl.multiple_of(j * TILE, TILE), TILE)
            put_part(s, j, dot(cc[s], wo[:, cols]))
            return carry

        lax.fori_loop(0, width // TILE, out, 0)

    def compute_c(s):
        def tile(j, carry):
            cols = pl.ds(pl.multiple_of(j * TILE, TILE), TILE)
            h = dot(whole(ua, s), wu[:, cols]) + vec_ref[6:7, cols]
            phi, density = gelu_parts(h)
            act[s, :, cols] = (h * phi).astype(LOW)
            gp[s, :, cols] = (phi + h * density).astype(LOW)
            return carry

        lax.fori_loop(0, hidden // TILE, tile, 0)

        def down(j, carry):
            cols = pl.ds(pl.multiple_of(j * TILE, TILE), TILE)
            put_part(s, j, dot(act[s], wd[:, cols]))
            return carry

        lax.fori_loop(0, width // TILE, down, 0)

    def compute_e_hidden(s):
        def tile(j, carry):
            cols = pl.ds(pl.multiple_of(j * TILE, TILE), TILE)
            gh = gp[s, :, cols].astype(F32) * dot(whole(g2a, s), wd[cols, :], 1, 1)
            vg[6:7, cols] += row_sum(gh)
            gp[s, :, cols] = gh.astype(LOW)
            return carry

        lax.fori_loop(0, hidden // TILE, tile, 0)

    def compute_e_back(s):
        def back(j, carry):
            rows_at = pl.ds(pl.multiple_of(j * TILE, TILE), TILE)
            put_part(s, j, dot(gp[s], wu[rows_at, :], 1, 1))
            return carry

        lax.fori_loop(0, width // TILE, back, 0)

    def head_pair_back(s, j):
        cols = slice(j * 128, (j + 1) * 128)
        q, k, v = qkv[s, 0, :, cols], qkv[s, 1, :, cols], qkv[s, 2, :, cols]
        gc = grads[:, cols]
        dq = jnp.zeros((128, rows), F32)
        dk = jnp.zeros((rows, 128), F32)
        dv = jnp.zeros((rows, 128), F32)
        for h in range(2):
            gc_h = masked(gc, h)
            p = pt[s, 2 * j + h]
            wide = p.astype(F32)
            product = wide * dot(v, gc_h, 1, 1)
            ds = (product - wide * row_sum(product)).astype(LOW)
            dv = dv + dot(p, gc_h)
            dk = dk + dot(ds, masked(q, h))
            dq = dq + dot(masked(k, h).T, ds)
        dq = dq.T * (HD ** (-0.5))
        vg[7:8, cols] += row_sum(dq)
        vg[7:8, head_cols + j * 128 : head_cols + (j + 1) * 128] += row_sum(dv)
        qkv[s, 0, :, cols] = dq.astype(LOW)
        qkv[s, 1, :, cols] = dk.astype(LOW)
        qkv[s, 2, :, cols] = dv.astype(LOW)

    def compute_g_first(s):
        grads[...] = dot(whole(g1a, s), wo[...], 1, 1).astype(LOW)
        for j in range(pairs // 2):
            head_pair_back(s, j)

    def compute_g_second(s):
        for j in range(pairs // 2, pairs):
            head_pair_back(s, j)

    def compute_g_back(s):
        def back(j, carry):
            at = pl.ds(pl.multiple_of(j * TILE, TILE), TILE)
            total = dot(qkv[s, 0], wq[0, at, :], 1, 1)
            total = total + dot(qkv[s, 1], wq[1, at, :], 1, 1)
            total = total + dot(qkv[s, 2], wq[2, at, :], 1, 1)
            put_part(s, j, total)
            return carry

        lax.fori_loop(0, width // TILE, back, 0)

    computes = (
        (compute_a,),
        (compute_c,),
        (compute_e_hidden, compute_e_back),
        (compute_g_first, compute_g_second, compute_g_back),
    )

    def reduced(p, s):
        rs_y(p, s).wait()
        rs_c(p, s).wait_send()
        return part[s, c, y].astype(F32) + rc[s, y].astype(F32) + ry[s].astype(F32)

    def send_on(p, s):
        ag_y(p, s, t).start()
        ag_c(p, s, t).start()

    def finish_a(s):
        z = xa[s, t].astype(F32) + (reduced(0, s) + vec(0))
        centred = z - row_mean(z)
        rstd = lax.rsqrt(row_mean(centred * centred) + EPSILON)
        hat = centred * rstd
        xh1[s] = hat
        rstd1[s] = jnp.broadcast_to(rstd, rstd1.shape[1:])
        ua[s, t] = (hat * vec(1) + vec(2)).astype(LOW)
        send_on(1, s)

    def finish_c(s):
        z = (xh1[s] * vec(1) + vec(2)) + (reduced(1, s) + vec(3))
        centred = z - row_mean(z)
        rstd = lax.rsqrt(row_mean(centred * centred) + EPSILON)
        hat = centred * rstd
        valid = t * block + lax.broadcasted_iota(jnp.int32, (block, width), 0) < lengths_ref[0, s]
        incoming = jnp.where(valid, cot[s].astype(F32), 0.0)
        scaled = incoming * vec(4)
        grad = rstd * (scaled - row_mean(scaled) - hat * row_mean(scaled * hat))
        resid[s] = grad
        g2a[s, t] = grad.astype(LOW)
        send_on(2, s)
        cot[s] = jnp.where(valid, hat * vec(4) + vec(5), 0.0).astype(LOW)
        store(s, cot.at[s], out_ref.at[s]).start()
        vg[3:4, :] += row_sum(grad)
        vg[4:5, :] += row_sum(incoming * hat)
        vg[5:6, :] += row_sum(incoming)

    def finish_e(s):
        gu = resid[s] + reduced(2, s)
        hat = xh1[s]
        scaled = gu * vec(1)
        grad = rstd1[s, :, :1] * (scaled - row_mean(scaled) - hat * row_mean(scaled * hat))
        resid[s] = grad
        g1a[s, t] = grad.astype(LOW)
        send_on(3, s)
        vg[0:1, :] += row_sum(grad)
        vg[1:2, :] += row_sum(gu * hat)
        vg[2:3, :] += row_sum(gu)

    def finish_g(s):
        store(s, cot.at[s], out_ref.at[s]).wait()
        cot[s] = (resid[s] + reduced(3, s)).astype(LOW)
        store(batches + s, cot.at[s], gin_ref.at[s]).start()

    finishes = (finish_a, finish_c, finish_e, finish_g)

    def forward_block(p, s):
        ag_y(p, s, t_y).wait_recv()
        ag_f(p, s, t_y).start()

    def gathered(p, s):
        ag_c(p, s, t_core).wait_recv()
        ag_f(p, s, t_far).wait_recv()

    def send_sums(p, s):
        rs_c(p, s).start()

    def pass_sums(p, s):
        rs_c(p, s).wait_recv()
        ys[s] = (part[s, c, 1 - y].astype(F32) + rc[s, 1 - y].astype(F32)).astype(LOW)
        rs_y(p, s).start()

    def tall(values):
        return values.reshape(batches * rows, -1)

    per_piece = TILE // UNIT
    down_pieces = hidden // TILE
    up_pieces = width // TILE
    early_pieces = down_pieces + up_pieces
    pieces = early_pieces + 1 + 3

    def piece(d):
        if d < early_pieces:
            if d < down_pieces:
                cols = slice(d * TILE, (d + 1) * TILE)
                left, right = tall(act[:, :, cols]), g2a
            else:
                cols = slice((d - down_pieces) * TILE, (d - down_pieces + 1) * TILE)
                left, right = tall(ua[:, :, :, cols]), gp
        elif d == early_pieces:
            left, right = tall(cc[...]), g1a
        else:
            right = tall(qkv[:, d - early_pieces - 1])
            for j in range(per_piece):
                cols = slice(j * TILE, (j + 1) * TILE)
                product = dot(tall(xa[:, :, :, cols]), right, 0, 0).astype(LOW)
                for h in range(per_piece):
                    gb[d * per_piece + j, :, :, h * head_cols : (h + 1) * head_cols] = product[
                        h * UNIT : (h + 1) * UNIT
                    ].reshape(2, UNIT // 2, head_cols)
            return

        def half(j, carry):
            cols = pl.ds(pl.multiple_of(j * (width // 2), width // 2), width // 2)
            columns = right[:, :, cols] if len(right.shape) == 3 else right[:, :, :, cols]
            product = dot(left, tall(columns), 0, 0).astype(LOW)
            for u in range(per_piece):
                gb[d * per_piece + u, :, :, cols] = product[u * UNIT : (u + 1) * UNIT].reshape(
                    2, UNIT // 2, width // 2
                )
            return carry

        lax.fori_loop(0, 2, half, 0)

    def unit_store(i, src):
        at = i
        for ref in (gdown_ref, gup_ref, gout_ref, gqkv_ref):
            if at < ref.shape[0]:
                break
            at -= ref.shape[0]
        return pltpu.make_async_copy(src, ref.at[at], grad_sem.at[i])

    unit_pairs = pieces * per_piece // 2

    def pair_stores(k):
        return unit_store(2 * k, rx.at[k % RING]), unit_store(2 * k + 1, rb.at[k % RING])

    ticks = iter(range(-1, unit_pairs + STAGE_AT[-1] + STORE_TICKS + 1))

    def tick():
        now = next(ticks, None)
        if now is None:
            return False
        k = now + 1
        if k < unit_pairs and 2 * k % per_piece == 0:
            piece(2 * k // per_piece)

        def serve():
            if k < unit_pairs:
                reducer.start(k)
            for stage, at in zip(reducer.stages, STAGE_AT):
                if 0 <= now - at < unit_pairs:
                    stage(reducer, now - at)
            if 0 <= now - STAGE_AT[-1] < unit_pairs:
                for cp in pair_stores(now - STAGE_AT[-1]):
                    cp.start()
            old = now - STAGE_AT[-1] - STORE_TICKS
            if 0 <= old < unit_pairs:
                reducer.drain(old)
                for cp in pair_stores(old):
                    cp.wait()

        for inside in (True, False):
            reducer.inside = inside

            @pl.when(reducer.inner if inside else reducer.outer)
            def _():
                serve()

        reducer.inside = None
        return True

    def step(s, carry, p):
        gathered(p, s)
        for compute in computes[p]:
            compute(s)
        send_sums(p, s)
        pass_sums(p, s)
        if p > 0:

            @pl.when(s == 0)
            def _():
                finishes[p - 1](batches - 1)

        @pl.when(s > 0)
        def _():
            finishes[p](s - 1)

        @pl.when(s < batches - 1)
        def _():
            forward_block(p, s + 1)

        @pl.when(s == batches - 1)
        def _():
            forward_block(p + 1, 0)

        return carry

    forward_block(0, 0)
    for cp in loads:
        cp.wait()
    load_wq.wait()
    load_wo.wait()
    lax.fori_loop(0, batches, functools.partial(step, p=0), 0)
    load_wu.wait()
    load_wd.wait()
    load_cot.wait()
    lax.fori_loop(0, batches, functools.partial(step, p=1), 0)

    hops = iter(range(VECTOR_HOPS + 1))

    def vector_hop():
        hop = next(hops, None)
        if hop is None:
            return False
        if hop == 0:
            held[0] = vg[...]
        else:
            vectors.end(hop - 1)
        if hop < VECTOR_HOPS:
            vectors.begin(hop)
        return True

    actions = {
        "gather": gathered,
        "compute": lambda p, s, part: computes[p][part](s),
        "send": send_sums,
        "pass": pass_sums,
        "finish": lambda p, s: finishes[p](s),
        "forward": forward_block,
    }
    last = PHASES * batches - 1
    vectors_wait = {("compute", last, 1), ("finish", last - batches)}
    for action in SCHEDULE:
        if action == TICK:
            if summed:
                if not vectors_wait:
                    vector_hop()
                tick()
        else:
            name, index, *which = action
            actions[name](index // batches, index % batches, *which)
            vectors_wait.discard(action)
    def drain(i, carry):
        for p in range(PHASES):
            ag_y(p, i, t).wait_send()
            ag_c(p, i, t).wait_send()
            ag_f(p, i, t_y).wait_send()
        return carry

    lax.fori_loop(0, batches, drain, 0)

    if summed:
        while tick():
            vector_hop()
        while vector_hop():
            pass
        store_sums = store(2 * batches, held.at[VECTOR_HOPS - 1], vsum_ref)
        store_sums.start()
    else:
        stores = []
        for d in range(pieces):
            piece(d)
            for i in range(d * per_piece, (d + 1) * per_piece):
                stores.append(unit_store(i, gb.at[i]))
                stores[-1].start()
        store_sums = store(2 * batches, vg, vsum_ref)
        store_sums.start()
        for cp in stores:
            cp.wait()
    for s in range(batches):
        store(batches + s, cot.at[s], gin_ref.at[s]).wait()
    store_sums.wait()


def run_layer(lengths, x, cot, wqkv, wout, wup, wdown, vectors, summed):
    batches, block, width = x.shape
    rows = 4 * block
    head_cols = wout.shape[0]
    heads = head_cols // HD
    hidden = wup.shape[1]
    half = UNIT // 2
    down, up, out = hidden // UNIT, width // UNIT, head_cols // UNIT
    units = down + up + out + 3 * out
    ring, short_ring = (RING, SHORT_RING) if summed else (1, 1)
    any_space = pl.BlockSpec(memory_space=pl.ANY)
    dma = pltpu.SemaphoreType.DMA
    low = lambda *shape: pltpu.VMEM(shape, LOW)
    wide = lambda *shape: pltpu.VMEM(shape, F32)
    gathered = low(batches, 4, block, width)
    scratch = [
        gathered,
        low(3, width, head_cols),
        low(head_cols, width),
        low(width, hidden),
        low(hidden, width),
        low(batches, 3, rows, head_cols),
        low(batches, heads, rows, rows),
        low(batches, rows, head_cols),
        gathered,
        low(batches, rows, hidden),
        low(batches, rows, hidden),
        gathered,
        gathered,
        low(batches, 2, 2, block, width),
        low(batches, 2, block, width),
        low(batches, block, width),
        low(batches, block, width),
        wide(batches, block, width),
        wide(batches, block, 128),
        wide(batches, block, width),
        low(batches, block, width),
        low(units, 2, half, width),
        low(ring, 2, half, width),
        low(short_ring, half, width),
        low(short_ring, half, width),
        low(ring, 2, half, width),
        low(short_ring, half, width),
        low(short_ring, half, width),
        wide(VECTOR_HOPS, 8, width),
        wide(VECTOR_HOPS - 1, 8, width),
        wide(8, width),
        wide(8, width),
        low(rows, head_cols),
        pltpu.SMEM(lengths.shape, jnp.int32),
        dma((batches + 15,)),
        dma((2 * batches + 1,)),
    ]
    scratch += [dma((PHASES, batches))] * 10 + [dma((HOPS, units // 2))] * 2 + [dma((VECTOR_HOPS,))] * 2
    scratch.append(dma((units,)))
    scratch += [low(width)] * 7 + [low(head_cols)] * 2
    low_out = lambda *shape: jax.ShapeDtypeStruct(shape, LOW)
    return pl.pallas_call(
        functools.partial(layer_kernel, summed=summed),
        out_shape=(
            low_out(batches, block, width),
            low_out(batches, block, width),
            low_out(down, 2, half, width),
            low_out(up, 2, half, hidden),
            low_out(out, 2, half, width),
            low_out(3 * out, 2, half, width),
            jax.ShapeDtypeStruct((8, width), F32),
        ),
        in_specs=[any_space] * 16,
        out_specs=(any_space,) * 7,
        scratch_shapes=scratch,
        compiler_params=pltpu.CompilerParams(
            collective_id=0, has_side_effects=True, vmem_limit_bytes=63 << 20
        ),
        name="layer",
    )(lengths, x, cot, wqkv, wout, wup, wdown, *vectors)


def widen_kernel(
    down_ref, up_ref, out_ref, qkv_ref, sums_ref, rows_ref, gin_ref,
    down_wide, up_wide, out_wide, qkv_wide, *refs,
):
    vectors, refs = refs[:9], refs[9:]
    rows_copy, gin_copy, low, wide, low_qkv, wide_qkv, rows, sums, load_sem, store_sem, vec_sem, *made_vectors = refs
    work = []

    def part(src, dst, held, made):
        n = len(work)
        get = pltpu.make_async_copy(src, held, load_sem.at[n])
        put = pltpu.make_async_copy(made, dst, store_sem.at[n])
        work.append((get, held, made, put))

    i = 0
    for src, dst in ((down_ref, down_wide), (up_ref, up_wide), (out_ref, out_wide)):
        for at in range(0, src.shape[0], TILE):
            part(src.at[pl.ds(at, TILE)], dst.at[pl.ds(at, TILE)], low.at[i], wide.at[i])
            i += 1
    for i in range(3):
        part(qkv_ref.at[i], qkv_wide.at[i], low_qkv.at[i], wide_qkv.at[i])
    fold = low_qkv.shape[3] // wide_qkv.shape[2]
    for i, (src, dst) in enumerate(((rows_ref, rows_copy), (gin_ref, gin_copy))):
        block = rows.at[i]
        part(src, dst, block, block)
    load_sums = pltpu.make_async_copy(sums_ref, sums, vec_sem.at[0])
    for get, _, _, _ in work[:LOADS_AHEAD]:
        get.start()
    load_sums.start()
    for n, (get, held, made, put) in enumerate(work):
        get.wait()
        if n + LOADS_AHEAD < len(work):
            work[n + LOADS_AHEAD][0].start()
        if len(held.shape) == 3 and made is not held:
            cols = made.shape[1]
            for j in range(held.shape[0]):
                for h in range(fold):
                    at = (j * fold + h) * UNIT
                    made[at : at + UNIT, :] = held[j, :, h * cols : (h + 1) * cols].astype(F32)
        elif made is not held:
            made[...] = held[...].astype(F32)
        put.start()
    load_sums.wait()
    head_cols = out_ref.shape[0]
    for i in range(2):
        made_vectors[i][...] = sums[7, i * head_cols : (i + 1) * head_cols]
    for ref, row in zip(made_vectors[2:], (0, 1, 2, 6, 3, 4, 5)):
        ref[...] = sums[row]
    puts = [
        pltpu.make_async_copy(src, dst, vec_sem.at[1 + i])
        for i, (src, dst) in enumerate(zip(made_vectors, vectors))
    ]
    for cp in puts:
        cp.start()
    for cp in puts:
        cp.wait()
    for _, _, _, put in work:
        put.wait()


def widen(down, up, out, qkv, sums, rows, gin):
    any_space = pl.BlockSpec(memory_space=pl.ANY)
    dma = pltpu.SemaphoreType.DMA
    width = down.shape[1]
    pieces = (down.shape[0] + up.shape[0] + out.shape[0]) // TILE
    as_wide = lambda a: jax.ShapeDtypeStruct(a.shape, F32)
    vector = lambda n: jax.ShapeDtypeStruct((n,), F32)
    return pl.pallas_call(
        widen_kernel,
        out_shape=(
            *map(as_wide, (down, up, out)),
            jax.ShapeDtypeStruct((3, width, out.shape[0]), F32),
            *[vector(out.shape[0])] * 2,
            *[vector(width)] * 7,
            jax.ShapeDtypeStruct(rows.shape, rows.dtype),
            jax.ShapeDtypeStruct(gin.shape, gin.dtype),
        ),
        in_specs=[any_space] * 7,
        out_specs=(any_space,) * 15,
        scratch_shapes=[
            pltpu.VMEM((pieces, TILE, width), LOW),
            pltpu.VMEM((pieces, TILE, width), F32),
            pltpu.VMEM(qkv.shape, LOW),
            pltpu.VMEM((3, width, out.shape[0]), F32),
            pltpu.VMEM((2, *rows.shape), LOW),
            pltpu.VMEM(sums.shape, F32),
            dma((pieces + 5,)),
            dma((pieces + 5,)),
            dma((10,)),
            *[pltpu.VMEM((out.shape[0],), F32)] * 2,
            *[pltpu.VMEM((width,), F32)] * 7,
        ],
        compiler_params=pltpu.CompilerParams(vmem_limit_bytes=62 << 20),
        name="widen",
    )(down, up, out, qkv, sums, rows, gin)


def per_device(
    inputs,
    lengths,
    cotangent,
    w_qkv,
    b_query,
    b_value,
    w_out,
    b_out,
    ln1_gain,
    ln1_bias,
    w_up,
    b_up,
    w_down,
    b_down,
    ln2_gain,
    ln2_bias,
):
    width = inputs.shape[3]
    head_cols = w_out.shape[0]
    hidden = w_up.shape[1]
    summed = lax.axis_size("dp") == 8
    output, grad_inputs, grad_down, grad_up, grad_out, grad_qkv, sums = run_layer(
        lengths,
        inputs[0],
        cotangent[0],
        jnp.transpose(w_qkv, (1, 0, 2)),
        w_out,
        w_up,
        w_down,
        (b_out, ln1_gain, ln1_bias, b_down, ln2_gain, ln2_bias, b_up, b_query, b_value),
        summed,
    )
    if not summed:
        grad_down, grad_up, grad_out, grad_qkv, sums = lax.psum(
            (grad_down, grad_up, grad_out, grad_qkv, sums), "dp"
        )
        sums = jnp.concatenate([lax.psum(sums[:6], "tensor"), sums[6:]])
    grad_down, grad_up, grad_out, grad_qkv, *rest = widen(
        grad_down.reshape(hidden, width),
        grad_up.reshape(width, hidden),
        grad_out.reshape(head_cols, width),
        grad_qkv.reshape(3, -1, UNIT, width),
        sums,
        output,
        grad_inputs,
    )
    gquery, gvalue, gbout, ggain1, gbias1, gbup, gbdown, ggain2, gbias2, output, grad_inputs = rest
    return (
        output[None],
        grad_inputs[None],
        jnp.transpose(grad_qkv, (1, 0, 2)),
        gquery,
        gvalue,
        grad_out,
        gbout,
        ggain1,
        gbias1,
        grad_up,
        gbup,
        grad_down,
        gbdown,
        ggain2,
        gbias2,
    )


def solution(mesh):
    return jax.shard_map(
        per_device,
        mesh=mesh,
        in_specs=(
            P("dp", None, "tensor", None),
            P("dp", None),
            P("dp", None, "tensor", None),
            P(None, None, "tensor"),
            P("tensor"),
            P("tensor"),
            P("tensor", None),
            P(),
            P(),
            P(),
            P(None, "tensor"),
            P("tensor"),
            P("tensor", None),
            P(),
            P(),
            P(),
        ),
        out_specs=(
            P("dp", None, "tensor", None),
            P("dp", None, "tensor", None),
            P(None, None, "tensor"),
            P("tensor"),
            P("tensor"),
            P("tensor", None),
            P(),
            P(),
            P(),
            P(None, "tensor"),
            P("tensor"),
            P("tensor", None),
            P(),
            P(),
            P(),
        ),
        check_vma=False,
    )
```
